128 devices in a mesh: row: 16 (over z, y), col: 8 (over x, core).
Axes of the slice: x: 4, y: 4, z: 4, core: 2. Of those that a mesh axis runs over, the one named last changes fastest.
Arguments:
- frame_one: bfloat16 [256, 256, 256], P('row', 'col'), may hold values from -6 to 6
- frame_two: bfloat16 [256, 256, 256], P('row', 'col'), may hold values from -6 to 6
- context: bfloat16 [256, 256, 256], P('row', 'col'), may hold values from -6 to 6
- cotangent: bfloat16 [256, 256, 128], P('row', 'col'), may hold values from -6 to 6
- corr_weight: bfloat16 [324, 256], replicated, may hold values from -0.3125 to 0.3125
- conv_weight: bfloat16 [3, 3, 256, 128], replicated, may hold values from -0.125 to 0.125
- partners: int32 [16, 8, 4], P('row', 'col'), may hold values from 0 to 14, as said below
- counts: int32 [16, 8], P('row', 'col'), may hold values from 1 to 4
- radius: int32 [16, 8], P('row', 'col'), may hold values from 1 to 4
Outputs:
- motion_features: bfloat16 [256, 256, 128], P('row', 'col')
- context_grad: bfloat16 [256, 256, 256], P('row', 'col')
- frame_one_grad: float32 [256, 256, 256], P('row', 'col')
- frame_two_grad: float32 [256, 256, 256], P('row', 'col')
- corr_weight_grad: float32 [324, 256], replicated
- conv_weight_grad: float32 [3, 3, 256, 128], replicated
The draws below stay inside these ranges and needn't reach their ends.
Inputs may be any that keep to these rules, and one draw needn't show every extreme that they name: `partners`: each tile's 4 entries are different offsets. Offset 7 denotes the tile itself (dy = 0, dx = 0); it need not be among a tile's entries.
All inputs are finite; a program needn't handle non-finite values.
Results may differ from the reference program's by a relative error of at most 0.0075.
Values may be sent and summed in bfloat16 or wider, within the bound.
No kernel may reach another device: no remote copies, remote signals or barrier semaphores. Data moves between devices by JAX's collectives and lax.ppermute only.
A program may use at most 192 MiB of HBM per device.

```python
import math
import jax
import jax.numpy as jnp
from jax import lax

CH = 256
HID = 256
OUTC = 128
SLOTS = 4
REACH = 4
TR = 16
TC = 32
FH = 256
FW = 256
N_ROW = 16
N_COL = 8


def draw_partners(key, part):
    scores = jax.random.randint(key, (N_ROW, N_COL, 15), 0, 1 << 20) * 16 + jnp.arange(15, dtype=jnp.int32)
    order = jnp.argsort(scores, axis=-1)
    return order[..., :SLOTS].astype(jnp.int32)


def touch_ends(result, rng, least, largest):
    shape = result.shape
    place = [jax.random.randint(jax.random.fold_in(rng, axis), (), 0, shape[axis]) for axis in range(len(shape))]
    result = result.at[tuple(place)].set(least)
    longest = shape.index(max(shape))
    place[longest] = (place[longest] + 1) % shape[longest]
    return result.at[tuple(place)].set(largest)


def block_levels(stream_key, shape, pieces, least, largest):
    factor_of = 1.0
    for position, blocks in pieces:
        steps = jax.random.uniform(jax.random.fold_in(jax.random.fold_in(stream_key, 6), position), (blocks,), jnp.float32, least / len(pieces), largest / len(pieces))
        factor_of = factor_of * jnp.repeat(jnp.exp(steps), shape[position] // blocks).reshape((-1,) + (1,) * (len(shape) - 1 - position))
    return factor_of


def scatter_about(key, dims, scale, most, cuts=(), kind=jnp.bfloat16):
    result = scale * jax.random.normal(key, dims, jnp.float32)
    if cuts:
        result = result * block_levels(key, dims, cuts, -0.22, 0.18)
    return jnp.clip(result, -most, most).astype(kind)


def setup_inputs(seed: int = 0) -> dict:
    streams_of = jax.random.split(jax.random.key(seed), 10)
    frame_one = scatter_about(streams_of[0], (FH, FW, CH), 1.0, 6.0, ((0, 16), (1, 8)))
    frame_two = scatter_about(streams_of[1], (FH, FW, CH), 1.0, 6.0, ((0, 16), (1, 8)))
    context = scatter_about(streams_of[2], (FH, FW, HID), 1.0, 6.0, ((0, 16), (1, 8)))
    cotangent = scatter_about(streams_of[3], (FH, FW, OUTC), 1.0, 6.0, ((0, 16), (1, 8)))
    corr_weight = scatter_about(streams_of[4], (SLOTS * (2 * REACH + 1) ** 2, HID), (SLOTS * (2 * REACH + 1) ** 2) ** -0.5, 0.3125)
    conv_weight = scatter_about(streams_of[5], (3, 3, HID, OUTC), (9 * HID) ** -0.5, 0.125)
    partners = draw_partners(jax.random.fold_in(streams_of[9], 71), 0)
    counts = touch_ends(jax.random.randint(streams_of[7], (N_ROW, N_COL), 1, SLOTS + 1), jax.random.fold_in(streams_of[7], 1), 1, SLOTS).astype(jnp.int32)
    radius = touch_ends(jax.random.randint(streams_of[8], (N_ROW, N_COL), 1, REACH + 1), jax.random.fold_in(streams_of[8], 1), 1, REACH).astype(jnp.int32)
    return dict(frame_one=frame_one, frame_two=frame_two, context=context, cotangent=cotangent, corr_weight=corr_weight, conv_weight=conv_weight, partners=partners, counts=counts, radius=radius)


def to_tiles(frame):
    return frame.reshape(N_ROW, TR, N_COL, TC, frame.shape[-1]).transpose(0, 2, 1, 3, 4)

def to_frame(tiles):
    return tiles.transpose(0, 2, 1, 3, 4).reshape(N_ROW * TR, N_COL * TC, tiles.shape[-1])

def window_mask(count, reach_now):
    span = 2 * REACH + 1
    live = (jnp.arange(SLOTS) < count).astype(jnp.float32)
    inside = (jnp.abs(jnp.arange(span) - REACH) <= reach_now).astype(jnp.float32)
    return live[:, None, None] * inside[None, :, None] * inside[None, None, :]

def tile_correlation(first, parts, mask):
    span = 2 * REACH + 1
    padded = jnp.pad(parts, ((0, 0), (REACH, REACH), (REACH, REACH), (0, 0)))
    planes = []
    for tap_row in range(span):
        for tap_col in range(span):
            planes.append(lax.optimization_barrier(jnp.sum(first[None] * padded[:, tap_row:tap_row + TR, tap_col:tap_col + TC], axis=-1)))
    volume = jnp.stack(planes, axis=-1).reshape(SLOTS, TR, TC, span, span)
    return volume.transpose(1, 2, 0, 3, 4) * mask * (1.0 / math.sqrt(CH))

def reference(frame_one, frame_two, context, cotangent, corr_weight, conv_weight, partners, counts, radius):
    span = 2 * REACH + 1
    width = SLOTS * span * span
    count_tiles = N_ROW * N_COL
    first_tiles = to_tiles(frame_one)
    second_pad = jnp.pad(to_tiles(frame_two), ((1, 1), (2, 2), (0, 0), (0, 0), (0, 0)))

    def pick(tile):
        row_tile = tile // N_COL
        col_tile = tile % N_COL
        offsets = partners[row_tile, col_tile]
        row_src = row_tile + offsets // 5
        col_src = col_tile + offsets % 5
        parts = second_pad[row_src, col_src].astype(jnp.float32)
        mask = window_mask(counts[row_tile, col_tile], radius[row_tile, col_tile])
        first = first_tiles[row_tile, col_tile].astype(jnp.float32)
        return (first, parts, mask, row_src, col_src)

    def forward_tile(tile):
        first, parts, mask, row_src, col_src = pick(tile)
        return tile_correlation(first, parts, mask)
    tile_ids = jnp.arange(count_tiles, dtype=jnp.int32)
    volume = lax.map(forward_tile, tile_ids)
    corr_feat = to_frame(volume.reshape(N_ROW, N_COL, TR, TC, width)).astype(jnp.bfloat16).reshape(-1, width)
    pre = jnp.dot(corr_feat, corr_weight, preferred_element_type=jnp.float32) + context.reshape(-1, HID).astype(jnp.float32)
    motion = jax.nn.silu(pre).astype(jnp.bfloat16).reshape(FH, FW, HID)
    motion_pad = jnp.pad(motion, ((1, 1), (1, 1), (0, 0)))
    cot_pad = jnp.pad(cotangent, ((1, 1), (1, 1), (0, 0)))
    flat_cot = cotangent.reshape(-1, OUTC)
    output = jnp.zeros((FH * FW, OUTC), jnp.float32)
    grad_motion = jnp.zeros((FH * FW, HID), jnp.float32)
    conv_terms = []
    for tap_row in range(3):
        for tap_col in range(3):
            window = motion_pad[tap_row:tap_row + FH, tap_col:tap_col + FW].reshape(-1, HID)
            output = output + jnp.dot(window, conv_weight[tap_row, tap_col], preferred_element_type=jnp.float32)
            back = cot_pad[2 - tap_row:2 - tap_row + FH, 2 - tap_col:2 - tap_col + FW].reshape(-1, OUTC)
            grad_motion = grad_motion + jnp.dot(back, conv_weight[tap_row, tap_col].T, preferred_element_type=jnp.float32)
            conv_terms.append(jnp.dot(window.T, flat_cot, preferred_element_type=jnp.float32))
    motion_features = output.astype(jnp.bfloat16).reshape(FH, FW, OUTC)
    conv_weight_grad = jnp.stack(conv_terms).reshape(3, 3, HID, OUTC)
    sigma = jax.nn.sigmoid(pre)
    context_grad = (grad_motion * sigma * (1.0 + pre * (1.0 - sigma))).astype(jnp.bfloat16)
    corr_weight_grad = jnp.dot(corr_feat.T, context_grad, preferred_element_type=jnp.float32)
    grad_corr = jnp.dot(context_grad, corr_weight.T, preferred_element_type=jnp.float32).astype(jnp.bfloat16)
    grad_tiles = to_tiles(grad_corr.reshape(FH, FW, width)).reshape(count_tiles, TR, TC, SLOTS, span, span)

    def backward_tile(tile, carry):
        first_grads, second_grads = carry
        first, parts, mask, row_src, col_src = pick(tile)

        def local_corr(left, right):
            return tile_correlation(left, right, mask)
        unused, pull = jax.vjp(local_corr, first, parts)
        grad_first, grad_parts = pull(grad_tiles[tile].astype(jnp.float32))
        first_grads = first_grads.at[tile].set(grad_first)
        second_grads = second_grads.at[row_src, col_src].add(grad_parts)
        return (first_grads, second_grads)
    start = (jnp.zeros((count_tiles, TR, TC, CH), jnp.float32), jnp.zeros((N_ROW + 2, N_COL + 4, TR, TC, CH), jnp.float32))
    first_grads, second_grads = lax.fori_loop(0, count_tiles, backward_tile, start)
    frame_one_grad = to_frame(first_grads.reshape(N_ROW, N_COL, TR, TC, CH))
    frame_two_grad = to_frame(second_grads[1:1 + N_ROW, 2:2 + N_COL])
    return (motion_features, context_grad.reshape(FH, FW, HID), frame_one_grad, frame_two_grad, corr_weight_grad, conv_weight_grad)
```

```python
import functools
import math

import jax
import jax.numpy as jnp
from jax import lax
from jax.experimental import pallas as pl
from jax.experimental.pallas import tpu as pltpu
from jax.sharding import PartitionSpec as P

REACH = 4
SPAN = 2 * REACH + 1
GROUP = 128
WINDOW = 384
LEAD, LEAD_BACK = 3, 4
F32 = jnp.float32
BF16 = jnp.bfloat16
VMEM_LIMIT = 56 * 1024 * 1024
VMEM = pl.BlockSpec(memory_space=pltpu.VMEM)
SMEM = pl.BlockSpec(memory_space=pltpu.SMEM)
ANY = pl.BlockSpec(memory_space=pl.ANY)


def from_behind(array, axis, by):
    peers = lax.axis_size(axis)
    pairs = [(i, i + by) for i in range(peers) if 0 <= i + by < peers]
    return lax.ppermute(array, axis, pairs)


def swap(array, axis, bits):
    return lax.ppermute(array, axis, [(i, i ^ bits) for i in range(lax.axis_size(axis))])


def with_halo(cells, sides, width):
    for axis, dim in sides:
        count = lax.axis_size(axis)
        ends = count - 1
        head = lax.slice_in_dim(cells, 0, width, axis=dim)
        tail = lax.slice_in_dim(cells, cells.shape[dim] - width, cells.shape[dim], axis=dim)
        cells = jnp.concatenate(
            [
                lax.ppermute(tail, axis, [(i, (i + 1) % count) for i in range(ends)]),
                cells,
                lax.ppermute(head, axis, [((i + 1) % count, i) for i in range(ends)]),
            ],
            axis=dim,
        )
    return cells


def tap_mask(radius, lead, backwards):
    cell = lax.broadcasted_iota(jnp.int32, (GROUP, WINDOW), 0)
    cell = GROUP - 1 - cell if backwards else cell
    tap = lax.broadcasted_iota(jnp.int32, (GROUP, WINDOW), 1)
    down = (tap >> 5) - REACH
    across = (tap & 31) - lead - REACH
    column = (cell & 31) + across
    return (
        (jnp.abs(down) <= radius)
        & (jnp.abs(across) <= radius)
        & (column >= 0)
        & (column < 32)
    )


def forward_kernel(
    info,
    first,
    context,
    cot_taps,
    corr_weight,
    back_weight,
    own,
    rows,
    sides,
    corners,
    near_own,
    near_rows,
    parts,
    motion,
    context_grad,
    weights_sent,
    weights_kept,
    taps,
    weight_grads,
    sems,
):
    cells = first.shape[0]
    slots = parts.shape[0]
    source = {}
    for o in range(15):
        dy, dx = o // 5 - 1, o % 5 - 2
        if dy == 0:
            source[o] = {
                0: own,
                -2: sides.at[0],
                2: sides.at[1],
                -1: near_own.at[0],
                1: near_own.at[1],
            }[dx]
        else:
            r = (dy + 1) // 2
            source[o] = {
                0: rows.at[r],
                -2: corners.at[r],
                2: corners.at[2 + r],
                -1: near_rows.at[r],
                1: near_rows.at[2 + r],
            }[dx]
    for k in range(slots):
        for o in range(15):
            @pl.when(info[k] == o)
            def _():
                pltpu.make_async_copy(
                    source[o], parts.at[k, pl.ds(GROUP, cells)], sems.at[k]
                ).start()
        parts[k, :GROUP] = jnp.zeros((GROUP, parts.shape[2]), BF16)
        parts[k, GROUP + cells :] = jnp.zeros((GROUP, parts.shape[2]), BF16)
    inside = tap_mask(info[slots + 1], LEAD, True)
    flip = (
        lax.broadcasted_iota(jnp.int32, (GROUP, GROUP), 0)
        + lax.broadcasted_iota(jnp.int32, (GROUP, GROUP), 1)
        == GROUP - 1
    ).astype(F32).astype(BF16)
    gains = []
    for k in range(slots):
        live = jnp.where(k < info[slots], 1.0 / math.sqrt(first.shape[1]), 0.0).astype(F32)
        gains.append(jnp.where(inside, live, 0.0))
    for k in range(slots):
        pltpu.make_async_copy(own, parts.at[k, pl.ds(GROUP, cells)], sems.at[k]).wait()
    for q in range(cells // GROUP):
        at = slice(q * GROUP, (q + 1) * GROUP)
        features = jnp.dot(flip, first[at], preferred_element_type=F32).astype(BF16)
        for k in range(slots):
            scores = lax.dot_general(
                features,
                parts[k, q * GROUP : q * GROUP + WINDOW],
                (((1,), (1,)), ((), ())),
                preferred_element_type=F32,
            )
            turn = WINDOW + REACH + LEAD - (GROUP - 1)
            band = pltpu.roll(scores, turn, 1, stride=1, stride_axis=0) * gains[k]
            packed = (
                band[:, :128]
                + pltpu.roll(band[:, 128:256], SPAN, 1)
                + pltpu.roll(band[:, 256:], 2 * SPAN, 1)
            )
            taps[at, k * 128 : (k + 1) * 128] = jnp.dot(
                flip, packed.astype(BF16), preferred_element_type=F32
            ).astype(BF16)
        pre = jnp.dot(taps[at], corr_weight[...], preferred_element_type=F32) + context[
            at
        ].astype(F32)
        grad_motion = jnp.zeros_like(pre)
        for a in range(3):
            start = (2 - a) * 32 + q * GROUP
            grad_motion += jnp.dot(
                cot_taps[start : start + GROUP], back_weight[a], preferred_element_type=F32
            )
        sigma = jax.nn.sigmoid(pre)
        motion[at] = (pre * sigma).astype(BF16)
        context_grad[at] = (grad_motion * sigma * (1.0 + pre * (1.0 - sigma))).astype(BF16)
    over_cells = (((0,), (0,)), ((), ()))
    for a in range(3):
        start = (2 - a) * 32
        term = lax.dot_general(
            motion[...], cot_taps[start : start + cells], over_cells, preferred_element_type=F32
        )
        for b in range(3):
            weight_grads[(3 * a + b) * 256 : (3 * a + b + 1) * 256] = term[
                :, b * 128 : (b + 1) * 128
            ]
    term = lax.dot_general(taps[...], context_grad[...], over_cells, preferred_element_type=F32)
    base = 9 * 256
    for h in range(2):
        weight_grads[base + h * 384 + 320 : base + (h + 1) * 384] = jnp.zeros((64, 128), F32)
        for k in range(slots):
            for u in range(SPAN):
                row = k * 128 + (u % 4) * 32 + (u // 4) * SPAN + LEAD
                to = base + h * 384 + (k * SPAN + u) * SPAN
                weight_grads[to : to + SPAN] = term[row : row + SPAN, h * 128 : (h + 1) * 128]
    half = weight_grads.shape[0] // 2
    core = info[slots + 2]
    weights_kept[...] = weight_grads[pl.ds(pl.multiple_of(core * half, half), half)]
    weights_sent[...] = weight_grads[pl.ds(pl.multiple_of((1 - core) * half, half), half)].astype(
        BF16
    )


def backward_kernel(
    info, first, context_grad, corr_weight, parts, first_grad, kept, lent, totals
):
    cells = first.shape[0]
    slots = parts.shape[0]
    scale = 1.0 / math.sqrt(first.shape[1])
    inside = tap_mask(info[slots + 1], LEAD_BACK, False)
    totals[...] = jnp.zeros_like(totals)
    kept[...] = jnp.zeros_like(kept)
    lent[...] = jnp.zeros_like(lent)
    for q in range(cells // GROUP):
        at = slice(q * GROUP, (q + 1) * GROUP)
        packed = (
            lax.dot_general(
                context_grad[at],
                corr_weight[...],
                (((1,), (1,)), ((), ())),
                preferred_element_type=F32,
            )
            .astype(BF16)
            .astype(F32)
        )
        first_here = jnp.zeros((GROUP, first.shape[1]), F32)
        for k in range(slots):
            mine = packed[:, k * 128 : (k + 1) * 128]
            band = jnp.concatenate(
                [mine, pltpu.roll(mine, 128 - SPAN, 1), pltpu.roll(mine, 128 - 2 * SPAN, 1)],
                axis=1,
            )
            band = jnp.where(inside & (k < info[slots]), band, 0.0)
            scores = pltpu.roll(band, WINDOW - REACH - LEAD_BACK, 1, stride=1, stride_axis=0).astype(BF16)
            window = slice(q * GROUP, q * GROUP + WINDOW)
            first_here += jnp.dot(scores, parts[k, window], preferred_element_type=F32)
            totals[k, window] += lax.dot_general(
                scores, first[at], (((0,), (0,)), ((), ())), preferred_element_type=F32
            )
        first_grad[at] = first_here * scale
    for k in range(slots):
        value = (totals[k, GROUP : GROUP + cells] * scale).astype(BF16)
        down, across = info[k] // 5, info[k] % 5
        even = across % 2 == 0

        @pl.when(even)
        def _():
            kept[down * 3 + across // 2] = value

        @pl.when(jnp.logical_not(even))
        def _():
            lent[down * 2 + across // 2] = value


def features_kernel(motion_taps, weight, out):
    cells = out.shape[0]
    total = jnp.zeros(out.shape, F32)
    for a in range(3):
        total += jnp.dot(
            motion_taps[a * 32 : a * 32 + cells], weight[a], preferred_element_type=F32
        )
    out[...] = total.astype(BF16)


def finish_kernel(info, s0, s1, s2, s3, far, conv, corr, whole):
    size = s0.shape[0]
    core, chip = info[6], info[7]
    half = whole.shape[0] // 2
    for s, ref in enumerate((s0, s1, s2, s3)):
        other = chip ^ s
        to = pl.multiple_of(core * half + other * size, size)
        whole[pl.ds(to, size)] = ref[...].astype(F32)
        to = pl.multiple_of((1 - core) * half + other * size, size)
        whole[pl.ds(to, size)] = far[s].astype(F32)
    conv[...] = whole[: conv.shape[0]]
    base = conv.shape[0]
    for h in range(2):
        corr[:, h * 128 : (h + 1) * 128] = whole[base + h * 384 : base + h * 384 + corr.shape[0]]


def call(kernel, out_shape, in_specs, scratch=(), flops=0):
    return pl.pallas_call(
        kernel,
        out_shape=out_shape,
        in_specs=in_specs,
        out_specs=jax.tree.map(lambda _: VMEM, out_shape),
        scratch_shapes=list(scratch),
        compiler_params=pltpu.CompilerParams(vmem_limit_bytes=VMEM_LIMIT),
        cost_estimate=pl.CostEstimate(flops=flops, bytes_accessed=flops // 300, transcendentals=0),
    )


def sum_weights(sent, kept):
    cur = kept + swap(sent, "col", 1).astype(F32)
    size = cur.shape[0] // 4
    chip = lax.axis_index("col") // 2
    pieces = [
        lax.dynamic_slice_in_dim(cur, (chip ^ s) * size, size, axis=0) for s in range(4)
    ]
    got = [swap(pieces[s].astype(BF16), "col", 2 * s).astype(F32) for s in (1, 2, 3)]
    cur = (pieces[0] + got[0]) + (got[1] + got[2])
    for unit in (1, 4):
        mine = cur.astype(BF16)
        got = [swap(mine, "row", unit * s).astype(F32) for s in (1, 2, 3)]
        cur = (mine.astype(F32) + got[0]) + (got[1] + got[2])
    mine = cur.astype(BF16)
    shards = [mine] + [swap(mine, "col", 2 * s) for s in (1, 2, 3)]
    far = swap(jnp.stack(shards), "col", 1)
    return shards, far


def body(
    frame_one, frame_two, context, cotangent, corr_weight, conv_weight, partners, counts, radius
):
    rows_tile, cols_tile, channels = frame_one.shape
    slots = partners.shape[-1]
    cells = rows_tile * cols_tile
    hidden = context.shape[-1]
    out_width = conv_weight.shape[-1]
    col = lax.axis_index("col")
    core = col % 2
    info = jnp.concatenate(
        [
            partners[0, 0],
            counts[0],
            radius[0],
            core[None].astype(jnp.int32),
            (col // 2)[None].astype(jnp.int32),
        ]
    )
    first = frame_one.reshape(cells, channels)
    own = frame_two.reshape(cells, channels)
    up, down = from_behind(own, "row", 1), from_behind(own, "row", -1)
    rows = jnp.stack([up, down])
    west, east = from_behind(own, "col", 2), from_behind(own, "col", -2)
    sides = jnp.stack([west, east])
    far_west, far_east = from_behind(rows, "col", 2), from_behind(rows, "col", -2)
    corners = jnp.concatenate([far_west, far_east])
    second_core = core == 1
    near_own = swap(
        jnp.stack([jnp.where(second_core, west, own), jnp.where(second_core, own, east)]),
        "col",
        1,
    )
    near_rows = swap(
        jnp.concatenate(
            [jnp.where(second_core, far_west, rows), jnp.where(second_core, rows, far_east)]
        ),
        "col",
        1,
    )
    grad_rim = with_halo(cotangent, (("row", 0), ("col", 1)), 1)
    cot_taps = jnp.concatenate(
        [grad_rim[:, 2 - b : 2 - b + cols_tile] for b in range(3)], axis=2
    ).reshape((rows_tile + 2) * cols_tile, 3 * out_width)
    spread = jnp.pad(
        corr_weight.reshape(slots, SPAN, SPAN, hidden), ((0, 0), (0, 3), (0, 0), (0, 0))
    )
    spread = spread.reshape(slots, 3, 4, SPAN, hidden).transpose(0, 2, 1, 3, 4)
    spread = spread.reshape(slots, 4, 3 * SPAN, hidden)
    spread, spread_back = (
        jnp.pad(spread, ((0, 0), (0, 0), (lead, 5 - lead), (0, 0))).reshape(slots * 128, hidden)
        for lead in (LEAD, LEAD_BACK)
    )
    back_weight = conv_weight.transpose(0, 1, 3, 2).reshape(3, 3 * out_width, hidden)
    shape = jax.ShapeDtypeStruct
    total_rows = 9 * hidden + 2 * 384
    parts, motion, context_grad, weights_sent, weights_kept = call(
        forward_kernel,
        (
            shape((slots, cells + 2 * GROUP, channels), BF16),
            shape((cells, hidden), BF16),
            shape((cells, hidden), BF16),
            shape((total_rows // 2, 128), BF16),
            shape((total_rows // 2, 128), F32),
        ),
        [SMEM] + [VMEM] * 5 + [ANY] * 6,
        [
            pltpu.VMEM((cells, slots * 128), BF16),
            pltpu.VMEM((total_rows, 128), F32),
            pltpu.SemaphoreType.DMA((slots,)),
        ],
        flops=3 * 10**9,
    )(
        info,
        first,
        context.reshape(cells, hidden),
        cot_taps,
        spread,
        back_weight,
        own,
        rows,
        sides,
        corners,
        near_own,
        near_rows,
    )
    shards, far = sum_weights(weights_sent, weights_kept)
    first_grad, kept, lent = call(
        backward_kernel,
        (
            shape((cells, channels), F32),
            shape((9, cells, channels), BF16),
            shape((6, cells, channels), BF16),
        ),
        [SMEM] + [VMEM] * 4,
        [pltpu.VMEM((slots, cells + 2 * GROUP, channels), F32)],
        flops=3 * 10**9,
    )(info, first, context_grad, spread_back, parts)
    kept = kept.reshape(3, 3, cells, channels).astype(F32)
    lent = swap(lent, "col", 1).reshape(3, 2, cells, channels).astype(F32)
    to_west = kept[:, 0] + jnp.where(second_core, lent[:, 0], 0.0)
    middle = kept[:, 1] + jnp.where(second_core, lent[:, 1], lent[:, 0])
    to_east = kept[:, 2] + jnp.where(second_core, 0.0, lent[:, 1])
    middle = middle + from_behind(to_west.astype(BF16), "col", -2).astype(F32)
    middle = middle + from_behind(to_east.astype(BF16), "col", 2).astype(F32)
    second_grad = middle[1]
    second_grad = second_grad + from_behind(middle[0].astype(BF16), "row", -1).astype(F32)
    second_grad = second_grad + from_behind(middle[2].astype(BF16), "row", 1).astype(F32)
    rimmed = with_halo(
        motion.reshape(rows_tile, cols_tile, hidden), (("row", 0), ("col", 1)), 1
    )
    motion_taps = jnp.concatenate(
        [rimmed[:, b : b + cols_tile] for b in range(3)], axis=2
    ).reshape((rows_tile + 2) * cols_tile, 3 * hidden)
    features = call(features_kernel, shape((cells, out_width), BF16), [VMEM] * 2, flops=10**9)(
        motion_taps, conv_weight.reshape(3, 3 * hidden, out_width)
    )
    conv_total, corr_total = call(
        finish_kernel,
        (shape((9 * hidden, out_width), F32), shape(corr_weight.shape, F32)),
        [SMEM] + [VMEM] * 5,
        [pltpu.VMEM((total_rows, 128), F32)],
    )(info, *shards, far)
    return (
        features.reshape(rows_tile, cols_tile, out_width),
        context_grad.reshape(rows_tile, cols_tile, hidden),
        first_grad.reshape(frame_one.shape),
        second_grad.reshape(frame_two.shape),
        corr_total,
        conv_total.reshape(conv_weight.shape),
    )


def solution(mesh):
    return jax.shard_map(
        body,
        mesh=mesh,
        in_specs=(
            P("row", "col", None),
            P("row", "col", None),
            P("row", "col", None),
            P("row", "col", None),
            P(),
            P(),
            P("row", "col", None),
            P("row", "col"),
            P("row", "col"),
        ),
        out_specs=(
            P("row", "col", None),
            P("row", "col", None),
            P("row", "col", None),
            P("row", "col", None),
            P(),
            P(),
        ),
        check_vma=False,
    )
```

```python
import functools
import math

import jax
import jax.numpy as jnp
from jax import lax
from jax.experimental import pallas as pl
from jax.experimental.pallas import tpu as pltpu
from jax.sharding import PartitionSpec as P

REACH = 4
SPAN = 2 * REACH + 1
GROUP = 128
WINDOW = 384
LEAD, LEAD_BACK = 3, 4
F32 = jnp.float32
BF16 = jnp.bfloat16
VMEM_LIMIT = 56 * 1024 * 1024
VMEM = pl.BlockSpec(memory_space=pltpu.VMEM)
SMEM = pl.BlockSpec(memory_space=pltpu.SMEM)
ANY = pl.BlockSpec(memory_space=pl.ANY)


def swap(array, axis, bits):
    return lax.ppermute(array, axis, [(i, i ^ bits) for i in range(lax.axis_size(axis))])


def swap_pairs(array, axis, odd, unit=1):
    count = lax.axis_size(axis) // unit
    pairs = []
    for i in range(odd, count - 1, 2):
        for low in range(unit):
            here, there = i * unit + low, (i + 1) * unit + low
            pairs += [(here, there), (there, here)]
    return lax.ppermute(array, axis, pairs)


def rim(cells, row_even, col_even):
    top, bottom = cells[0], cells[-1]
    even = swap_pairs(jnp.where(row_even, bottom, top), "row", 0)
    odd = swap_pairs(jnp.where(row_even, top, bottom), "row", 1)
    north, south = jnp.where(row_even, odd, even), jnp.where(row_even, even, odd)
    left = jnp.concatenate([north[:1], cells[:, 0], south[:1]])
    right = jnp.concatenate([north[-1:], cells[:, -1], south[-1:]])
    even = swap_pairs(jnp.where(col_even, right, left), "col", 0)
    odd = swap_pairs(jnp.where(col_even, left, right), "col", 1)
    west, east = jnp.where(col_even, odd, even), jnp.where(col_even, even, odd)
    return north, south, west, east


def write_taps(taps, own, north, south, west, east, backwards):
    width = own.shape[1]
    line = north.shape[0]
    taps[:line, width : 2 * width] = north[...]
    taps[line:-line, width : 2 * width] = own[...]
    taps[-line:, width : 2 * width] = south[...]
    middle = taps[:, width : 2 * width].astype(F32)
    place = lax.broadcasted_iota(jnp.int32, middle.shape, 0) % line

    def stretched(ends):
        shape = (ends.shape[0], line, width)
        return jnp.broadcast_to(ends[...].astype(F32)[:, None], shape).reshape(middle.shape)

    left = jnp.where(place == 0, stretched(west), pltpu.roll(middle, 1, 0)).astype(BF16)
    right = jnp.where(
        place == line - 1, stretched(east), pltpu.roll(middle, middle.shape[0] - 1, 0)
    ).astype(BF16)
    taps[:, :width] = right if backwards else left
    taps[:, 2 * width :] = left if backwards else right


def tap_mask(radius, lead, backwards):
    cell = lax.broadcasted_iota(jnp.int32, (GROUP, WINDOW), 0)
    cell = GROUP - 1 - cell if backwards else cell
    tap = lax.broadcasted_iota(jnp.int32, (GROUP, WINDOW), 1)
    down = (tap >> 5) - REACH
    across = (tap & 31) - lead - REACH
    column = (cell & 31) + across
    return (
        (jnp.abs(down) <= radius)
        & (jnp.abs(across) <= radius)
        & (column >= 0)
        & (column < 32)
    )


def flip_matrix():
    return (
        (
            lax.broadcasted_iota(jnp.int32, (GROUP, GROUP), 0)
            + lax.broadcasted_iota(jnp.int32, (GROUP, GROUP), 1)
            == GROUP - 1
        )
        .astype(F32)
        .astype(BF16)
    )


def early_kernel(
    first, cotangent, north, south, west, east, back_weight, cot_taps, grad_motion, flipped
):
    cells = first.shape[0]
    write_taps(cot_taps, cotangent, north, south, west, east, True)
    total = jnp.zeros(grad_motion.shape, F32)
    for a in range(3):
        start = (2 - a) * 32
        total += jnp.dot(
            cot_taps[start : start + cells], back_weight[a], preferred_element_type=F32
        )
    grad_motion[...] = total
    flip = flip_matrix()
    for q in range(cells // GROUP):
        at = slice(q * GROUP, (q + 1) * GROUP)
        flipped[at] = jnp.dot(flip, first[at], preferred_element_type=F32).astype(BF16)


def forward_kernel(info, flipped, context, cot_taps, grad_motion, corr_weight, *refs):
    tiles, refs = refs[:18], refs[18:]
    parts, motion, context_grad, weights_sent, weights_kept, taps, weight_grads, sems = refs
    cells = flipped.shape[0]
    slots = parts.shape[0]
    for k in range(slots):
        for t in range(18):
            @pl.when(info[k] == t)
            def _():
                pltpu.make_async_copy(
                    tiles[t], parts.at[k, pl.ds(GROUP, cells)], sems.at[k]
                ).start()
        parts[k, :GROUP] = jnp.zeros((GROUP, parts.shape[2]), BF16)
        parts[k, GROUP + cells :] = jnp.zeros((GROUP, parts.shape[2]), BF16)
    inside = tap_mask(info[slots + 1], LEAD, True)
    flip = flip_matrix()
    gains = []
    for k in range(slots):
        live = jnp.where(k < info[slots], 1.0 / math.sqrt(flipped.shape[1]), 0.0).astype(F32)
        gains.append(jnp.where(inside, live, 0.0))
    for k in range(slots):
        pltpu.make_async_copy(tiles[0], parts.at[k, pl.ds(GROUP, cells)], sems.at[k]).wait()
    for q in range(cells // GROUP):
        at = slice(q * GROUP, (q + 1) * GROUP)
        features = flipped[at]
        for k in range(slots):
            scores = lax.dot_general(
                features,
                parts[k, q * GROUP : q * GROUP + WINDOW],
                (((1,), (1,)), ((), ())),
                preferred_element_type=F32,
            )
            turn = WINDOW + REACH + LEAD - (GROUP - 1)
            band = pltpu.roll(scores, turn, 1, stride=1, stride_axis=0) * gains[k]
            packed = (
                band[:, :128]
                + pltpu.roll(band[:, 128:256], SPAN, 1)
                + pltpu.roll(band[:, 256:], 2 * SPAN, 1)
            )
            taps[at, k * 128 : (k + 1) * 128] = jnp.dot(
                flip, packed.astype(BF16), preferred_element_type=F32
            ).astype(BF16)
    pre = jnp.dot(taps[...], corr_weight[...], preferred_element_type=F32) + context[...].astype(
        F32
    )
    sigma = jax.nn.sigmoid(pre)
    motion[...] = (pre * sigma).astype(BF16)
    context_grad[...] = (grad_motion[...] * sigma * (1.0 + pre * (1.0 - sigma))).astype(BF16)
    over_cells = (((0,), (0,)), ((), ()))
    for a in range(3):
        start = (2 - a) * 32
        term = lax.dot_general(
            motion[...], cot_taps[start : start + cells], over_cells, preferred_element_type=F32
        )
        for b in range(3):
            weight_grads[(3 * a + b) * 256 : (3 * a + b + 1) * 256] = term[
                :, b * 128 : (b + 1) * 128
            ]
    term = lax.dot_general(taps[...], context_grad[...], over_cells, preferred_element_type=F32)
    base = 9 * 256
    for h in range(2):
        weight_grads[base + h * 384 + 320 : base + (h + 1) * 384] = jnp.zeros((64, 128), F32)
        for k in range(slots):
            for u in range(SPAN):
                row = k * 128 + (u % 4) * 32 + (u // 4) * SPAN + LEAD
                to = base + h * 384 + (k * SPAN + u) * SPAN
                weight_grads[to : to + SPAN] = term[row : row + SPAN, h * 128 : (h + 1) * 128]
    half = weight_grads.shape[0] // 2
    core = info[slots + 2]
    weights_kept[...] = weight_grads[pl.ds(pl.multiple_of(core * half, half), half)]
    weights_sent[...] = weight_grads[pl.ds(pl.multiple_of((1 - core) * half, half), half)].astype(
        BF16
    )


def backward_kernel(
    info, first, context_grad, corr_weight, parts, first_grad, kept, lent, totals
):
    cells = first.shape[0]
    slots = parts.shape[0]
    scale = 1.0 / math.sqrt(first.shape[1])
    inside = tap_mask(info[slots + 1], LEAD_BACK, False)
    totals[...] = jnp.zeros_like(totals)
    kept[...] = jnp.zeros_like(kept)
    lent[...] = jnp.zeros_like(lent)
    for q in range(cells // GROUP):
        at = slice(q * GROUP, (q + 1) * GROUP)
        packed = (
            lax.dot_general(
                context_grad[at],
                corr_weight[...],
                (((1,), (1,)), ((), ())),
                preferred_element_type=F32,
            )
            .astype(BF16)
            .astype(F32)
        )
        first_here = jnp.zeros((GROUP, first.shape[1]), F32)
        for k in range(slots):
            mine = packed[:, k * 128 : (k + 1) * 128]
            band = jnp.concatenate(
                [mine, pltpu.roll(mine, 128 - SPAN, 1), pltpu.roll(mine, 128 - 2 * SPAN, 1)],
                axis=1,
            )
            band = jnp.where(inside & (k < info[slots]), band, 0.0)
            scores = pltpu.roll(band, WINDOW - REACH - LEAD_BACK, 1, stride=1, stride_axis=0).astype(BF16)
            window = slice(q * GROUP, q * GROUP + WINDOW)
            first_here += jnp.dot(scores, parts[k, window], preferred_element_type=F32)
            totals[k, window] += lax.dot_general(
                scores, first[at], (((0,), (0,)), ((), ())), preferred_element_type=F32
            )
        first_grad[at] = first_here * scale
    for k in range(slots):
        value = (totals[k, GROUP : GROUP + cells] * scale).astype(BF16)
        place = info[k]
        same = place % 2 == 0

        @pl.when(same)
        def _():
            kept[place // 2] = value

        @pl.when(jnp.logical_not(same))
        def _():
            lent[place // 6 * 2 + (place % 6 > 1).astype(jnp.int32)] = value


def features_kernel(motion, north, south, west, east, weight, out, taps):
    cells = out.shape[0]
    write_taps(taps, motion, north, south, west, east, False)
    total = jnp.zeros(out.shape, F32)
    for a in range(3):
        total += jnp.dot(taps[a * 32 : a * 32 + cells], weight[a], preferred_element_type=F32)
    out[...] = total.astype(BF16)


def finish_kernel(info, *refs):
    shards, (conv, corr, whole) = refs[:8], refs[8:]
    size = shards[0].shape[0]
    core, chip = info[6], info[7]
    half = whole.shape[0] // 2
    for s in range(4):
        other = chip ^ s
        to = pl.multiple_of(core * half + other * size, size)
        whole[pl.ds(to, size)] = shards[s][...].astype(F32)
        to = pl.multiple_of((1 - core) * half + other * size, size)
        whole[pl.ds(to, size)] = shards[4 + s][...].astype(F32)
    conv[...] = whole[: conv.shape[0]]
    base = conv.shape[0]
    for h in range(2):
        corr[:, h * 128 : (h + 1) * 128] = whole[base + h * 384 : base + h * 384 + corr.shape[0]]


def call(kernel, out_shape, in_specs, scratch=(), flops=0):
    return pl.pallas_call(
        kernel,
        out_shape=out_shape,
        in_specs=in_specs,
        out_specs=jax.tree.map(lambda _: VMEM, out_shape),
        scratch_shapes=list(scratch),
        compiler_params=pltpu.CompilerParams(vmem_limit_bytes=VMEM_LIMIT),
        cost_estimate=pl.CostEstimate(flops=flops, bytes_accessed=flops // 300, transcendentals=0),
    )


def sum_weights(sent, kept):
    cur = kept + swap(sent, "col", 1).astype(F32)
    size = cur.shape[0] // 4
    chip = lax.axis_index("col") // 2
    pieces = [
        lax.dynamic_slice_in_dim(cur, (chip ^ s) * size, size, axis=0) for s in range(4)
    ]
    got = [swap(pieces[s].astype(BF16), "col", 2 * s).astype(F32) for s in (1, 2, 3)]
    cur = (pieces[0] + got[0]) + (got[1] + got[2])
    for unit in (1, 4):
        mine = cur.astype(BF16)
        got = [swap(mine, "row", unit * s).astype(F32) for s in (1, 2, 3)]
        cur = (mine.astype(F32) + got[0]) + (got[1] + got[2])
    mine = cur.astype(BF16)
    shards = [mine] + [swap(mine, "col", 2 * s) for s in (1, 2, 3)]
    return shards + [swap(shard, "col", 1) for shard in shards]


def body(
    frame_one, frame_two, context, cotangent, corr_weight, conv_weight, partners, counts, radius
):
    rows_tile, cols_tile, channels = frame_one.shape
    slots = partners.shape[-1]
    cells = rows_tile * cols_tile
    hidden = context.shape[-1]
    out_width = conv_weight.shape[-1]
    row, col = lax.axis_index("row"), lax.axis_index("col")
    core, chip = col % 2, col // 2
    row_even, chip_even, col_even = row % 2 == 0, chip % 2 == 0, core == 0

    def role(step, even):
        return jnp.where(step == 0, 0, jnp.where((step > 0) == even, 1, 2))

    down, across = partners[0, 0] // 5 - 1, partners[0, 0] % 5 - 2
    chip_step = (core + across) >> 1
    place = role(down, row_even) * 6 + role(chip_step, chip_even) * 2 + (across & 1)
    info = jnp.concatenate(
        [place, counts[0], radius[0], core[None], chip[None]]
    ).astype(jnp.int32)
    first = frame_one.reshape(cells, channels)
    own = frame_two.reshape(cells, channels)
    tiles = {(0, 0): own}
    for r in (1, 2):
        tiles[r, 0] = swap_pairs(own, "row", r - 1)
        tiles[0, r] = swap_pairs(own, "col", r - 1, 2)
    for r in (1, 2):
        tiles[r, r] = swap_pairs(tiles[r, 0], "col", r - 1, 2)
        tiles[r, 3 - r] = swap_pairs(tiles[0, 3 - r], "row", r - 1)
    around = []
    for r in range(3):
        for x in range(3):
            around += [tiles[r, x], swap(tiles[r, x], "col", 1)]
    spread = jnp.pad(
        corr_weight.reshape(slots, SPAN, SPAN, hidden), ((0, 0), (0, 3), (0, 0), (0, 0))
    )
    spread = spread.reshape(slots, 3, 4, SPAN, hidden).transpose(0, 2, 1, 3, 4)
    spread = spread.reshape(slots, 4, 3 * SPAN, hidden)
    spread, spread_back = (
        jnp.pad(spread, ((0, 0), (0, 0), (lead, 5 - lead), (0, 0))).reshape(slots * 128, hidden)
        for lead in (LEAD, LEAD_BACK)
    )
    back_weight = conv_weight.transpose(0, 1, 3, 2).reshape(3, 3 * out_width, hidden)
    shape = jax.ShapeDtypeStruct
    total_rows = 9 * hidden + 2 * 384
    cot_taps, grad_motion, flipped = call(
        early_kernel,
        (
            shape(((rows_tile + 2) * cols_tile, 3 * out_width), BF16),
            shape((cells, hidden), F32),
            shape((cells, channels), BF16),
        ),
        [VMEM] * 7,
        flops=10**9,
    )(
        first,
        cotangent.reshape(cells, out_width),
        *rim(cotangent, row_even, col_even),
        back_weight,
    )
    parts, motion, context_grad, weights_sent, weights_kept = call(
        forward_kernel,
        (
            shape((slots, cells + 2 * GROUP, channels), BF16),
            shape((cells, hidden), BF16),
            shape((cells, hidden), BF16),
            shape((total_rows // 2, 128), BF16),
            shape((total_rows // 2, 128), F32),
        ),
        [SMEM] + [VMEM] * 5 + [ANY] * 18,
        [
            pltpu.VMEM((cells, slots * 128), BF16),
            pltpu.VMEM((total_rows, 128), F32),
            pltpu.SemaphoreType.DMA((slots,)),
        ],
        flops=3 * 10**9,
    )(info, flipped, context.reshape(cells, hidden), cot_taps, grad_motion, spread, *around)
    shards = sum_weights(weights_sent, weights_kept)
    first_grad, kept, lent = call(
        backward_kernel,
        (
            shape((cells, channels), F32),
            shape((9, cells, channels), BF16),
            shape((6, cells, channels), BF16),
        ),
        [SMEM] + [VMEM] * 4,
        [pltpu.VMEM((slots, cells + 2 * GROUP, channels), F32)],
        flops=3 * 10**9,
    )(info, first, context_grad, spread_back, parts)
    lent = swap(lent, "col", 1).reshape(3, 2, cells, channels).astype(F32)
    kept = kept.reshape(3, 3, cells, channels).astype(F32)
    side = jnp.where((core == 0) == chip_even, 1, 2)
    sums = {}
    for r in range(3):
        sums[r, 0] = kept[r, 0] + lent[r, 0]
        for x in (1, 2):
            sums[r, x] = kept[r, x] + jnp.where(side == x, lent[r, 1], 0.0)
    for r in (1, 2):
        sums[r, 0] += swap_pairs(sums[r, r].astype(BF16), "col", r - 1, 2).astype(F32)
        sums[0, 3 - r] += swap_pairs(sums[r, 3 - r].astype(BF16), "row", r - 1).astype(F32)
    second_grad = sums[0, 0]
    for r in (1, 2):
        second_grad += swap_pairs(sums[r, 0].astype(BF16), "row", r - 1).astype(F32)
        second_grad += swap_pairs(sums[0, r].astype(BF16), "col", r - 1, 2).astype(F32)
    features = call(
        features_kernel,
        shape((cells, out_width), BF16),
        [VMEM] * 6,
        [pltpu.VMEM(((rows_tile + 2) * cols_tile, 3 * hidden), BF16)],
        flops=10**9,
    )(
        motion,
        *rim(motion.reshape(rows_tile, cols_tile, hidden), row_even, col_even),
        conv_weight.reshape(3, 3 * hidden, out_width),
    )
    conv_total, corr_total = call(
        finish_kernel,
        (shape((9 * hidden, out_width), F32), shape(corr_weight.shape, F32)),
        [SMEM] + [VMEM] * 8,
        [pltpu.VMEM((total_rows, 128), F32)],
    )(info, *shards)
    return (
        features.reshape(rows_tile, cols_tile, out_width),
        context_grad.reshape(rows_tile, cols_tile, hidden),
        first_grad.reshape(frame_one.shape),
        second_grad.reshape(frame_two.shape),
        corr_total,
        conv_total.reshape(conv_weight.shape),
    )


def solution(mesh):
    return jax.shard_map(
        body,
        mesh=mesh,
        in_specs=(
            P("row", "col", None),
            P("row", "col", None),
            P("row", "col", None),
            P("row", "col", None),
            P(),
            P(),
            P("row", "col", None),
            P("row", "col"),
            P("row", "col"),
        ),
        out_specs=(
            P("row", "col", None),
            P("row", "col", None),
            P("row", "col", None),
            P("row", "col", None),
            P(),
            P(),
        ),
        check_vma=False,
    )
```

```python
import functools
import math

import jax
import jax.numpy as jnp
from jax import lax
from jax.experimental import pallas as pl
from jax.experimental.pallas import tpu as pltpu
from jax.sharding import PartitionSpec as P

REACH = 4
SPAN = 2 * REACH + 1
GROUP = 128
WINDOW = 384
LEAD, LEAD_BACK = 3, 4
F32 = jnp.float32
BF16 = jnp.bfloat16
VMEM_LIMIT = 56 * 1024 * 1024
VMEM = pl.BlockSpec(memory_space=pltpu.VMEM)
SMEM = pl.BlockSpec(memory_space=pltpu.SMEM)
ANY = pl.BlockSpec(memory_space=pl.ANY)


def swap(array, axis, bits):
    return lax.ppermute(array, axis, [(i, i ^ bits) for i in range(lax.axis_size(axis))])


def swap_pairs(array, axis, odd, unit=1):
    count = lax.axis_size(axis) // unit
    pairs = []
    for i in range(odd, count - 1, 2):
        for low in range(unit):
            here, there = i * unit + low, (i + 1) * unit + low
            pairs += [(here, there), (there, here)]
    return lax.ppermute(array, axis, pairs)


def rim(facing, away, ends, row_even, col_even):
    even = swap_pairs(facing, "row", 0)
    odd = swap_pairs(away, "row", 1)
    north, south = jnp.where(row_even, odd, even), jnp.where(row_even, even, odd)
    left = jnp.concatenate([north[:1], ends[0], south[:1]])
    right = jnp.concatenate([north[-1:], ends[1], south[-1:]])
    even = swap_pairs(jnp.where(col_even, right, left), "col", 0)
    odd = swap_pairs(jnp.where(col_even, left, right), "col", 1)
    west, east = jnp.where(col_even, odd, even), jnp.where(col_even, even, odd)
    return north, south, west, east


def outer_columns(cells):
    count = cells.shape[0]
    line = lax.broadcasted_iota(jnp.int32, (32, count), 0)
    cell = lax.broadcasted_iota(jnp.int32, (32, count), 1)
    wanted = (line & 15) * 32 + (line >> 4) * 31
    pick = (cell == wanted).astype(F32).astype(BF16)
    return jnp.dot(pick, cells[...], preferred_element_type=F32).astype(BF16)


def write_taps(taps, own, north, south, west, east, backwards):
    width = own.shape[1]
    line = north.shape[0]
    taps[:line, width : 2 * width] = north
    taps[line:-line, width : 2 * width] = own[...]
    taps[-line:, width : 2 * width] = south
    middle = taps[:, width : 2 * width].astype(F32)
    place = lax.broadcasted_iota(jnp.int32, middle.shape, 0) % line

    def stretched(ends):
        shape = (ends.shape[0], line, width)
        return jnp.broadcast_to(ends.astype(F32)[:, None], shape).reshape(middle.shape)

    left = jnp.where(place == 0, stretched(west), pltpu.roll(middle, 1, 0)).astype(BF16)
    right = jnp.where(
        place == line - 1, stretched(east), pltpu.roll(middle, middle.shape[0] - 1, 0)
    ).astype(BF16)
    taps[:, :width] = right if backwards else left
    taps[:, 2 * width :] = left if backwards else right


def tap_mask(radius, lead, backwards):
    cell = lax.broadcasted_iota(jnp.int32, (GROUP, WINDOW), 0)
    cell = GROUP - 1 - cell if backwards else cell
    tap = lax.broadcasted_iota(jnp.int32, (GROUP, WINDOW), 1)
    down = (tap >> 5) - REACH
    across = (tap & 31) - lead - REACH
    column = (cell & 31) + across
    return (
        (jnp.abs(down) <= radius)
        & (jnp.abs(across) <= radius)
        & (column >= 0)
        & (column < 32)
    )


def flip_matrix():
    return (
        (
            lax.broadcasted_iota(jnp.int32, (GROUP, GROUP), 0)
            + lax.broadcasted_iota(jnp.int32, (GROUP, GROUP), 1)
            == GROUP - 1
        )
        .astype(F32)
        .astype(BF16)
    )


def pack_kernel(tile, cotangent, out):
    cells = tile.shape[0]
    out[:cells] = tile[...]
    out[cells : cells + 32, :128] = cotangent[:32]
    out[cells : cells + 32, 128:] = cotangent[cells - 32 :]
    ends = outer_columns(cotangent)
    out[cells + 32 :, :128] = ends[:16]
    out[cells + 32 :, 128:] = ends[16:]


def forward_kernel(info, first, context, cotangent, back_weight, corr_weight, *refs):
    tiles, refs = refs[:18], refs[18:]
    parts, motion, context_grad, facing, away, ends, weights_sent, weights_kept = refs[:8]
    edges, cot_taps, taps, weight_grads, sems, edge_sems = refs[8:]
    cells = first.shape[0]
    slots = parts.shape[0]
    row_sides, chip_sides = (6, 12), (1, 3, 5)
    options = [row_sides] * 2 + [chip_sides] * 2 + [[r + x for r in row_sides for x in chip_sides]] * 4
    for n in range(8):
        for t in options[n]:
            @pl.when(info[8 + n] == t)
            def _():
                pltpu.make_async_copy(
                    tiles[t].at[pl.ds(cells, 48)], edges.at[n], edge_sems.at[n]
                ).start()
    for k in range(slots):
        for t in range(18):
            @pl.when(info[k] == t)
            def _():
                pltpu.make_async_copy(
                    tiles[t].at[pl.ds(0, cells)], parts.at[k, pl.ds(GROUP, cells)], sems.at[k]
                ).start()
        parts[k, :GROUP] = jnp.zeros((GROUP, parts.shape[2]), BF16)
        parts[k, GROUP + cells :] = jnp.zeros((GROUP, parts.shape[2]), BF16)
    inside = tap_mask(info[slots + 1], LEAD, True)
    flip = flip_matrix()
    gains = []
    for k in range(slots):
        live = jnp.where(k < info[slots], 1.0 / math.sqrt(first.shape[1]), 0.0).astype(F32)
        gains.append(jnp.where(inside, live, 0.0))
    for n in range(8):
        pltpu.make_async_copy(tiles[0].at[pl.ds(cells, 48)], edges.at[n], edge_sems.at[n]).wait()
    north, south = edges[0, :32, 128:], edges[1, :32, :128]
    west = jnp.concatenate(
        [
            edges[4, :32, 128:].astype(F32)[31:],
            edges[2, 32:, 128:].astype(F32),
            edges[6, :32, :128].astype(F32)[31:],
        ]
    )
    east = jnp.concatenate(
        [
            edges[5, :32, 128:].astype(F32)[:1],
            edges[3, 32:, :128].astype(F32),
            edges[7, :32, :128].astype(F32)[:1],
        ]
    )
    write_taps(cot_taps, cotangent, north, south, west, east, True)
    grad_motion = jnp.zeros(context_grad.shape, F32)
    for a in range(3):
        start = (2 - a) * 32
        grad_motion += jnp.dot(
            cot_taps[start : start + cells], back_weight[a], preferred_element_type=F32
        )
    for k in range(slots):
        pltpu.make_async_copy(
            tiles[0].at[pl.ds(0, cells)], parts.at[k, pl.ds(GROUP, cells)], sems.at[k]
        ).wait()
    for q in range(cells // GROUP):
        at = slice(q * GROUP, (q + 1) * GROUP)
        features = jnp.dot(flip, first[at], preferred_element_type=F32).astype(BF16)
        for k in range(slots):
            scores = lax.dot_general(
                features,
                parts[k, q * GROUP : q * GROUP + WINDOW],
                (((1,), (1,)), ((), ())),
                preferred_element_type=F32,
            )
            turn = WINDOW + REACH + LEAD - (GROUP - 1)
            band = pltpu.roll(scores, turn, 1, stride=1, stride_axis=0) * gains[k]
            packed = (
                band[:, :128]
                + pltpu.roll(band[:, 128:256], SPAN, 1)
                + pltpu.roll(band[:, 256:], 2 * SPAN, 1)
            )
            taps[at, k * 128 : (k + 1) * 128] = jnp.dot(
                flip, packed.astype(BF16), preferred_element_type=F32
            ).astype(BF16)
    pre = jnp.dot(taps[...], corr_weight[...], preferred_element_type=F32) + context[...].astype(
        F32
    )
    sigma = jax.nn.sigmoid(pre)
    motion[...] = (pre * sigma).astype(BF16)
    context_grad[...] = (grad_motion * sigma * (1.0 + pre * (1.0 - sigma))).astype(BF16)
    row_odd = info[16]
    facing[...] = motion[pl.ds(pl.multiple_of((1 - row_odd) * (cells - 32), 32), 32)]
    away[...] = motion[pl.ds(pl.multiple_of(row_odd * (cells - 32), 32), 32)]
    ends[...] = outer_columns(motion).reshape(ends.shape)
    over_cells = (((0,), (0,)), ((), ()))
    for a in range(3):
        start = (2 - a) * 32
        term = lax.dot_general(
            motion[...], cot_taps[start : start + cells], over_cells, preferred_element_type=F32
        )
        for b in range(3):
            weight_grads[(3 * a + b) * 256 : (3 * a + b + 1) * 256] = term[
                :, b * 128 : (b + 1) * 128
            ]
    term = lax.dot_general(taps[...], context_grad[...], over_cells, preferred_element_type=F32)
    base = 9 * 256
    for h in range(2):
        weight_grads[base + h * 384 + 320 : base + (h + 1) * 384] = jnp.zeros((64, 128), F32)
        for k in range(slots):
            for u in range(SPAN):
                row = k * 128 + (u % 4) * 32 + (u // 4) * SPAN + LEAD
                to = base + h * 384 + (k * SPAN + u) * SPAN
                weight_grads[to : to + SPAN] = term[row : row + SPAN, h * 128 : (h + 1) * 128]
    half = weight_grads.shape[0] // 2
    core = info[slots + 2]
    weights_kept[...] = weight_grads[pl.ds(pl.multiple_of(core * half, half), half)]
    weights_sent[...] = weight_grads[pl.ds(pl.multiple_of((1 - core) * half, half), half)].astype(
        BF16
    )


def backward_kernel(
    info, first, context_grad, corr_weight, parts, first_grad, kept, lent, totals
):
    cells = first.shape[0]
    slots = parts.shape[0]
    scale = 1.0 / math.sqrt(first.shape[1])
    inside = tap_mask(info[slots + 1], LEAD_BACK, False)
    totals[...] = jnp.zeros_like(totals)
    kept[...] = jnp.zeros_like(kept)
    lent[...] = jnp.zeros_like(lent)
    for q in range(cells // GROUP):
        at = slice(q * GROUP, (q + 1) * GROUP)
        packed = (
            lax.dot_general(
                context_grad[at],
                corr_weight[...],
                (((1,), (1,)), ((), ())),
                preferred_element_type=F32,
            )
            .astype(BF16)
            .astype(F32)
        )
        first_here = jnp.zeros((GROUP, first.shape[1]), F32)
        for k in range(slots):
            mine = packed[:, k * 128 : (k + 1) * 128]
            band = jnp.concatenate(
                [mine, pltpu.roll(mine, 128 - SPAN, 1), pltpu.roll(mine, 128 - 2 * SPAN, 1)],
                axis=1,
            )
            band = jnp.where(inside & (k < info[slots]), band, 0.0)
            scores = pltpu.roll(band, WINDOW - REACH - LEAD_BACK, 1, stride=1, stride_axis=0).astype(BF16)
            window = slice(q * GROUP, q * GROUP + WINDOW)
            first_here += jnp.dot(scores, parts[k, window], preferred_element_type=F32)
            totals[k, window] += lax.dot_general(
                scores, first[at], (((0,), (0,)), ((), ())), preferred_element_type=F32
            )
        first_grad[at] = first_here * scale
    for k in range(slots):
        value = (totals[k, GROUP : GROUP + cells] * scale).astype(BF16)
        place = info[k]
        same = place % 2 == 0

        @pl.when(same)
        def _():
            kept[place % 6 // 2 * 3 + place // 6] = value

        @pl.when(jnp.logical_not(same))
        def _():
            lent[(place % 6 > 1).astype(jnp.int32) * 3 + place // 6] = value


def features_kernel(motion, north, south, west, east, weight, out, taps):
    cells = out.shape[0]
    write_taps(taps, motion, north[...], south[...], west[...], east[...], False)
    total = jnp.zeros(out.shape, F32)
    for a in range(3):
        total += jnp.dot(taps[a * 32 : a * 32 + cells], weight[a], preferred_element_type=F32)
    out[...] = total.astype(BF16)


def finish_kernel(info, near, near_across, far, far_across, conv, corr, whole):
    size = near.shape[0] // 2
    core, low, high = info[6], info[7] & 1, info[7] >> 1
    half = whole.shape[0] // 2
    for ref, owner, at in (
        (near, core, low),
        (near_across, core, 1 - low),
        (far, 1 - core, low),
        (far_across, 1 - core, 1 - low),
    ):
        for s in range(2):
            to = owner * half + at * 2 * size + (high ^ s) * size
            whole[pl.ds(pl.multiple_of(to, size), size)] = ref[s * size : (s + 1) * size].astype(F32)
    conv[...] = whole[: conv.shape[0]]
    base = conv.shape[0]
    for h in range(2):
        corr[:, h * 128 : (h + 1) * 128] = whole[base + h * 384 : base + h * 384 + corr.shape[0]]


def call(kernel, out_shape, in_specs, scratch=(), flops=0):
    return pl.pallas_call(
        kernel,
        out_shape=out_shape,
        in_specs=in_specs,
        out_specs=jax.tree.map(lambda _: VMEM, out_shape),
        scratch_shapes=list(scratch),
        compiler_params=pltpu.CompilerParams(vmem_limit_bytes=VMEM_LIMIT),
        cost_estimate=pl.CostEstimate(flops=flops, bytes_accessed=flops // 300, transcendentals=0),
    )


def sum_weights(sent, kept, chip):
    cur = kept + swap(sent, "col", 1).astype(F32)
    for bit in (0, 1):
        size = cur.shape[0] // 2
        mine = (chip >> bit) & 1
        gone = lax.dynamic_slice_in_dim(cur, (1 - mine) * size, size).astype(BF16)
        cur = lax.dynamic_slice_in_dim(cur, mine * size, size)
        cur = cur + swap(gone, "col", 2 << bit).astype(F32)
    for bits in (1, 2, 4, 8):
        mine = cur.astype(BF16)
        cur = mine.astype(F32) + swap(mine, "row", bits).astype(F32)
    mine = cur.astype(BF16)
    near = jnp.concatenate([mine, swap(mine, "col", 4)])
    across = swap(near, "col", 2)
    return near, across, swap(near, "col", 1), swap(across, "col", 1)


def body(
    frame_one, frame_two, context, cotangent, corr_weight, conv_weight, partners, counts, radius
):
    rows_tile, cols_tile, channels = frame_one.shape
    slots = partners.shape[-1]
    cells = rows_tile * cols_tile
    hidden = context.shape[-1]
    out_width = conv_weight.shape[-1]
    row, col = lax.axis_index("row"), lax.axis_index("col")
    core, chip = col % 2, col // 2
    row_even, chip_even, col_even = row % 2 == 0, chip % 2 == 0, core == 0

    def role(step, even):
        step = jnp.asarray(step)
        return jnp.where(step == 0, 0, jnp.where((step > 0) == even, 1, 2))

    down, across = partners[0, 0] // 5 - 1, partners[0, 0] % 5 - 2
    chip_step = (core + across) >> 1
    place = role(down, row_even) * 6 + role(chip_step, chip_even) * 2 + (across & 1)
    north, south = role(-1, row_even) * 6, role(1, row_even) * 6
    west = jnp.where(col_even, role(-1, chip_even), 0) * 2 + 1
    east = jnp.where(col_even, 0, role(1, chip_even)) * 2 + 1
    beside = [north, south, west, east, north + west, north + east, south + west, south + east]
    info = jnp.concatenate(
        [place, counts[0], radius[0], jnp.stack([core, chip, *beside, row % 2])]
    ).astype(jnp.int32)
    first = frame_one.reshape(cells, channels)
    shape = jax.ShapeDtypeStruct
    cot = cotangent.reshape(cells, out_width)
    own = call(pack_kernel, shape((cells + 48, channels), BF16), [VMEM] * 2)(
        frame_two.reshape(cells, channels), cot
    )
    tiles = {(0, 0): own}
    for r in (1, 2):
        tiles[r, 0] = swap_pairs(own, "row", r - 1)
        tiles[0, r] = swap_pairs(own, "col", r - 1, 2)
    for r in (1, 2):
        tiles[r, r] = swap_pairs(tiles[r, 0], "col", r - 1, 2)
        tiles[r, 3 - r] = swap_pairs(tiles[0, 3 - r], "row", r - 1)
    around = []
    for r in range(3):
        for x in range(3):
            around += [tiles[r, x], swap(tiles[r, x], "col", 1)]
    spread = jnp.pad(
        corr_weight.reshape(slots, SPAN, SPAN, hidden), ((0, 0), (0, 3), (0, 0), (0, 0))
    )
    spread = spread.reshape(slots, 3, 4, SPAN, hidden).transpose(0, 2, 1, 3, 4)
    spread = spread.reshape(slots, 4, 3 * SPAN, hidden)
    spread, spread_back = (
        jnp.pad(spread, ((0, 0), (0, 0), (lead, 5 - lead), (0, 0))).reshape(slots * 128, hidden)
        for lead in (LEAD, LEAD_BACK)
    )
    back_weight = conv_weight.transpose(0, 1, 3, 2).reshape(3, 3 * out_width, hidden)
    total_rows = 9 * hidden + 2 * 384
    parts, motion, context_grad, facing, away, ends, weights_sent, weights_kept = call(
        forward_kernel,
        (
            shape((slots, cells + 2 * GROUP, channels), BF16),
            shape((cells, hidden), BF16),
            shape((cells, hidden), BF16),
            shape((cols_tile, hidden), BF16),
            shape((cols_tile, hidden), BF16),
            shape((2, rows_tile, hidden), BF16),
            shape((total_rows // 2, 128), BF16),
            shape((total_rows // 2, 128), F32),
        ),
        [SMEM] + [VMEM] * 5 + [ANY] * 18,
        [
            pltpu.VMEM((8, 48, channels), BF16),
            pltpu.VMEM(((rows_tile + 2) * cols_tile, 3 * out_width), BF16),
            pltpu.VMEM((cells, slots * 128), BF16),
            pltpu.VMEM((total_rows, 128), F32),
            pltpu.SemaphoreType.DMA((slots,)),
            pltpu.SemaphoreType.DMA((8,)),
        ],
        flops=3 * 10**9,
    )(info, first, context.reshape(cells, hidden), cot, back_weight, spread, *around)
    shards = sum_weights(weights_sent, weights_kept, chip)
    first_grad, kept, lent = call(
        backward_kernel,
        (
            shape((cells, channels), F32),
            shape((9, cells, channels), BF16),
            shape((6, cells, channels), BF16),
        ),
        [SMEM] + [VMEM] * 4,
        [pltpu.VMEM((slots, cells + 2 * GROUP, channels), F32)],
        flops=3 * 10**9,
    )(info, first, context_grad, spread_back, parts)
    lent = swap(lent, "col", 1).reshape(2, 3, cells, channels).astype(F32)
    kept = kept.reshape(3, 3, cells, channels).astype(F32)
    side = jnp.where((core == 0) == chip_even, 1, 2)
    middle = kept[0] + lent[0]
    for x in (1, 2):
        out = kept[x] + jnp.where(side == x, lent[1], 0.0)
        middle += swap_pairs(out.astype(BF16), "col", x - 1, 2).astype(F32)
    second_grad = middle[0]
    for r in (1, 2):
        second_grad += swap_pairs(middle[r].astype(BF16), "row", r - 1).astype(F32)
    features = call(
        features_kernel,
        shape((cells, out_width), BF16),
        [VMEM] * 6,
        [pltpu.VMEM(((rows_tile + 2) * cols_tile, 3 * hidden), BF16)],
        flops=10**9,
    )(
        motion,
        *rim(facing, away, ends, row_even, col_even),
        conv_weight.reshape(3, 3 * hidden, out_width),
    )
    conv_total, corr_total = call(
        finish_kernel,
        (shape((9 * hidden, out_width), F32), shape(corr_weight.shape, F32)),
        [SMEM] + [VMEM] * 4,
        [pltpu.VMEM((total_rows, 128), F32)],
    )(info, *shards)
    return (
        features.reshape(rows_tile, cols_tile, out_width),
        context_grad.reshape(rows_tile, cols_tile, hidden),
        first_grad.reshape(frame_one.shape),
        second_grad.reshape(frame_two.shape),
        corr_total,
        conv_total.reshape(conv_weight.shape),
    )


def solution(mesh):
    return jax.shard_map(
        body,
        mesh=mesh,
        in_specs=(
            P("row", "col", None),
            P("row", "col", None),
            P("row", "col", None),
            P("row", "col", None),
            P(),
            P(),
            P("row", "col", None),
            P("row", "col"),
            P("row", "col"),
        ),
        out_specs=(
            P("row", "col", None),
            P("row", "col", None),
            P("row", "col", None),
            P("row", "col", None),
            P(),
            P(),
        ),
        check_vma=False,
    )
```

```python
import functools
import math

import jax
import jax.numpy as jnp
from jax import lax
from jax.experimental import pallas as pl
from jax.experimental.pallas import tpu as pltpu
from jax.sharding import PartitionSpec as P

REACH = 4
SPAN = 2 * REACH + 1
GROUP = 128
WINDOW = 384
LEAD, LEAD_BACK = 3, 4
F32 = jnp.float32
BF16 = jnp.bfloat16
VMEM_LIMIT = 56 * 1024 * 1024
VMEM = pl.BlockSpec(memory_space=pltpu.VMEM)
SMEM = pl.BlockSpec(memory_space=pltpu.SMEM)
ANY = pl.BlockSpec(memory_space=pl.ANY)


def swap(array, axis, bits):
    return lax.ppermute(array, axis, [(i, i ^ bits) for i in range(lax.axis_size(axis))])


def swap_pairs(array, axis, odd, unit=1):
    count = lax.axis_size(axis) // unit
    pairs = []
    for i in range(odd, count - 1, 2):
        for low in range(unit):
            here, there = i * unit + low, (i + 1) * unit + low
            pairs += [(here, there), (there, here)]
    return lax.ppermute(array, axis, pairs)


def rim(facing, away, ends, row_even, col_even):
    even = swap_pairs(facing, "row", 0)
    odd = swap_pairs(away, "row", 1)
    north, south = jnp.where(row_even, odd, even), jnp.where(row_even, even, odd)
    left = jnp.concatenate([north[:1], ends[0], south[:1]])
    right = jnp.concatenate([north[-1:], ends[1], south[-1:]])
    even = swap_pairs(jnp.where(col_even, right, left), "col", 0)
    odd = swap_pairs(jnp.where(col_even, left, right), "col", 1)
    west, east = jnp.where(col_even, odd, even), jnp.where(col_even, even, odd)
    return north, south, west, east


def outer_columns(cells):
    count = cells.shape[0]
    line = lax.broadcasted_iota(jnp.int32, (32, count), 0)
    cell = lax.broadcasted_iota(jnp.int32, (32, count), 1)
    wanted = (line & 15) * 32 + (line >> 4) * 31
    pick = (cell == wanted).astype(F32).astype(BF16)
    return jnp.dot(pick, cells[...], preferred_element_type=F32).astype(BF16)


def write_taps(taps, own, north, south, west, east, backwards):
    width = own.shape[1]
    line = north.shape[0]
    taps[:line, width : 2 * width] = north
    taps[line:-line, width : 2 * width] = own[...]
    taps[-line:, width : 2 * width] = south
    middle = taps[:, width : 2 * width].astype(F32)
    place = lax.broadcasted_iota(jnp.int32, middle.shape, 0) % line

    def stretched(ends):
        shape = (ends.shape[0], line, width)
        return jnp.broadcast_to(ends.astype(F32)[:, None], shape).reshape(middle.shape)

    left = jnp.where(place == 0, stretched(west), pltpu.roll(middle, 1, 0)).astype(BF16)
    right = jnp.where(
        place == line - 1, stretched(east), pltpu.roll(middle, middle.shape[0] - 1, 0)
    ).astype(BF16)
    taps[:, :width] = right if backwards else left
    taps[:, 2 * width :] = left if backwards else right


def tap_mask(radius, lead, backwards):
    cell = lax.broadcasted_iota(jnp.int32, (GROUP, WINDOW), 0)
    cell = GROUP - 1 - cell if backwards else cell
    tap = lax.broadcasted_iota(jnp.int32, (GROUP, WINDOW), 1)
    down = (tap >> 5) - REACH
    across = (tap & 31) - lead - REACH
    column = (cell & 31) + across
    return (
        (jnp.abs(down) <= radius)
        & (jnp.abs(across) <= radius)
        & (column >= 0)
        & (column < 32)
    )


def flip_matrix():
    return (
        (
            lax.broadcasted_iota(jnp.int32, (GROUP, GROUP), 0)
            + lax.broadcasted_iota(jnp.int32, (GROUP, GROUP), 1)
            == GROUP - 1
        )
        .astype(F32)
        .astype(BF16)
    )


def pack_kernel(tile, cotangent, out):
    cells = tile.shape[0]
    out[:cells] = tile[...]
    out[cells : cells + 32, :128] = cotangent[:32]
    out[cells : cells + 32, 128:] = cotangent[cells - 32 :]
    ends = outer_columns(cotangent)
    out[cells + 32 :, :128] = ends[:16]
    out[cells + 32 :, 128:] = ends[16:]


def role(step, even):
    step = jnp.asarray(step)
    return jnp.where(step == 0, 0, jnp.where((step > 0) == even, 1, 2))


def position():
    col = lax.axis_index("col")
    return lax.axis_index("row"), col >> 1, col & 1


def tile_of(offset):
    row, chip, core = position()
    down, across = offset // 5 - 1, offset % 5 - 2
    return (
        role(down, row % 2 == 0) * 6 + role((core + across) >> 1, chip % 2 == 0) * 2 + (across & 1)
    )


def tiles_beside():
    row, chip, core = position()
    row_even, chip_even = row % 2 == 0, chip % 2 == 0
    north, south = role(-1, row_even) * 6, role(1, row_even) * 6
    west = jnp.where(core == 0, role(-1, chip_even), 0) * 2 + 1
    east = jnp.where(core == 0, 0, role(1, chip_even)) * 2 + 1
    return [north, south, west, east, north + west, north + east, south + west, south + east]


def spread_kernel(weight, out, out_back, wide):
    for lead, ref in ((LEAD, out), (LEAD_BACK, out_back)):
        wide[...] = jnp.zeros_like(wide)
        for k in range(4):
            for u in range(SPAN):
                row = k * 128 + (u % 4) * 32 + (u // 4) * SPAN + lead
                at = (k * SPAN + u) * SPAN
                wide[row : row + SPAN] = weight[at : at + SPAN]
        ref[...] = wide[...].astype(BF16)


def forward_kernel(partners, counts, radius, first, context, cotangent, conv_weight, corr_weight, *refs):
    tiles, refs = refs[:18], refs[18:]
    parts, motion, context_grad, facing, away, ends, weights_sent, weights_kept = refs[:8]
    edges, cot_taps, taps, weight_grads, sems, edge_sems = refs[8:]
    cells = first.shape[0]
    slots = parts.shape[0]
    row_sides, chip_sides = (6, 12), (1, 3, 5)
    options = [row_sides] * 2 + [chip_sides] * 2 + [[r + x for r in row_sides for x in chip_sides]] * 4
    for n, tile in enumerate(tiles_beside()):
        for t in options[n]:
            @pl.when(tile == t)
            def _():
                pltpu.make_async_copy(
                    tiles[t].at[pl.ds(cells, 48)], edges.at[n], edge_sems.at[n]
                ).start()
    for k in range(slots):
        tile = tile_of(partners[0, 0, k])
        for t in range(18):
            @pl.when(tile == t)
            def _():
                pltpu.make_async_copy(
                    tiles[t].at[pl.ds(0, cells)], parts.at[k, pl.ds(GROUP, cells)], sems.at[k]
                ).start()
        parts[k, :GROUP] = jnp.zeros((GROUP, parts.shape[2]), BF16)
        parts[k, GROUP + cells :] = jnp.zeros((GROUP, parts.shape[2]), BF16)
    inside = tap_mask(radius[0, 0], LEAD, True)
    flip = flip_matrix()
    gains = []
    for k in range(slots):
        live = jnp.where(k < counts[0, 0], 1.0 / math.sqrt(first.shape[1]), 0.0).astype(F32)
        gains.append(jnp.where(inside, live, 0.0))
    for n in range(8):
        pltpu.make_async_copy(tiles[0].at[pl.ds(cells, 48)], edges.at[n], edge_sems.at[n]).wait()
    north, south = edges[0, :32, 128:], edges[1, :32, :128]
    west = jnp.concatenate(
        [
            edges[4, :32, 128:].astype(F32)[31:],
            edges[2, 32:, 128:].astype(F32),
            edges[6, :32, :128].astype(F32)[31:],
        ]
    )
    east = jnp.concatenate(
        [
            edges[5, :32, 128:].astype(F32)[:1],
            edges[3, 32:, :128].astype(F32),
            edges[7, :32, :128].astype(F32)[:1],
        ]
    )
    write_taps(cot_taps, cotangent, north, south, west, east, True)
    grad_motion = jnp.zeros(context_grad.shape, F32)
    for a in range(3):
        start = (2 - a) * 32
        for b in range(3):
            grad_motion += lax.dot_general(
                cot_taps[start : start + cells, b * 128 : (b + 1) * 128],
                conv_weight[a, b],
                (((1,), (1,)), ((), ())),
                preferred_element_type=F32,
            )
    for k in range(slots):
        pltpu.make_async_copy(
            tiles[0].at[pl.ds(0, cells)], parts.at[k, pl.ds(GROUP, cells)], sems.at[k]
        ).wait()
    for q in range(cells // GROUP):
        at = slice(q * GROUP, (q + 1) * GROUP)
        features = jnp.dot(flip, first[at], preferred_element_type=F32).astype(BF16)
        for k in range(slots):
            scores = lax.dot_general(
                features,
                parts[k, q * GROUP : q * GROUP + WINDOW],
                (((1,), (1,)), ((), ())),
                preferred_element_type=F32,
            )
            turn = WINDOW + REACH + LEAD - (GROUP - 1)
            band = pltpu.roll(scores, turn, 1, stride=1, stride_axis=0) * gains[k]
            packed = (
                band[:, :128]
                + pltpu.roll(band[:, 128:256], SPAN, 1)
                + pltpu.roll(band[:, 256:], 2 * SPAN, 1)
            )
            taps[at, k * 128 : (k + 1) * 128] = jnp.dot(
                flip, packed.astype(BF16), preferred_element_type=F32
            ).astype(BF16)
    pre = jnp.dot(taps[...], corr_weight[...], preferred_element_type=F32) + context[...].astype(
        F32
    )
    sigma = jax.nn.sigmoid(pre)
    motion[...] = (pre * sigma).astype(BF16)
    context_grad[...] = (grad_motion * sigma * (1.0 + pre * (1.0 - sigma))).astype(BF16)
    row, _, core = position()
    row_odd = row % 2
    facing[...] = motion[pl.ds(pl.multiple_of((1 - row_odd) * (cells - 32), 32), 32)]
    away[...] = motion[pl.ds(pl.multiple_of(row_odd * (cells - 32), 32), 32)]
    ends[...] = outer_columns(motion).reshape(ends.shape)
    over_cells = (((0,), (0,)), ((), ()))
    for a in range(3):
        start = (2 - a) * 32
        term = lax.dot_general(
            motion[...], cot_taps[start : start + cells], over_cells, preferred_element_type=F32
        )
        for b in range(3):
            weight_grads[(3 * a + b) * 256 : (3 * a + b + 1) * 256] = term[
                :, b * 128 : (b + 1) * 128
            ]
    term = lax.dot_general(taps[...], context_grad[...], over_cells, preferred_element_type=F32)
    base = 9 * 256
    for h in range(2):
        weight_grads[base + h * 384 + 320 : base + (h + 1) * 384] = jnp.zeros((64, 128), F32)
        for k in range(slots):
            for u in range(SPAN):
                row = k * 128 + (u % 4) * 32 + (u // 4) * SPAN + LEAD
                to = base + h * 384 + (k * SPAN + u) * SPAN
                weight_grads[to : to + SPAN] = term[row : row + SPAN, h * 128 : (h + 1) * 128]
    half = weight_grads.shape[0] // 2
    weights_kept[...] = weight_grads[pl.ds(pl.multiple_of(core * half, half), half)]
    weights_sent[...] = weight_grads[pl.ds(pl.multiple_of((1 - core) * half, half), half)].astype(
        BF16
    )


def backward_kernel(
    partners, counts, radius, first, context_grad, corr_weight, parts, first_grad, *refs
):
    cells = first.shape[0]
    slots = parts.shape[0]
    scale = 1.0 / math.sqrt(first.shape[1])
    inside = tap_mask(radius[0, 0], LEAD_BACK, False)
    *kept, lent, totals = refs
    for ref in refs:
        ref[...] = jnp.zeros_like(ref)
    for q in range(cells // GROUP):
        at = slice(q * GROUP, (q + 1) * GROUP)
        packed = (
            lax.dot_general(
                context_grad[at],
                corr_weight[...],
                (((1,), (1,)), ((), ())),
                preferred_element_type=F32,
            )
            .astype(BF16)
            .astype(F32)
        )
        first_here = jnp.zeros((GROUP, first.shape[1]), F32)
        for k in range(slots):
            mine = packed[:, k * 128 : (k + 1) * 128]
            band = jnp.concatenate(
                [mine, pltpu.roll(mine, 128 - SPAN, 1), pltpu.roll(mine, 128 - 2 * SPAN, 1)],
                axis=1,
            )
            band = jnp.where(inside & (k < counts[0, 0]), band, 0.0)
            scores = pltpu.roll(band, WINDOW - REACH - LEAD_BACK, 1, stride=1, stride_axis=0).astype(BF16)
            window = slice(q * GROUP, q * GROUP + WINDOW)
            first_here += jnp.dot(scores, parts[k, window], preferred_element_type=F32)
            totals[k, window] += lax.dot_general(
                scores, first[at], (((0,), (0,)), ((), ())), preferred_element_type=F32
            )
        first_grad[at] = first_here * scale
    for k in range(slots):
        value = (totals[k, GROUP : GROUP + cells] * scale).astype(BF16)
        place = tile_of(partners[0, 0, k])
        for x in range(3):
            @pl.when(place % 6 == 2 * x)
            def _():
                kept[x][place // 6] = value

        @pl.when(place % 2 == 1)
        def _():
            lent[(place % 6 > 1).astype(jnp.int32) * 3 + place // 6] = value


def features_kernel(motion, north, south, west, east, weight, out, taps):
    cells = out.shape[0]
    write_taps(taps, motion, north[...], south[...], west[...], east[...], False)
    total = jnp.zeros(out.shape, F32)
    for a in range(3):
        total += jnp.dot(taps[a * 32 : a * 32 + cells], weight[a], preferred_element_type=F32)
    out[...] = total.astype(BF16)


def finish_kernel(*refs):
    shards, (conv, corr, whole) = refs[:8], refs[8:]
    size = shards[0].shape[0]
    _, chip, core = position()
    half = whole.shape[0] // 2
    for n, ref in enumerate(shards):
        owner = core if n < 4 else 1 - core
        to = owner * half + (chip ^ (n % 4)) * size
        whole[pl.ds(pl.multiple_of(to, size), size)] = ref[...].astype(F32)
    conv[...] = whole[: conv.shape[0]]
    base = conv.shape[0]
    for h in range(2):
        corr[:, h * 128 : (h + 1) * 128] = whole[base + h * 384 : base + h * 384 + corr.shape[0]]


def call(kernel, out_shape, in_specs, scratch=(), flops=0):
    return pl.pallas_call(
        kernel,
        out_shape=out_shape,
        in_specs=in_specs,
        out_specs=jax.tree.map(lambda _: VMEM, out_shape),
        scratch_shapes=list(scratch),
        compiler_params=pltpu.CompilerParams(vmem_limit_bytes=VMEM_LIMIT),
        cost_estimate=pl.CostEstimate(flops=flops, bytes_accessed=flops // 300, transcendentals=0),
    )


def halve(cur, mine, axis, bits):
    size = cur.shape[0] // 2
    gone = lax.dynamic_slice_in_dim(cur, (1 - mine) * size, size).astype(BF16)
    return lax.dynamic_slice_in_dim(cur, mine * size, size), swap(gone, axis, bits)


def sum_everywhere(cur, axis, unit):
    mine = cur.astype(BF16)
    got = [swap(mine, axis, unit * s).astype(F32) for s in (1, 2, 3)]
    return (mine.astype(F32) + got[0]) + (got[1] + got[2])


def body(
    frame_one, frame_two, context, cotangent, corr_weight, conv_weight, partners, counts, radius
):
    rows_tile, cols_tile, channels = frame_one.shape
    slots = partners.shape[-1]
    cells = rows_tile * cols_tile
    hidden = context.shape[-1]
    out_width = conv_weight.shape[-1]
    row, col = lax.axis_index("row"), lax.axis_index("col")
    core, chip = col % 2, col // 2
    row_even, chip_even, col_even = row % 2 == 0, chip % 2 == 0, core == 0
    tables = (partners, counts, radius)
    first = frame_one.reshape(cells, channels)
    shape = jax.ShapeDtypeStruct
    cot = cotangent.reshape(cells, out_width)
    own = call(pack_kernel, shape((cells + 48, channels), BF16), [VMEM] * 2)(
        frame_two.reshape(cells, channels), cot
    )
    tiles = {(0, 0): own}
    for r in (1, 2):
        tiles[r, 0] = swap_pairs(own, "row", r - 1)
        tiles[0, r] = swap_pairs(own, "col", r - 1, 2)
    for r in (1, 2):
        tiles[r, r] = swap_pairs(tiles[r, 0], "col", r - 1, 2)
        tiles[r, 3 - r] = swap_pairs(tiles[0, 3 - r], "row", r - 1)
    around = []
    for r in range(3):
        for x in range(3):
            around += [tiles[r, x], swap(tiles[r, x], "col", 1)]
    spread, spread_back = call(
        spread_kernel,
        (shape((slots * 128, hidden), BF16), shape((slots * 128, hidden), BF16)),
        [VMEM],
        [pltpu.VMEM((slots * 128, hidden), F32)],
    )(corr_weight.astype(F32))
    total_rows = 9 * hidden + 2 * 384
    parts, motion, context_grad, facing, away, ends, weights_sent, weights_kept = call(
        forward_kernel,
        (
            shape((slots, cells + 2 * GROUP, channels), BF16),
            shape((cells, hidden), BF16),
            shape((cells, hidden), BF16),
            shape((cols_tile, hidden), BF16),
            shape((cols_tile, hidden), BF16),
            shape((2, rows_tile, hidden), BF16),
            shape((total_rows // 2, 128), BF16),
            shape((total_rows // 2, 128), F32),
        ),
        [SMEM] * 3 + [VMEM] * 5 + [ANY] * 18,
        [
            pltpu.VMEM((8, 48, channels), BF16),
            pltpu.VMEM(((rows_tile + 2) * cols_tile, 3 * out_width), BF16),
            pltpu.VMEM((cells, slots * 128), BF16),
            pltpu.VMEM((total_rows, 128), F32),
            pltpu.SemaphoreType.DMA((slots,)),
            pltpu.SemaphoreType.DMA((8,)),
        ],
        flops=3 * 10**9,
    )(
        *tables,
        first,
        context.reshape(cells, hidden),
        cot,
        conv_weight,
        spread,
        *around,
    )
    total = weights_kept + swap(weights_sent, "col", 1).astype(F32)
    total, got = halve(total, chip >> 1, "col", 4)
    first_grad, *kept, lent = call(
        backward_kernel,
        (
            shape((cells, channels), F32),
            *[shape((3, cells, channels), BF16)] * 3,
            shape((6, cells, channels), BF16),
        ),
        [SMEM] * 3 + [VMEM] * 4,
        [pltpu.VMEM((slots, cells + 2 * GROUP, channels), F32)],
        flops=3 * 10**9,
    )(*tables, first, context_grad, spread_back, parts)
    lent = swap(lent, "col", 1)
    side = jnp.where((core == 0) == chip_even, 1, 2)
    sent = [
        (kept[x].astype(F32) + jnp.where(side == x, lent[3:].astype(F32), 0.0)).astype(BF16)
        for x in (1, 2)
    ]
    total, got = halve(total + got.astype(F32), chip & 1, "col", 2)
    total, sent[0], sent[1] = lax.optimization_barrier((total + got.astype(F32), *sent))
    middle = kept[0].astype(F32) + lent[:3].astype(F32)
    for x in (1, 2):
        middle += swap_pairs(sent[x - 1], "col", x - 1, 2).astype(F32)
    total = sum_everywhere(sum_everywhere(total, "row", 1), "row", 4).astype(BF16)
    shards = [total] + [swap(total, "col", 2 * s) for s in (1, 2, 3)]
    shards += [swap(shard, "col", 1) for shard in shards]
    second_grad = middle[0]
    for r in (1, 2):
        second_grad += swap_pairs(middle[r].astype(BF16), "row", r - 1).astype(F32)
    features = call(
        features_kernel,
        shape((cells, out_width), BF16),
        [VMEM] * 6,
        [pltpu.VMEM(((rows_tile + 2) * cols_tile, 3 * hidden), BF16)],
        flops=10**9,
    )(
        motion,
        *rim(facing, away, ends, row_even, col_even),
        conv_weight.reshape(3, 3 * hidden, out_width),
    )
    conv_total, corr_total = call(
        finish_kernel,
        (shape((9 * hidden, out_width), F32), shape(corr_weight.shape, F32)),
        [VMEM] * 8,
        [pltpu.VMEM((total_rows, 128), F32)],
    )(*shards)
    return (
        features.reshape(rows_tile, cols_tile, out_width),
        context_grad.reshape(rows_tile, cols_tile, hidden),
        first_grad.reshape(frame_one.shape),
        second_grad.reshape(frame_two.shape),
        corr_total,
        conv_total.reshape(conv_weight.shape),
    )


def solution(mesh):
    return jax.shard_map(
        body,
        mesh=mesh,
        in_specs=(
            P("row", "col", None),
            P("row", "col", None),
            P("row", "col", None),
            P("row", "col", None),
            P(),
            P(),
            P("row", "col", None),
            P("row", "col"),
            P("row", "col"),
        ),
        out_specs=(
            P("row", "col", None),
            P("row", "col", None),
            P("row", "col", None),
            P("row", "col", None),
            P(),
            P(),
        ),
        check_vma=False,
    )
```

```python
import functools
import math

import jax
import jax.numpy as jnp
from jax import lax
from jax.experimental import pallas as pl
from jax.experimental.pallas import tpu as pltpu
from jax.sharding import PartitionSpec as P

REACH = 4
SPAN = 2 * REACH + 1
GROUP = 128
WINDOW = 384
LEAD, LEAD_BACK = 3, 4
F32 = jnp.float32
BF16 = jnp.bfloat16
VMEM_LIMIT = 56 * 1024 * 1024
VMEM = pl.BlockSpec(memory_space=pltpu.VMEM)
SMEM = pl.BlockSpec(memory_space=pltpu.SMEM)
ANY = pl.BlockSpec(memory_space=pl.ANY)


def swap(array, axis, bits):
    return lax.ppermute(array, axis, [(i, i ^ bits) for i in range(lax.axis_size(axis))])


def swap_pairs(array, axis, odd, unit=1):
    count = lax.axis_size(axis) // unit
    pairs = []
    for i in range(odd, count - 1, 2):
        for low in range(unit):
            here, there = i * unit + low, (i + 1) * unit + low
            pairs += [(here, there), (there, here)]
    return lax.ppermute(array, axis, pairs)


def rim(facing, away, ends, row_even, col_even):
    even = swap_pairs(facing, "row", 0)
    odd = swap_pairs(away, "row", 1)
    north, south = jnp.where(row_even, odd, even), jnp.where(row_even, even, odd)
    left = jnp.concatenate([north[:1], ends[0], south[:1]])
    right = jnp.concatenate([north[-1:], ends[1], south[-1:]])
    even = swap_pairs(jnp.where(col_even, right, left), "col", 0)
    odd = swap_pairs(jnp.where(col_even, left, right), "col", 1)
    west, east = jnp.where(col_even, odd, even), jnp.where(col_even, even, odd)
    return north, south, west, east


def outer_columns(cells):
    count = cells.shape[0]
    line = lax.broadcasted_iota(jnp.int32, (32, count), 0)
    cell = lax.broadcasted_iota(jnp.int32, (32, count), 1)
    wanted = (line & 15) * 32 + (line >> 4) * 31
    pick = (cell == wanted).astype(F32).astype(BF16)
    return jnp.dot(pick, cells[...], preferred_element_type=F32).astype(BF16)


def write_taps(taps, own, north, south, west, east, backwards):
    width = own.shape[1]
    line = north.shape[0]
    taps[:line, width : 2 * width] = north
    taps[line:-line, width : 2 * width] = own[...]
    taps[-line:, width : 2 * width] = south
    middle = taps[:, width : 2 * width].astype(F32)
    place = lax.broadcasted_iota(jnp.int32, middle.shape, 0) % line

    def stretched(ends):
        shape = (ends.shape[0], line, width)
        return jnp.broadcast_to(ends.astype(F32)[:, None], shape).reshape(middle.shape)

    left = jnp.where(place == 0, stretched(west), pltpu.roll(middle, 1, 0)).astype(BF16)
    right = jnp.where(
        place == line - 1, stretched(east), pltpu.roll(middle, middle.shape[0] - 1, 0)
    ).astype(BF16)
    taps[:, :width] = right if backwards else left
    taps[:, 2 * width :] = left if backwards else right


def tap_mask(radius, lead, backwards):
    cell = lax.broadcasted_iota(jnp.int32, (GROUP, WINDOW), 0)
    cell = GROUP - 1 - cell if backwards else cell
    tap = lax.broadcasted_iota(jnp.int32, (GROUP, WINDOW), 1)
    down = (tap >> 5) - REACH
    across = (tap & 31) - lead - REACH
    column = (cell & 31) + across
    return (
        (jnp.abs(down) <= radius)
        & (jnp.abs(across) <= radius)
        & (column >= 0)
        & (column < 32)
    )


def flip_matrix():
    return (
        (
            lax.broadcasted_iota(jnp.int32, (GROUP, GROUP), 0)
            + lax.broadcasted_iota(jnp.int32, (GROUP, GROUP), 1)
            == GROUP - 1
        )
        .astype(F32)
        .astype(BF16)
    )


def pack_kernel(tile, cotangent, out):
    cells = tile.shape[0]
    out[:cells] = tile[...]
    out[cells : cells + 32, :128] = cotangent[:32]
    out[cells : cells + 32, 128:] = cotangent[cells - 32 :]
    ends = outer_columns(cotangent)
    out[cells + 32 :, :128] = ends[:16]
    out[cells + 32 :, 128:] = ends[16:]


def role(step, even):
    step = jnp.asarray(step)
    return jnp.where(step == 0, 0, jnp.where((step > 0) == even, 1, 2))


def position():
    col = lax.axis_index("col")
    return lax.axis_index("row"), col >> 1, col & 1


def tile_of(offset):
    row, chip, core = position()
    down, across = offset // 5 - 1, offset % 5 - 2
    return (
        role(down, row % 2 == 0) * 6 + role((core + across) >> 1, chip % 2 == 0) * 2 + (across & 1)
    )


def tiles_beside():
    row, chip, core = position()
    row_even, chip_even = row % 2 == 0, chip % 2 == 0
    north, south = role(-1, row_even) * 6, role(1, row_even) * 6
    west = jnp.where(core == 0, role(-1, chip_even), 0) * 2 + 1
    east = jnp.where(core == 0, 0, role(1, chip_even)) * 2 + 1
    return [north, south, west, east, north + west, north + east, south + west, south + east]


def spread_rows(weight, narrow, wide, lead):
    narrow[...] = weight[...].astype(F32)
    wide[...] = jnp.zeros_like(wide)
    for k in range(wide.shape[0] // 128):
        for u in range(SPAN):
            row = k * 128 + (u % 4) * 32 + (u // 4) * SPAN + lead
            at = (k * SPAN + u) * SPAN
            wide[row : row + SPAN] = narrow[at : at + SPAN]


def forward_kernel(partners, counts, radius, first, context, cotangent, conv_weight, corr_weight, *refs):
    tiles, refs = refs[:18], refs[18:]
    motion, context_grad, facing, away, ends, weights_sent, weights_kept, parts = refs[:8]
    edges, cot_taps, taps_back, taps, flipped, narrow, wide, spread, weight_grads = refs[8:17]
    sems, edge_sems = refs[17:]
    cells = first.shape[0]
    slots = parts.shape[0]
    row_sides, chip_sides = (6, 12), (1, 3, 5)
    options = [row_sides] * 2 + [chip_sides] * 2 + [[r + x for r in row_sides for x in chip_sides]] * 4
    for n, tile in enumerate(tiles_beside()):
        for t in options[n]:
            @pl.when(tile == t)
            def _():
                pltpu.make_async_copy(
                    tiles[t].at[pl.ds(cells, 48)], edges.at[n], edge_sems.at[n]
                ).start()
    for k in range(slots):
        tile = tile_of(partners[0, 0, k])
        for t in range(18):
            @pl.when(tile == t)
            def _():
                pltpu.make_async_copy(
                    tiles[t].at[pl.ds(0, cells)], parts.at[k, pl.ds(GROUP, cells)], sems.at[k]
                ).start()
        parts[k, :GROUP] = jnp.zeros((GROUP, parts.shape[2]), BF16)
        parts[k, GROUP + cells :] = jnp.zeros((GROUP, parts.shape[2]), BF16)
    inside = tap_mask(radius[0, 0], LEAD, True)
    flip = flip_matrix()
    gains = []
    for k in range(slots):
        live = jnp.where(k < counts[0, 0], 1.0 / math.sqrt(first.shape[1]), 0.0).astype(F32)
        gains.append(jnp.where(inside, live, 0.0))
    for q in range(cells // GROUP):
        at = slice(q * GROUP, (q + 1) * GROUP)
        flipped[at] = jnp.dot(flip, first[at], preferred_element_type=F32).astype(BF16)
    spread_rows(corr_weight, narrow, wide, LEAD)
    spread[...] = wide[...].astype(BF16)
    for n in range(8):
        pltpu.make_async_copy(tiles[0].at[pl.ds(cells, 48)], edges.at[n], edge_sems.at[n]).wait()
    north, south = edges[0, :32, 128:], edges[1, :32, :128]
    west = jnp.concatenate(
        [
            edges[4, :32, 128:].astype(F32)[31:],
            edges[2, 32:, 128:].astype(F32),
            edges[6, :32, :128].astype(F32)[31:],
        ]
    )
    east = jnp.concatenate(
        [
            edges[5, :32, 128:].astype(F32)[:1],
            edges[3, 32:, :128].astype(F32),
            edges[7, :32, :128].astype(F32)[:1],
        ]
    )
    write_taps(cot_taps, cotangent, north, south, west, east, True)
    grad_motion = jnp.zeros(context_grad.shape, F32)
    for a in range(3):
        start = (2 - a) * 32
        for b in range(3):
            grad_motion += lax.dot_general(
                cot_taps[start : start + cells, b * 128 : (b + 1) * 128],
                conv_weight[a, b],
                (((1,), (1,)), ((), ())),
                preferred_element_type=F32,
            )
    for k in range(slots):
        pltpu.make_async_copy(
            tiles[0].at[pl.ds(0, cells)], parts.at[k, pl.ds(GROUP, cells)], sems.at[k]
        ).wait()
    for q in range(cells // GROUP):
        at = slice(q * GROUP, (q + 1) * GROUP)
        features = flipped[at]
        for k in range(slots):
            scores = lax.dot_general(
                features,
                parts[k, q * GROUP : q * GROUP + WINDOW],
                (((1,), (1,)), ((), ())),
                preferred_element_type=F32,
            )
            turn = WINDOW + REACH + LEAD - (GROUP - 1)
            band = pltpu.roll(scores, turn, 1, stride=1, stride_axis=0) * gains[k]
            packed = (
                band[:, :128]
                + pltpu.roll(band[:, 128:256], SPAN, 1)
                + pltpu.roll(band[:, 256:], 2 * SPAN, 1)
            )
            taps_back[at, k * 128 : (k + 1) * 128] = packed.astype(BF16)
    for q in range(cells // GROUP):
        at = slice(q * GROUP, (q + 1) * GROUP)
        taps[at] = jnp.dot(flip, taps_back[at], preferred_element_type=F32).astype(BF16)
    pre = jnp.dot(taps[...], spread[...], preferred_element_type=F32) + context[...].astype(
        F32
    )
    sigma = jax.nn.sigmoid(pre)
    motion[...] = (pre * sigma).astype(BF16)
    context_grad[...] = (grad_motion * sigma * (1.0 + pre * (1.0 - sigma))).astype(BF16)
    row, _, core = position()
    row_odd = row % 2
    facing[...] = motion[pl.ds(pl.multiple_of((1 - row_odd) * (cells - 32), 32), 32)]
    away[...] = motion[pl.ds(pl.multiple_of(row_odd * (cells - 32), 32), 32)]
    ends[...] = outer_columns(motion).reshape(ends.shape)
    over_cells = (((0,), (0,)), ((), ()))
    for a in range(3):
        start = (2 - a) * 32
        term = lax.dot_general(
            motion[...], cot_taps[start : start + cells], over_cells, preferred_element_type=F32
        )
        for b in range(3):
            weight_grads[(3 * a + b) * 256 : (3 * a + b + 1) * 256] = term[
                :, b * 128 : (b + 1) * 128
            ]
    term = lax.dot_general(taps[...], context_grad[...], over_cells, preferred_element_type=F32)
    base = 9 * 256
    for h in range(2):
        weight_grads[base + h * 384 + 320 : base + (h + 1) * 384] = jnp.zeros((64, 128), F32)
        for k in range(slots):
            for u in range(SPAN):
                row = k * 128 + (u % 4) * 32 + (u // 4) * SPAN + LEAD
                to = base + h * 384 + (k * SPAN + u) * SPAN
                weight_grads[to : to + SPAN] = term[row : row + SPAN, h * 128 : (h + 1) * 128]
    half = weight_grads.shape[0] // 2
    weights_kept[...] = weight_grads[pl.ds(pl.multiple_of(core * half, half), half)]
    weights_sent[...] = weight_grads[pl.ds(pl.multiple_of((1 - core) * half, half), half)].astype(
        BF16
    )


def backward_kernel(
    partners, counts, radius, first, context_grad, corr_weight, parts, *refs
):
    cells = first.shape[0]
    slots = parts.shape[0]
    scale = 1.0 / math.sqrt(first.shape[1])
    inside = tap_mask(radius[0, 0], LEAD_BACK, False)
    first_grad, *kept, lent, totals, narrow, wide, spread = refs[-9:]
    for ref in (*kept, lent, totals):
        ref[...] = jnp.zeros_like(ref)
    spread_rows(corr_weight, narrow, wide, LEAD_BACK)
    spread[...] = wide[...].astype(BF16)
    across = first[...].T
    for q in range(cells // GROUP):
        at = slice(q * GROUP, (q + 1) * GROUP)
        packed = (
            lax.dot_general(
                context_grad[at],
                spread[...],
                (((1,), (1,)), ((), ())),
                preferred_element_type=F32,
            )
            .astype(BF16)
            .astype(F32)
        )
        first_here = jnp.zeros((GROUP, first.shape[1]), F32)
        for k in range(slots):
            mine = packed[:, k * 128 : (k + 1) * 128]
            band = jnp.concatenate(
                [mine, pltpu.roll(mine, 128 - SPAN, 1), pltpu.roll(mine, 128 - 2 * SPAN, 1)],
                axis=1,
            )
            band = jnp.where(inside & (k < counts[0, 0]), band, 0.0)
            scores = pltpu.roll(band, WINDOW - REACH - LEAD_BACK, 1, stride=1, stride_axis=0).astype(BF16)
            window = slice(q * GROUP, q * GROUP + WINDOW)
            first_here += jnp.dot(scores, parts[k, window], preferred_element_type=F32)
            totals[k, :, window] += jnp.dot(
                across[:, at], scores, preferred_element_type=F32
            )
        first_grad[at] = first_here * scale
    for k in range(slots):
        value = (totals[k, :, GROUP : GROUP + cells] * scale).astype(BF16).T
        place = tile_of(partners[0, 0, k])
        for x in range(3):
            @pl.when(place % 6 == 2 * x)
            def _():
                kept[x][place // 6] = value

        @pl.when(place % 2 == 1)
        def _():
            lent[(place % 6 > 1).astype(jnp.int32) * 3 + place // 6] = value


def features_kernel(motion, north, south, west, east, weight, out, taps):
    cells = out.shape[0]
    write_taps(taps, motion, north[...], south[...], west[...], east[...], False)
    total = jnp.zeros(out.shape, F32)
    for a in range(3):
        total += jnp.dot(taps[a * 32 : a * 32 + cells], weight[a], preferred_element_type=F32)
    out[...] = total.astype(BF16)


def finish_kernel(*refs):
    shards, (conv, corr, whole) = refs[:8], refs[8:]
    size = shards[0].shape[0]
    _, chip, core = position()
    half = whole.shape[0] // 2
    for n, ref in enumerate(shards):
        owner = core if n < 4 else 1 - core
        to = owner * half + (chip ^ (n % 4)) * size
        whole[pl.ds(pl.multiple_of(to, size), size)] = ref[...].astype(F32)
    conv[...] = whole[: conv.shape[0]]
    base = conv.shape[0]
    for h in range(2):
        corr[:, h * 128 : (h + 1) * 128] = whole[base + h * 384 : base + h * 384 + corr.shape[0]]


def call(kernel, out_shape, in_specs, scratch=(), flops=0):
    return pl.pallas_call(
        kernel,
        out_shape=out_shape,
        in_specs=in_specs,
        out_specs=jax.tree.map(lambda _: VMEM, out_shape),
        scratch_shapes=list(scratch),
        compiler_params=pltpu.CompilerParams(vmem_limit_bytes=VMEM_LIMIT),
        cost_estimate=pl.CostEstimate(flops=flops, bytes_accessed=flops // 300, transcendentals=0),
    )


def halve(cur, mine, axis, bits):
    size = cur.shape[0] // 2
    gone = lax.dynamic_slice_in_dim(cur, (1 - mine) * size, size).astype(BF16)
    return lax.dynamic_slice_in_dim(cur, mine * size, size), gone, swap(gone, axis, bits)


def sum_everywhere(cur, axis, unit):
    mine = cur.astype(BF16)
    got = [swap(mine, axis, unit * s).astype(F32) for s in (1, 2, 3)]
    return (mine.astype(F32) + got[0]) + (got[1] + got[2])


def forward(tables, first, context, cotangent, conv_weight, corr_weight, around):
    cells, channels = first.shape
    hidden = context.shape[1]
    slots = tables[0].shape[-1]
    shape = jax.ShapeDtypeStruct
    total_rows = 9 * hidden + 2 * 384
    return call(
        forward_kernel,
        (
            shape((cells, hidden), BF16),
            shape((cells, hidden), BF16),
            shape((32, hidden), BF16),
            shape((32, hidden), BF16),
            shape((2, 16, hidden), BF16),
            shape((total_rows // 2, 128), BF16),
            shape((total_rows // 2, 128), F32),
            shape((slots, cells + 2 * GROUP, channels), BF16),
        ),
        [SMEM] * 3 + [VMEM] * 5 + [ANY] * 18,
        [
            pltpu.VMEM((8, 48, channels), BF16),
            pltpu.VMEM((cells + 64, 384), BF16),
            pltpu.VMEM((cells, slots * 128), BF16),
            pltpu.VMEM((cells, slots * 128), BF16),
            pltpu.VMEM((cells, channels), BF16),
            pltpu.VMEM(corr_weight.shape, F32),
            pltpu.VMEM((slots * 128, hidden), F32),
            pltpu.VMEM((slots * 128, hidden), BF16),
            pltpu.VMEM((total_rows, 128), F32),
            pltpu.SemaphoreType.DMA((slots,)),
            pltpu.SemaphoreType.DMA((8,)),
        ],
        flops=3 * 10**9,
    )(*tables, first, context, cotangent, conv_weight, corr_weight, *around)


def backward(tables, first, context_grad, corr_weight, parts, after=()):
    cells, channels = first.shape
    slots, hidden = parts.shape[0], context_grad.shape[1]
    shape = jax.ShapeDtypeStruct
    return call(
        backward_kernel,
        (
            shape((cells, channels), F32),
            *[shape((3, cells, channels), BF16)] * 3,
            shape((6, cells, channels), BF16),
        ),
        [SMEM] * 3 + [VMEM] * 4 + [ANY] * len(after),
        [
            pltpu.VMEM((slots, channels, cells + 2 * GROUP), F32),
            pltpu.VMEM(corr_weight.shape, F32),
            pltpu.VMEM((slots * 128, hidden), F32),
            pltpu.VMEM((slots * 128, hidden), BF16),
        ],
        flops=3 * 10**9,
    )(*tables, first, context_grad, corr_weight, parts, *after)


def body(
    frame_one, frame_two, context, cotangent, corr_weight, conv_weight, partners, counts, radius
):
    rows_tile, cols_tile, channels = frame_one.shape
    slots = partners.shape[-1]
    cells = rows_tile * cols_tile
    hidden = context.shape[-1]
    out_width = conv_weight.shape[-1]
    row, col = lax.axis_index("row"), lax.axis_index("col")
    core, chip = col % 2, col // 2
    row_even, chip_even, col_even = row % 2 == 0, chip % 2 == 0, core == 0
    tables = (partners, counts, radius)
    first = frame_one.reshape(cells, channels)
    shape = jax.ShapeDtypeStruct
    cot = cotangent.reshape(cells, out_width)
    own = call(pack_kernel, shape((cells + 48, channels), BF16), [VMEM] * 2)(
        frame_two.reshape(cells, channels), cot
    )
    tiles = {(0, 0): own}
    for r in (1, 2):
        tiles[r, 0] = swap_pairs(own, "row", r - 1)
        tiles[0, r] = swap_pairs(own, "col", r - 1, 2)
    for r in (1, 2):
        tiles[r, r] = swap_pairs(tiles[r, 0], "col", r - 1, 2)
        tiles[r, 3 - r] = swap_pairs(tiles[0, 3 - r], "row", r - 1)
    around = []
    for r in range(3):
        for x in range(3):
            around += [tiles[r, x], swap(tiles[r, x], "col", 1)]
    motion, context_grad, facing, away, ends, weights_sent, weights_kept, parts = forward(
        tables, first, context.reshape(cells, hidden), cot, conv_weight, corr_weight, around
    )
    total = weights_kept + swap(weights_sent, "col", 1).astype(F32)
    total, gone, got = halve(total, chip >> 1, "col", 4)
    around_motion = rim(facing, away, ends, row_even, col_even)
    first_grad, *kept, lent = backward(
        tables, first, context_grad, corr_weight, parts, (gone, *around_motion)
    )
    lent = swap(lent, "col", 1)
    side = jnp.where((core == 0) == chip_even, 1, 2)
    sent = [
        (kept[x].astype(F32) + jnp.where(side == x, lent[3:].astype(F32), 0.0)).astype(BF16)
        for x in (1, 2)
    ]
    total, _, got = halve(total + got.astype(F32), chip & 1, "col", 2)
    features = call(
        features_kernel,
        shape((cells, out_width), BF16),
        [VMEM] * 6,
        [pltpu.VMEM(((rows_tile + 2) * cols_tile, 3 * hidden), BF16)],
        flops=10**9,
    )(motion, *around_motion, conv_weight.reshape(3, 3 * hidden, out_width))
    total, features, *sent = lax.optimization_barrier((total + got.astype(F32), features, *sent))
    middle = kept[0].astype(F32) + lent[:3].astype(F32)
    for x in (1, 2):
        middle += swap_pairs(sent[x - 1], "col", x - 1, 2).astype(F32)
    total = sum_everywhere(sum_everywhere(total, "row", 1), "row", 4).astype(BF16)
    shards = [total] + [swap(total, "col", 2 * s) for s in (1, 2, 3)]
    shards += [swap(shard, "col", 1) for shard in shards]
    second_grad = middle[0]
    for r in (1, 2):
        second_grad += swap_pairs(middle[r].astype(BF16), "row", r - 1).astype(F32)
    conv_total, corr_total = call(
        finish_kernel,
        (shape((9 * hidden, out_width), F32), shape(corr_weight.shape, F32)),
        [VMEM] * 8,
        [pltpu.VMEM((9 * hidden + 2 * 384, 128), F32)],
    )(*shards)
    return (
        features.reshape(rows_tile, cols_tile, out_width),
        context_grad.reshape(rows_tile, cols_tile, hidden),
        first_grad.reshape(frame_one.shape),
        second_grad.reshape(frame_two.shape),
        corr_total,
        conv_total.reshape(conv_weight.shape),
    )


def solution(mesh):
    return jax.shard_map(
        body,
        mesh=mesh,
        in_specs=(
            P("row", "col", None),
            P("row", "col", None),
            P("row", "col", None),
            P("row", "col", None),
            P(),
            P(),
            P("row", "col", None),
            P("row", "col"),
            P("row", "col"),
        ),
        out_specs=(
            P("row", "col", None),
            P("row", "col", None),
            P("row", "col", None),
            P("row", "col", None),
            P(),
            P(),
        ),
        check_vma=False,
    )
```

```python
import functools
import math

import jax
import jax.numpy as jnp
from jax import lax
from jax.experimental import pallas as pl
from jax.experimental.pallas import tpu as pltpu
from jax.sharding import PartitionSpec as P

REACH = 4
SPAN = 2 * REACH + 1
GROUP = 128
WINDOW = 384
LEAD, LEAD_BACK = 3, 4
F32 = jnp.float32
BF16 = jnp.bfloat16
VMEM_LIMIT = 56 * 1024 * 1024
VMEM = pl.BlockSpec(memory_space=pltpu.VMEM)
SMEM = pl.BlockSpec(memory_space=pltpu.SMEM)
ANY = pl.BlockSpec(memory_space=pl.ANY)


def swap(array, axis, bits):
    return lax.ppermute(array, axis, [(i, i ^ bits) for i in range(lax.axis_size(axis))])


def swap_pairs(array, axis, odd, unit=1):
    count = lax.axis_size(axis) // unit
    pairs = []
    for i in range(odd, count - 1, 2):
        for low in range(unit):
            here, there = i * unit + low, (i + 1) * unit + low
            pairs += [(here, there), (there, here)]
    return lax.ppermute(array, axis, pairs)


def rim(facing, away, ends, row_even, col_even):
    even = swap_pairs(facing, "row", 0)
    odd = swap_pairs(away, "row", 1)
    north, south = jnp.where(row_even, odd, even), jnp.where(row_even, even, odd)
    left = jnp.concatenate([north[:1], ends[0], south[:1]])
    right = jnp.concatenate([north[-1:], ends[1], south[-1:]])
    even = swap_pairs(jnp.where(col_even, right, left), "col", 0)
    odd = swap_pairs(jnp.where(col_even, left, right), "col", 1)
    west, east = jnp.where(col_even, odd, even), jnp.where(col_even, even, odd)
    return north, south, west, east


def outer_columns(cells):
    count = cells.shape[0]
    line = lax.broadcasted_iota(jnp.int32, (32, count), 0)
    cell = lax.broadcasted_iota(jnp.int32, (32, count), 1)
    wanted = (line & 15) * 32 + (line >> 4) * 31
    pick = (cell == wanted).astype(F32).astype(BF16)
    return jnp.dot(pick, cells[...], preferred_element_type=F32).astype(BF16)


def write_taps(taps, own, north, south, west, east, backwards):
    width = own.shape[1]
    line = north.shape[0]
    taps[:line, width : 2 * width] = north
    taps[line:-line, width : 2 * width] = own[...]
    taps[-line:, width : 2 * width] = south
    middle = taps[:, width : 2 * width].astype(F32)
    place = lax.broadcasted_iota(jnp.int32, middle.shape, 0) % line

    def stretched(ends):
        shape = (ends.shape[0], line, width)
        return jnp.broadcast_to(ends.astype(F32)[:, None], shape).reshape(middle.shape)

    left = jnp.where(place == 0, stretched(west), pltpu.roll(middle, 1, 0)).astype(BF16)
    right = jnp.where(
        place == line - 1, stretched(east), pltpu.roll(middle, middle.shape[0] - 1, 0)
    ).astype(BF16)
    taps[:, :width] = right if backwards else left
    taps[:, 2 * width :] = left if backwards else right


def tap_mask(radius, lead, backwards):
    cell = lax.broadcasted_iota(jnp.int32, (GROUP, WINDOW), 0)
    cell = GROUP - 1 - cell if backwards else cell
    tap = lax.broadcasted_iota(jnp.int32, (GROUP, WINDOW), 1)
    down = (tap >> 5) - REACH
    across = (tap & 31) - lead - REACH
    column = (cell & 31) + across
    return (
        (jnp.abs(down) <= radius)
        & (jnp.abs(across) <= radius)
        & (column >= 0)
        & (column < 32)
    )


def flip_matrix():
    return (
        (
            lax.broadcasted_iota(jnp.int32, (GROUP, GROUP), 0)
            + lax.broadcasted_iota(jnp.int32, (GROUP, GROUP), 1)
            == GROUP - 1
        )
        .astype(F32)
        .astype(BF16)
    )


def pack_kernel(tile, cotangent, out):
    cells = tile.shape[0]
    out[:cells] = tile[...]
    out[cells : cells + 32, :128] = cotangent[:32]
    out[cells : cells + 32, 128:] = cotangent[cells - 32 :]
    ends = outer_columns(cotangent)
    out[cells + 32 :, :128] = ends[:16]
    out[cells + 32 :, 128:] = ends[16:]


def role(step, even):
    step = jnp.asarray(step)
    return jnp.where(step == 0, 0, jnp.where((step > 0) == even, 1, 2))


def position():
    col = lax.axis_index("col")
    return lax.axis_index("row"), col >> 1, col & 1


def tile_of(offset):
    row, chip, core = position()
    down, across = offset // 5 - 1, offset % 5 - 2
    return (
        role(down, row % 2 == 0) * 6 + role((core + across) >> 1, chip % 2 == 0) * 2 + (across & 1)
    )


def tiles_beside():
    row, chip, core = position()
    row_even, chip_even = row % 2 == 0, chip % 2 == 0
    north, south = role(-1, row_even) * 6, role(1, row_even) * 6
    west = jnp.where(core == 0, role(-1, chip_even), 0) * 2 + 1
    east = jnp.where(core == 0, 0, role(1, chip_even)) * 2 + 1
    return [north, south, west, east, north + west, north + east, south + west, south + east]


def spread_rows(weight, narrow, wide, lead):
    narrow[...] = weight[...].astype(F32)
    wide[...] = jnp.zeros_like(wide)
    for k in range(wide.shape[0] // 128):
        for u in range(SPAN):
            row = k * 128 + (u % 4) * 32 + (u // 4) * SPAN + lead
            at = (k * SPAN + u) * SPAN
            wide[row : row + SPAN] = narrow[at : at + SPAN]


def forward_kernel(partners, counts, radius, first, context, cotangent, conv_weight, corr_weight, *refs):
    tiles, refs = refs[:18], refs[18:]
    motion, context_grad, facing, away, ends, weights_sent, weights_kept, parts = refs[:8]
    edges, cot_taps, taps_back, taps, flipped, narrow, wide, spread, weight_grads = refs[8:17]
    sems, edge_sems = refs[17:]
    cells = first.shape[0]
    slots = parts.shape[0]
    row_sides, chip_sides = (6, 12), (1, 3, 5)
    options = [row_sides] * 2 + [chip_sides] * 2 + [[r + x for r in row_sides for x in chip_sides]] * 4
    for n, tile in enumerate(tiles_beside()):
        for t in options[n]:
            @pl.when(tile == t)
            def _():
                pltpu.make_async_copy(
                    tiles[t].at[pl.ds(cells, 48)], edges.at[n], edge_sems.at[n]
                ).start()
    for k in range(slots):
        tile = tile_of(partners[0, 0, k])
        for t in range(18):
            @pl.when(tile == t)
            def _():
                pltpu.make_async_copy(
                    tiles[t].at[pl.ds(0, cells)], parts.at[k, pl.ds(GROUP, cells)], sems.at[k]
                ).start()
        parts[k, :GROUP] = jnp.zeros((GROUP, parts.shape[2]), BF16)
        parts[k, GROUP + cells :] = jnp.zeros((GROUP, parts.shape[2]), BF16)
    inside = tap_mask(radius[0, 0], LEAD, True)
    flip = flip_matrix()
    gains = []
    for k in range(slots):
        live = jnp.where(k < counts[0, 0], 1.0 / math.sqrt(first.shape[1]), 0.0).astype(F32)
        gains.append(jnp.where(inside, live, 0.0))
    for q in range(cells // GROUP):
        at = slice(q * GROUP, (q + 1) * GROUP)
        flipped[at] = jnp.dot(flip, first[at], preferred_element_type=F32).astype(BF16)
    spread_rows(corr_weight, narrow, wide, LEAD)
    spread[...] = wide[...].astype(BF16)
    for n in range(8):
        pltpu.make_async_copy(tiles[0].at[pl.ds(cells, 48)], edges.at[n], edge_sems.at[n]).wait()
    north, south = edges[0, :32, 128:], edges[1, :32, :128]
    west = jnp.concatenate(
        [
            edges[4, :32, 128:].astype(F32)[31:],
            edges[2, 32:, 128:].astype(F32),
            edges[6, :32, :128].astype(F32)[31:],
        ]
    )
    east = jnp.concatenate(
        [
            edges[5, :32, 128:].astype(F32)[:1],
            edges[3, 32:, :128].astype(F32),
            edges[7, :32, :128].astype(F32)[:1],
        ]
    )
    write_taps(cot_taps, cotangent, north, south, west, east, True)
    grad_motion = jnp.zeros(context_grad.shape, F32)
    for a in range(3):
        start = (2 - a) * 32
        for b in range(3):
            grad_motion += lax.dot_general(
                cot_taps[start : start + cells, b * 128 : (b + 1) * 128],
                conv_weight[a, b],
                (((1,), (1,)), ((), ())),
                preferred_element_type=F32,
            )
    for k in range(slots):
        pltpu.make_async_copy(
            tiles[0].at[pl.ds(0, cells)], parts.at[k, pl.ds(GROUP, cells)], sems.at[k]
        ).wait()
    for q in range(cells // GROUP):
        at = slice(q * GROUP, (q + 1) * GROUP)
        features = flipped[at]
        for k in range(slots):
            scores = lax.dot_general(
                features,
                parts[k, q * GROUP : q * GROUP + WINDOW],
                (((1,), (1,)), ((), ())),
                preferred_element_type=F32,
            )
            turn = WINDOW + REACH + LEAD - (GROUP - 1)
            band = pltpu.roll(scores, turn, 1, stride=1, stride_axis=0) * gains[k]
            packed = (
                band[:, :128]
                + pltpu.roll(band[:, 128:256], SPAN, 1)
                + pltpu.roll(band[:, 256:], 2 * SPAN, 1)
            )
            taps_back[at, k * 128 : (k + 1) * 128] = packed.astype(BF16)
    for q in range(cells // GROUP):
        at = slice(q * GROUP, (q + 1) * GROUP)
        taps[at] = jnp.dot(flip, taps_back[at], preferred_element_type=F32).astype(BF16)
    pre = jnp.dot(taps[...], spread[...], preferred_element_type=F32) + context[...].astype(
        F32
    )
    sigma = jax.nn.sigmoid(pre)
    motion[...] = (pre * sigma).astype(BF16)
    context_grad[...] = (grad_motion * sigma * (1.0 + pre * (1.0 - sigma))).astype(BF16)
    row, _, core = position()
    row_odd = row % 2
    facing[...] = motion[pl.ds(pl.multiple_of((1 - row_odd) * (cells - 32), 32), 32)]
    away[...] = motion[pl.ds(pl.multiple_of(row_odd * (cells - 32), 32), 32)]
    ends[...] = outer_columns(motion).reshape(ends.shape)
    over_cells = (((0,), (0,)), ((), ()))
    for a in range(3):
        start = (2 - a) * 32
        term = lax.dot_general(
            motion[...], cot_taps[start : start + cells], over_cells, preferred_element_type=F32
        )
        for b in range(3):
            weight_grads[(3 * a + b) * 256 : (3 * a + b + 1) * 256] = term[
                :, b * 128 : (b + 1) * 128
            ]
    term = lax.dot_general(taps[...], context_grad[...], over_cells, preferred_element_type=F32)
    base = 9 * 256
    for h in range(2):
        weight_grads[base + h * 384 + 320 : base + (h + 1) * 384] = jnp.zeros((64, 128), F32)
        for k in range(slots):
            for u in range(SPAN):
                row = k * 128 + (u % 4) * 32 + (u // 4) * SPAN + LEAD
                to = base + h * 384 + (k * SPAN + u) * SPAN
                weight_grads[to : to + SPAN] = term[row : row + SPAN, h * 128 : (h + 1) * 128]
    half = weight_grads.shape[0] // 2
    weights_kept[...] = weight_grads[pl.ds(pl.multiple_of(core * half, half), half)]
    weights_sent[...] = weight_grads[pl.ds(pl.multiple_of((1 - core) * half, half), half)].astype(
        BF16
    )


def scores_kernel(
    counts, radius, context_grad, corr_weight, parts, first_grad, scores, narrow, wide, spread
):
    cells = context_grad.shape[0]
    slots = parts.shape[0]
    inside = tap_mask(radius[0, 0], LEAD_BACK, False)
    spread_rows(corr_weight, narrow, wide, LEAD_BACK)
    spread[...] = wide[...].astype(BF16)
    for q in range(cells // GROUP):
        at = slice(q * GROUP, (q + 1) * GROUP)
        packed = (
            lax.dot_general(
                context_grad[at],
                spread[...],
                (((1,), (1,)), ((), ())),
                preferred_element_type=F32,
            )
            .astype(BF16)
            .astype(F32)
        )
        first_here = jnp.zeros((GROUP, parts.shape[2]), F32)
        for k in range(slots):
            mine = packed[:, k * 128 : (k + 1) * 128]
            band = jnp.concatenate(
                [mine, pltpu.roll(mine, 128 - SPAN, 1), pltpu.roll(mine, 128 - 2 * SPAN, 1)],
                axis=1,
            )
            band = jnp.where(inside & (k < counts[0, 0]), band, 0.0)
            turn = WINDOW - REACH - LEAD_BACK
            here = pltpu.roll(band, turn, 1, stride=1, stride_axis=0).astype(BF16)
            scores[k, at] = here
            window = slice(q * GROUP, q * GROUP + WINDOW)
            first_here += jnp.dot(here, parts[k, window], preferred_element_type=F32)
        first_grad[at] = first_here * (1.0 / math.sqrt(parts.shape[2]))


def partners_kernel(partners, first, scores, *refs):
    *kept, lent, totals = refs[-5:]
    cells, channels = first.shape
    scale = 1.0 / math.sqrt(channels)
    for ref in (*kept, lent, totals):
        ref[...] = jnp.zeros_like(ref)
    across = first[...].T
    for k in range(scores.shape[0]):
        for q in range(cells // GROUP):
            at = slice(q * GROUP, (q + 1) * GROUP)
            totals[k, :, q * GROUP : q * GROUP + WINDOW] += jnp.dot(
                across[:, at], scores[k, at], preferred_element_type=F32
            )
        value = (totals[k, :, GROUP : GROUP + cells] * scale).astype(BF16).T
        place = tile_of(partners[0, 0, k])
        for x in range(3):
            @pl.when(place % 6 == 2 * x)
            def _():
                kept[x][place // 6] = value

        @pl.when(place % 2 == 1)
        def _():
            lent[(place % 6 > 1).astype(jnp.int32) * 3 + place // 6] = value


def features_kernel(motion, north, south, west, east, weight, out, taps):
    cells = out.shape[0]
    write_taps(taps, motion, north[...], south[...], west[...], east[...], False)
    total = jnp.zeros(out.shape, F32)
    for a in range(3):
        total += jnp.dot(taps[a * 32 : a * 32 + cells], weight[a], preferred_element_type=F32)
    out[...] = total.astype(BF16)


def finish_kernel(*refs):
    shards, (conv, corr, whole) = refs[:8], refs[8:]
    size = shards[0].shape[0]
    _, chip, core = position()
    half = whole.shape[0] // 2
    for n, ref in enumerate(shards):
        owner = core if n < 4 else 1 - core
        to = owner * half + (chip ^ (n % 4)) * size
        whole[pl.ds(pl.multiple_of(to, size), size)] = ref[...].astype(F32)
    conv[...] = whole[: conv.shape[0]]
    base = conv.shape[0]
    for h in range(2):
        corr[:, h * 128 : (h + 1) * 128] = whole[base + h * 384 : base + h * 384 + corr.shape[0]]


def call(kernel, out_shape, in_specs, scratch=(), flops=1000):
    return pl.pallas_call(
        kernel,
        out_shape=out_shape,
        in_specs=in_specs,
        out_specs=jax.tree.map(lambda _: VMEM, out_shape),
        scratch_shapes=list(scratch),
        compiler_params=pltpu.CompilerParams(vmem_limit_bytes=VMEM_LIMIT),
        cost_estimate=pl.CostEstimate(flops=flops, bytes_accessed=flops // 300, transcendentals=0),
    )


def sum_everywhere(cur, axis, unit):
    mine = cur.astype(BF16)
    got = [swap(mine, axis, unit * s).astype(F32) for s in (1, 2, 3)]
    return (mine.astype(F32) + got[0]) + (got[1] + got[2])


def forward(tables, first, context, cotangent, conv_weight, corr_weight, around):
    cells, channels = first.shape
    hidden = context.shape[1]
    slots = tables[0].shape[-1]
    shape = jax.ShapeDtypeStruct
    total_rows = 9 * hidden + 2 * 384
    return call(
        forward_kernel,
        (
            shape((cells, hidden), BF16),
            shape((cells, hidden), BF16),
            shape((32, hidden), BF16),
            shape((32, hidden), BF16),
            shape((2, 16, hidden), BF16),
            shape((total_rows // 2, 128), BF16),
            shape((total_rows // 2, 128), F32),
            shape((slots, cells + 2 * GROUP, channels), BF16),
        ),
        [SMEM] * 3 + [VMEM] * 5 + [ANY] * 18,
        [
            pltpu.VMEM((8, 48, channels), BF16),
            pltpu.VMEM((cells + 64, 384), BF16),
            pltpu.VMEM((cells, slots * 128), BF16),
            pltpu.VMEM((cells, slots * 128), BF16),
            pltpu.VMEM((cells, channels), BF16),
            pltpu.VMEM(corr_weight.shape, F32),
            pltpu.VMEM((slots * 128, hidden), F32),
            pltpu.VMEM((slots * 128, hidden), BF16),
            pltpu.VMEM((total_rows, 128), F32),
            pltpu.SemaphoreType.DMA((slots,)),
            pltpu.SemaphoreType.DMA((8,)),
        ],
        flops=3 * 10**9,
    )(*tables, first, context, cotangent, conv_weight, corr_weight, *around)


def backward_scores(tables, context_grad, corr_weight, parts):
    cells, hidden = context_grad.shape
    slots, _, channels = parts.shape
    shape = jax.ShapeDtypeStruct
    return call(
        scores_kernel,
        (shape((cells, channels), F32), shape((slots, cells, WINDOW), BF16)),
        [SMEM] * 2 + [VMEM] * 3,
        [
            pltpu.VMEM(corr_weight.shape, F32),
            pltpu.VMEM((slots * 128, hidden), F32),
            pltpu.VMEM((slots * 128, hidden), BF16),
        ],
        flops=4 * 10**9,
    )(*tables[1:], context_grad, corr_weight, parts)


def backward_partners(tables, first, scores, after=()):
    cells, channels = first.shape
    shape = jax.ShapeDtypeStruct
    return call(
        partners_kernel,
        (*[shape((3, cells, channels), BF16)] * 3, shape((6, cells, channels), BF16)),
        [SMEM] + [VMEM] * 2 + [ANY] * len(after),
        [pltpu.VMEM((scores.shape[0], channels, cells + 2 * GROUP), F32)],
        flops=4 * 10**9,
    )(tables[0], first, scores, *after)


def body(
    frame_one, frame_two, context, cotangent, corr_weight, conv_weight, partners, counts, radius
):
    rows_tile, cols_tile, channels = frame_one.shape
    slots = partners.shape[-1]
    cells = rows_tile * cols_tile
    hidden = context.shape[-1]
    out_width = conv_weight.shape[-1]
    row, col = lax.axis_index("row"), lax.axis_index("col")
    core, chip = col % 2, col // 2
    row_even, chip_even, col_even = row % 2 == 0, chip % 2 == 0, core == 0
    tables = (partners, counts, radius)
    first = frame_one.reshape(cells, channels)
    shape = jax.ShapeDtypeStruct
    cot = cotangent.reshape(cells, out_width)
    own = call(pack_kernel, shape((cells + 48, channels), BF16), [VMEM] * 2)(
        frame_two.reshape(cells, channels), cot
    )
    tiles = {(0, 0): own}
    for r in (1, 2):
        tiles[r, 0] = swap_pairs(own, "row", r - 1)
        tiles[0, r] = swap_pairs(own, "col", r - 1, 2)
    for r in (1, 2):
        tiles[r, r] = swap_pairs(tiles[r, 0], "col", r - 1, 2)
        tiles[r, 3 - r] = swap_pairs(tiles[0, 3 - r], "row", r - 1)
    around = []
    for r in range(3):
        for x in range(3):
            around += [tiles[r, x], swap(tiles[r, x], "col", 1)]
    motion, context_grad, facing, away, ends, weights_sent, weights_kept, parts = forward(
        tables, first, context.reshape(cells, hidden), cot, conv_weight, corr_weight, around
    )
    total = weights_kept + swap(weights_sent, "col", 1).astype(F32)
    size = total.shape[0] // 4
    pieces = [lax.dynamic_slice_in_dim(total, (chip ^ s) * size, size) for s in range(4)]
    gone = [piece.astype(BF16) for piece in pieces[1:]]
    got = [swap(piece, "col", 2 * s) for s, piece in zip((1, 2, 3), gone)]
    around_motion = rim(facing, away, ends, row_even, col_even)
    first_grad, scores = backward_scores(tables, context_grad, corr_weight, parts)
    *kept, lent = backward_partners(
        tables, first, scores, (*got, *around_motion[:2])
    )
    lent = swap(lent, "col", 1)
    side = jnp.where((core == 0) == chip_even, 1, 2)
    sent = [
        (kept[x].astype(F32) + jnp.where(side == x, lent[3:].astype(F32), 0.0)).astype(BF16)
        for x in (1, 2)
    ]
    total = (pieces[0] + got[0].astype(F32)) + (got[1].astype(F32) + got[2].astype(F32))
    total, *ready = lax.optimization_barrier((total, *sent, *around_motion))
    sent, around_motion = ready[:2], ready[2:]
    middle = kept[0].astype(F32) + lent[:3].astype(F32)
    for x in (1, 2):
        middle += swap_pairs(sent[x - 1], "col", x - 1, 2).astype(F32)
    total = sum_everywhere(sum_everywhere(total, "row", 1), "row", 4).astype(BF16)
    shards = [total] + [swap(total, "col", 2 * s) for s in (1, 2, 3)]
    features = call(
        features_kernel,
        shape((cells, out_width), BF16),
        [VMEM] * 6,
        [pltpu.VMEM(((rows_tile + 2) * cols_tile, 3 * hidden), BF16)],
    )(motion, *around_motion, conv_weight.reshape(3, 3 * hidden, out_width))
    features, *shards = lax.optimization_barrier((features, *shards))
    shards += [swap(shard, "col", 1) for shard in shards]
    second_grad = middle[0]
    for r in (1, 2):
        second_grad += swap_pairs(middle[r].astype(BF16), "row", r - 1).astype(F32)
    conv_total, corr_total = call(
        finish_kernel,
        (shape((9 * hidden, out_width), F32), shape(corr_weight.shape, F32)),
        [VMEM] * 8,
        [pltpu.VMEM((9 * hidden + 2 * 384, 128), F32)],
    )(*shards)
    return (
        features.reshape(rows_tile, cols_tile, out_width),
        context_grad.reshape(rows_tile, cols_tile, hidden),
        first_grad.reshape(frame_one.shape),
        second_grad.reshape(frame_two.shape),
        corr_total,
        conv_total.reshape(conv_weight.shape),
    )


def solution(mesh):
    return jax.shard_map(
        body,
        mesh=mesh,
        in_specs=(
            P("row", "col", None),
            P("row", "col", None),
            P("row", "col", None),
            P("row", "col", None),
            P(),
            P(),
            P("row", "col", None),
            P("row", "col"),
            P("row", "col"),
        ),
        out_specs=(
            P("row", "col", None),
            P("row", "col", None),
            P("row", "col", None),
            P("row", "col", None),
            P(),
            P(),
        ),
        check_vma=False,
    )
```

```python
import functools
import math

import jax
import jax.numpy as jnp
from jax import lax
from jax.experimental import pallas as pl
from jax.experimental.pallas import tpu as pltpu
from jax.sharding import PartitionSpec as P

REACH = 4
SPAN = 2 * REACH + 1
GROUP = 128
WINDOW = 384
LEAD, LEAD_BACK = 3, 4
F32 = jnp.float32
BF16 = jnp.bfloat16
VMEM_LIMIT = 56 * 1024 * 1024
VMEM = pl.BlockSpec(memory_space=pltpu.VMEM)
SMEM = pl.BlockSpec(memory_space=pltpu.SMEM)
ANY = pl.BlockSpec(memory_space=pl.ANY)


def swap(array, axis, bits):
    return lax.ppermute(array, axis, [(i, i ^ bits) for i in range(lax.axis_size(axis))])


def swap_pairs(array, axis, odd, unit=1):
    count = lax.axis_size(axis) // unit
    pairs = []
    for i in range(odd, count - 1, 2):
        for low in range(unit):
            here, there = i * unit + low, (i + 1) * unit + low
            pairs += [(here, there), (there, here)]
    return lax.ppermute(array, axis, pairs)


def rim_rows(facing, away, row_even):
    even = swap_pairs(facing, "row", 0)
    odd = swap_pairs(away, "row", 1)
    return jnp.where(row_even, odd, even), jnp.where(row_even, even, odd)


def rim_columns(north, south, ends, col_even):
    left = jnp.concatenate([north[:1], ends[0], south[:1]])
    right = jnp.concatenate([north[-1:], ends[1], south[-1:]])
    even = swap_pairs(jnp.where(col_even, right, left), "col", 0)
    odd = swap_pairs(jnp.where(col_even, left, right), "col", 1)
    return jnp.where(col_even, odd, even), jnp.where(col_even, even, odd)


def outer_columns(cells):
    count = cells.shape[0]
    line = lax.broadcasted_iota(jnp.int32, (32, count), 0)
    cell = lax.broadcasted_iota(jnp.int32, (32, count), 1)
    wanted = (line & 15) * 32 + (line >> 4) * 31
    pick = (cell == wanted).astype(F32).astype(BF16)
    return jnp.dot(pick, cells[...], preferred_element_type=F32).astype(BF16)


def write_taps(taps, own, north, south, west, east, backwards):
    width = own.shape[1]
    line = north.shape[0]
    taps[:line, width : 2 * width] = north
    taps[line:-line, width : 2 * width] = own[...]
    taps[-line:, width : 2 * width] = south
    middle = taps[:, width : 2 * width].astype(F32)
    place = lax.broadcasted_iota(jnp.int32, middle.shape, 0) % line

    def stretched(ends):
        shape = (ends.shape[0], line, width)
        return jnp.broadcast_to(ends.astype(F32)[:, None], shape).reshape(middle.shape)

    left = jnp.where(place == 0, stretched(west), pltpu.roll(middle, 1, 0)).astype(BF16)
    right = jnp.where(
        place == line - 1, stretched(east), pltpu.roll(middle, middle.shape[0] - 1, 0)
    ).astype(BF16)
    taps[:, :width] = right if backwards else left
    taps[:, 2 * width :] = left if backwards else right


def tap_mask(radius, lead, backwards):
    cell = lax.broadcasted_iota(jnp.int32, (GROUP, WINDOW), 0)
    cell = GROUP - 1 - cell if backwards else cell
    tap = lax.broadcasted_iota(jnp.int32, (GROUP, WINDOW), 1)
    down = (tap >> 5) - REACH
    across = (tap & 31) - lead - REACH
    column = (cell & 31) + across
    return (
        (jnp.abs(down) <= radius)
        & (jnp.abs(across) <= radius)
        & (column >= 0)
        & (column < 32)
    )


def flip_matrix():
    return (
        (
            lax.broadcasted_iota(jnp.int32, (GROUP, GROUP), 0)
            + lax.broadcasted_iota(jnp.int32, (GROUP, GROUP), 1)
            == GROUP - 1
        )
        .astype(F32)
        .astype(BF16)
    )


def pack_kernel(tile, cotangent, out):
    cells = tile.shape[0]
    out[:cells] = tile[...]
    out[cells : cells + 32, :128] = cotangent[:32]
    out[cells : cells + 32, 128:] = cotangent[cells - 32 :]
    ends = outer_columns(cotangent)
    out[cells + 32 :, :128] = ends[:16]
    out[cells + 32 :, 128:] = ends[16:]


def role(step, even):
    step = jnp.asarray(step)
    return jnp.where(step == 0, 0, jnp.where((step > 0) == even, 1, 2))


def position():
    col = lax.axis_index("col")
    return lax.axis_index("row"), col >> 1, col & 1


def tile_of(offset):
    row, chip, core = position()
    down, across = offset // 5 - 1, offset % 5 - 2
    return (
        role(down, row % 2 == 0) * 6 + role((core + across) >> 1, chip % 2 == 0) * 2 + (across & 1)
    )


def tiles_beside():
    row, chip, core = position()
    row_even, chip_even = row % 2 == 0, chip % 2 == 0
    north, south = role(-1, row_even) * 6, role(1, row_even) * 6
    west = jnp.where(core == 0, role(-1, chip_even), 0) * 2 + 1
    east = jnp.where(core == 0, 0, role(1, chip_even)) * 2 + 1
    return [north, south, west, east, north + west, north + east, south + west, south + east]


def spread_rows(weight, narrow, wide, lead):
    narrow[...] = weight[...].astype(F32)
    wide[...] = jnp.zeros_like(wide)
    for k in range(wide.shape[0] // 128):
        for u in range(SPAN):
            row = k * 128 + (u % 4) * 32 + (u // 4) * SPAN + lead
            at = (k * SPAN + u) * SPAN
            wide[row : row + SPAN] = narrow[at : at + SPAN]


def forward_kernel(partners, counts, radius, first, context, cotangent, conv_weight, corr_weight, *refs):
    around, refs = refs[:14], refs[14:]
    motion, context_grad, facing, away, ends, weights_sent, weights_kept, parts = refs[:8]
    edges, cot_taps, taps_back, taps, flipped, narrow, wide, spread, weight_grads = refs[8:17]
    sems, edge_sems = refs[17:]
    cells = first.shape[0]
    slots = parts.shape[0]
    height = cells + 48

    def tile_rows(t, start, size):
        r, x, other = t // 6, t // 2 % 3, t % 2
        which = r if x == 0 else 2 + x + (2 if r else 0)
        lead = (r - 1) * height if r and x else 0
        return around[2 * which + other].at[pl.ds(lead + start, size)]

    row_sides, chip_sides = (6, 12), (1, 3, 5)
    options = [row_sides] * 2 + [chip_sides] * 2 + [[r + x for r in row_sides for x in chip_sides]] * 4
    for n, tile in enumerate(tiles_beside()):
        for t in options[n]:
            @pl.when(tile == t)
            def _():
                pltpu.make_async_copy(
                    tile_rows(t, cells, 48), edges.at[n], edge_sems.at[n]
                ).start()
    for k in range(slots):
        tile = tile_of(partners[0, 0, k])
        for t in range(18):
            @pl.when(tile == t)
            def _():
                pltpu.make_async_copy(
                    tile_rows(t, 0, cells), parts.at[k, pl.ds(GROUP, cells)], sems.at[k]
                ).start()
        parts[k, :GROUP] = jnp.zeros((GROUP, parts.shape[2]), BF16)
        parts[k, GROUP + cells :] = jnp.zeros((GROUP, parts.shape[2]), BF16)
    inside = tap_mask(radius[0, 0], LEAD, True)
    flip = flip_matrix()
    gains = []
    for k in range(slots):
        live = jnp.where(k < counts[0, 0], 1.0 / math.sqrt(first.shape[1]), 0.0).astype(F32)
        gains.append(jnp.where(inside, live, 0.0))
    for q in range(cells // GROUP):
        at = slice(q * GROUP, (q + 1) * GROUP)
        flipped[at] = jnp.dot(flip, first[at], preferred_element_type=F32).astype(BF16)
    spread_rows(corr_weight, narrow, wide, LEAD)
    spread[...] = wide[...].astype(BF16)
    for n in range(8):
        pltpu.make_async_copy(tile_rows(0, cells, 48), edges.at[n], edge_sems.at[n]).wait()
    north, south = edges[0, :32, 128:], edges[1, :32, :128]
    west = jnp.concatenate(
        [
            edges[4, :32, 128:].astype(F32)[31:],
            edges[2, 32:, 128:].astype(F32),
            edges[6, :32, :128].astype(F32)[31:],
        ]
    )
    east = jnp.concatenate(
        [
            edges[5, :32, 128:].astype(F32)[:1],
            edges[3, 32:, :128].astype(F32),
            edges[7, :32, :128].astype(F32)[:1],
        ]
    )
    write_taps(cot_taps, cotangent, north, south, west, east, True)
    grad_motion = jnp.zeros(context_grad.shape, F32)
    for a in range(3):
        start = (2 - a) * 32
        for b in range(3):
            grad_motion += lax.dot_general(
                cot_taps[start : start + cells, b * 128 : (b + 1) * 128],
                conv_weight[a, b],
                (((1,), (1,)), ((), ())),
                preferred_element_type=F32,
            )
    for k in range(slots):
        pltpu.make_async_copy(
            tile_rows(0, 0, cells), parts.at[k, pl.ds(GROUP, cells)], sems.at[k]
        ).wait()
    for q in range(cells // GROUP):
        at = slice(q * GROUP, (q + 1) * GROUP)
        features = flipped[at]
        for k in range(slots):
            scores = lax.dot_general(
                features,
                parts[k, q * GROUP : q * GROUP + WINDOW],
                (((1,), (1,)), ((), ())),
                preferred_element_type=F32,
            )
            turn = WINDOW + REACH + LEAD - (GROUP - 1)
            band = pltpu.roll(scores, turn, 1, stride=1, stride_axis=0) * gains[k]
            packed = (
                band[:, :128]
                + pltpu.roll(band[:, 128:256], SPAN, 1)
                + pltpu.roll(band[:, 256:], 2 * SPAN, 1)
            )
            taps_back[at, k * 128 : (k + 1) * 128] = packed.astype(BF16)
    for q in range(cells // GROUP):
        at = slice(q * GROUP, (q + 1) * GROUP)
        taps[at] = jnp.dot(flip, taps_back[at], preferred_element_type=F32).astype(BF16)
    pre = jnp.dot(taps[...], spread[...], preferred_element_type=F32) + context[...].astype(
        F32
    )
    sigma = jax.nn.sigmoid(pre)
    motion[...] = (pre * sigma).astype(BF16)
    context_grad[...] = (grad_motion * sigma * (1.0 + pre * (1.0 - sigma))).astype(BF16)
    row, _, core = position()
    row_odd = row % 2
    facing[...] = motion[pl.ds(pl.multiple_of((1 - row_odd) * (cells - 32), 32), 32)]
    away[...] = motion[pl.ds(pl.multiple_of(row_odd * (cells - 32), 32), 32)]
    ends[...] = outer_columns(motion).reshape(ends.shape)
    over_cells = (((0,), (0,)), ((), ()))
    for a in range(3):
        start = (2 - a) * 32
        term = lax.dot_general(
            motion[...], cot_taps[start : start + cells], over_cells, preferred_element_type=F32
        )
        for b in range(3):
            weight_grads[(3 * a + b) * 256 : (3 * a + b + 1) * 256] = term[
                :, b * 128 : (b + 1) * 128
            ]
    term = lax.dot_general(taps[...], context_grad[...], over_cells, preferred_element_type=F32)
    base = 9 * 256
    for h in range(2):
        weight_grads[base + h * 384 + 320 : base + (h + 1) * 384] = jnp.zeros((64, 128), F32)
        for k in range(slots):
            for u in range(SPAN):
                row = k * 128 + (u % 4) * 32 + (u // 4) * SPAN + LEAD
                to = base + h * 384 + (k * SPAN + u) * SPAN
                weight_grads[to : to + SPAN] = term[row : row + SPAN, h * 128 : (h + 1) * 128]
    half = weight_grads.shape[0] // 2
    weights_kept[...] = weight_grads[pl.ds(pl.multiple_of(core * half, half), half)]
    weights_sent[...] = weight_grads[pl.ds(pl.multiple_of((1 - core) * half, half), half)].astype(
        BF16
    )


def scores_kernel(
    counts, radius, context_grad, corr_weight, parts, first_grad, scores, narrow, wide, spread
):
    cells = context_grad.shape[0]
    slots = parts.shape[0]
    inside = tap_mask(radius[0, 0], LEAD_BACK, False)
    spread_rows(corr_weight, narrow, wide, LEAD_BACK)
    spread[...] = wide[...].astype(BF16)
    for q in range(cells // GROUP):
        at = slice(q * GROUP, (q + 1) * GROUP)
        packed = (
            lax.dot_general(
                context_grad[at],
                spread[...],
                (((1,), (1,)), ((), ())),
                preferred_element_type=F32,
            )
            .astype(BF16)
            .astype(F32)
        )
        first_here = jnp.zeros((GROUP, parts.shape[2]), F32)
        for k in range(slots):
            mine = packed[:, k * 128 : (k + 1) * 128]
            band = jnp.concatenate(
                [mine, pltpu.roll(mine, 128 - SPAN, 1), pltpu.roll(mine, 128 - 2 * SPAN, 1)],
                axis=1,
            )
            band = jnp.where(inside & (k < counts[0, 0]), band, 0.0)
            turn = WINDOW - REACH - LEAD_BACK
            here = pltpu.roll(band, turn, 1, stride=1, stride_axis=0).astype(BF16)
            scores[k, at] = here
            window = slice(q * GROUP, q * GROUP + WINDOW)
            first_here += jnp.dot(here, parts[k, window], preferred_element_type=F32)
        first_grad[at] = first_here * (1.0 / math.sqrt(parts.shape[2]))


def partners_kernel(partners, first, scores, *refs):
    *kept, lent, totals = refs[-5:]
    cells, channels = first.shape
    scale = 1.0 / math.sqrt(channels)
    for ref in (*kept, lent, totals):
        ref[...] = jnp.zeros_like(ref)
    across = first[...].T
    for k in range(scores.shape[0]):
        for q in range(cells // GROUP):
            at = slice(q * GROUP, (q + 1) * GROUP)
            totals[k, :, q * GROUP : q * GROUP + WINDOW] += jnp.dot(
                across[:, at], scores[k, at], preferred_element_type=F32
            )
        value = (totals[k, :, GROUP : GROUP + cells] * scale).astype(BF16).T
        place = tile_of(partners[0, 0, k])
        for x in range(3):
            @pl.when(place % 6 == 2 * x)
            def _():
                kept[x][place // 6] = value

        @pl.when(place % 2 == 1)
        def _():
            lent[(place % 6 > 1).astype(jnp.int32) * 3 + place // 6] = value


def features_kernel(motion, north, south, west, east, weight, out, taps):
    cells = out.shape[0]
    write_taps(taps, motion, north[...], south[...], west[...], east[...], False)
    total = jnp.zeros(out.shape, F32)
    for a in range(3):
        total += jnp.dot(taps[a * 32 : a * 32 + cells], weight[a], preferred_element_type=F32)
    out[...] = total.astype(BF16)


def finish_kernel(*refs):
    shards, (conv, corr, whole) = refs[:8], refs[8:]
    size = shards[0].shape[0]
    _, chip, core = position()
    half = whole.shape[0] // 2
    for n, ref in enumerate(shards):
        owner = core if n < 4 else 1 - core
        to = owner * half + (chip ^ (n % 4)) * size
        whole[pl.ds(pl.multiple_of(to, size), size)] = ref[...].astype(F32)
    conv[...] = whole[: conv.shape[0]]
    base = conv.shape[0]
    for h in range(2):
        corr[:, h * 128 : (h + 1) * 128] = whole[base + h * 384 : base + h * 384 + corr.shape[0]]


def call(kernel, out_shape, in_specs, scratch=(), flops=1000):
    return pl.pallas_call(
        kernel,
        out_shape=out_shape,
        in_specs=in_specs,
        out_specs=jax.tree.map(lambda _: VMEM, out_shape),
        scratch_shapes=list(scratch),
        compiler_params=pltpu.CompilerParams(vmem_limit_bytes=VMEM_LIMIT),
        cost_estimate=pl.CostEstimate(flops=flops, bytes_accessed=flops // 300, transcendentals=0),
    )


def sum_everywhere(cur, axis, unit):
    mine = cur.astype(BF16)
    got = [swap(mine, axis, unit * s).astype(F32) for s in (1, 2, 3)]
    return (mine.astype(F32) + got[0]) + (got[1] + got[2])


def forward(tables, first, context, cotangent, conv_weight, corr_weight, around):
    cells, channels = first.shape
    hidden = context.shape[1]
    slots = tables[0].shape[-1]
    shape = jax.ShapeDtypeStruct
    total_rows = 9 * hidden + 2 * 384
    return call(
        forward_kernel,
        (
            shape((cells, hidden), BF16),
            shape((cells, hidden), BF16),
            shape((32, hidden), BF16),
            shape((32, hidden), BF16),
            shape((2, 16, hidden), BF16),
            shape((total_rows // 2, 128), BF16),
            shape((total_rows // 2, 128), F32),
            shape((slots, cells + 2 * GROUP, channels), BF16),
        ),
        [SMEM] * 3 + [VMEM] * 5 + [ANY] * 14,
        [
            pltpu.VMEM((8, 48, channels), BF16),
            pltpu.VMEM((cells + 64, 384), BF16),
            pltpu.VMEM((cells, slots * 128), BF16),
            pltpu.VMEM((cells, slots * 128), BF16),
            pltpu.VMEM((cells, channels), BF16),
            pltpu.VMEM(corr_weight.shape, F32),
            pltpu.VMEM((slots * 128, hidden), F32),
            pltpu.VMEM((slots * 128, hidden), BF16),
            pltpu.VMEM((total_rows, 128), F32),
            pltpu.SemaphoreType.DMA((slots,)),
            pltpu.SemaphoreType.DMA((8,)),
        ],
        flops=3 * 10**9,
    )(*tables, first, context, cotangent, conv_weight, corr_weight, *around)


def backward_scores(tables, context_grad, corr_weight, parts):
    cells, hidden = context_grad.shape
    slots, _, channels = parts.shape
    shape = jax.ShapeDtypeStruct
    return call(
        scores_kernel,
        (shape((cells, channels), F32), shape((slots, cells, WINDOW), BF16)),
        [SMEM] * 2 + [VMEM] * 3,
        [
            pltpu.VMEM(corr_weight.shape, F32),
            pltpu.VMEM((slots * 128, hidden), F32),
            pltpu.VMEM((slots * 128, hidden), BF16),
        ],
        flops=4 * 10**9,
    )(*tables[1:], context_grad, corr_weight, parts)


def backward_partners(tables, first, scores, after=()):
    cells, channels = first.shape
    shape = jax.ShapeDtypeStruct
    return call(
        partners_kernel,
        (*[shape((3, cells, channels), BF16)] * 3, shape((6, cells, channels), BF16)),
        [SMEM] + [VMEM] * 2 + [ANY] * len(after),
        [pltpu.VMEM((scores.shape[0], channels, cells + 2 * GROUP), F32)],
        flops=4 * 10**9,
    )(tables[0], first, scores, *after)


def body(
    frame_one, frame_two, context, cotangent, corr_weight, conv_weight, partners, counts, radius
):
    rows_tile, cols_tile, channels = frame_one.shape
    slots = partners.shape[-1]
    cells = rows_tile * cols_tile
    hidden = context.shape[-1]
    out_width = conv_weight.shape[-1]
    row, col = lax.axis_index("row"), lax.axis_index("col")
    core, chip = col % 2, col // 2
    row_even, chip_even, col_even = row % 2 == 0, chip % 2 == 0, core == 0
    tables = (partners, counts, radius)
    first = frame_one.reshape(cells, channels)
    shape = jax.ShapeDtypeStruct
    cot = cotangent.reshape(cells, out_width)
    own = call(pack_kernel, shape((cells + 48, channels), BF16), [VMEM] * 2)(
        frame_two.reshape(cells, channels), cot
    )
    rows = [swap_pairs(own, "row", odd) for odd in (1, 0)][::-1]
    sides = [swap_pairs(own, "col", odd, 2) for odd in (0, 1)]
    both = jnp.concatenate(rows)
    corners = [swap_pairs(both, "col", odd, 2) for odd in (0, 1)]
    around = []
    for tile in (own, *rows, *sides, *corners):
        around += [tile, swap(tile, "col", 1)]
    motion, context_grad, facing, away, ends, weights_sent, weights_kept, parts = forward(
        tables, first, context.reshape(cells, hidden), cot, conv_weight, corr_weight, around
    )
    total = weights_kept + swap(weights_sent, "col", 1).astype(F32)
    size = total.shape[0] // 4
    pieces = [lax.dynamic_slice_in_dim(total, (chip ^ s) * size, size) for s in range(4)]
    north, south = rim_rows(facing, away, row_even)
    north, south, *gone = lax.optimization_barrier(
        (north, south, *[piece.astype(BF16) for piece in pieces[1:]])
    )
    got = [swap(piece, "col", 2 * s) for s, piece in zip((1, 2, 3), gone)]
    around_motion = (north, south, *rim_columns(north, south, ends, col_even))
    first_grad, scores = backward_scores(tables, context_grad, corr_weight, parts)
    *kept, lent = backward_partners(tables, first, scores, got)
    lent = swap(lent, "col", 1)
    side = jnp.where((core == 0) == chip_even, 1, 2)
    sent = [
        (kept[x].astype(F32) + jnp.where(side == x, lent[3:].astype(F32), 0.0)).astype(BF16)
        for x in (1, 2)
    ]
    total = (pieces[0] + got[0].astype(F32)) + (got[1].astype(F32) + got[2].astype(F32))
    total, *ready = lax.optimization_barrier((total, *sent, *around_motion))
    sent, around_motion = ready[:2], ready[2:]
    middle = kept[0].astype(F32) + lent[:3].astype(F32)
    for x in (1, 2):
        middle += swap_pairs(sent[x - 1], "col", x - 1, 2).astype(F32)
    total = sum_everywhere(sum_everywhere(total, "row", 1), "row", 4).astype(BF16)
    shards = [total] + [swap(total, "col", 2 * s) for s in (1, 2, 3)]
    features = call(
        features_kernel,
        shape((cells, out_width), BF16),
        [VMEM] * 6,
        [pltpu.VMEM(((rows_tile + 2) * cols_tile, 3 * hidden), BF16)],
    )(motion, *around_motion, conv_weight.reshape(3, 3 * hidden, out_width))
    features, *shards = lax.optimization_barrier((features, *shards))
    shards += [swap(shard, "col", 1) for shard in shards]
    second_grad = middle[0]
    for r in (1, 2):
        second_grad += swap_pairs(middle[r].astype(BF16), "row", r - 1).astype(F32)
    conv_total, corr_total = call(
        finish_kernel,
        (shape((9 * hidden, out_width), F32), shape(corr_weight.shape, F32)),
        [VMEM] * 8,
        [pltpu.VMEM((9 * hidden + 2 * 384, 128), F32)],
    )(*shards)
    return (
        features.reshape(rows_tile, cols_tile, out_width),
        context_grad.reshape(rows_tile, cols_tile, hidden),
        first_grad.reshape(frame_one.shape),
        second_grad.reshape(frame_two.shape),
        corr_total,
        conv_total.reshape(conv_weight.shape),
    )


def solution(mesh):
    return jax.shard_map(
        body,
        mesh=mesh,
        in_specs=(
            P("row", "col", None),
            P("row", "col", None),
            P("row", "col", None),
            P("row", "col", None),
            P(),
            P(),
            P("row", "col", None),
            P("row", "col"),
            P("row", "col"),
        ),
        out_specs=(
            P("row", "col", None),
            P("row", "col", None),
            P("row", "col", None),
            P("row", "col", None),
            P(),
            P(),
        ),
        check_vma=False,
    )
```

```python
import functools
import math

import jax
import jax.numpy as jnp
from jax import lax
from jax.experimental import pallas as pl
from jax.experimental.pallas import tpu as pltpu
from jax.sharding import PartitionSpec as P

REACH = 4
SPAN = 2 * REACH + 1
GROUP = 128
WINDOW = 384
LEAD, LEAD_BACK = 3, 4
F32 = jnp.float32
BF16 = jnp.bfloat16
VMEM_LIMIT = 56 * 1024 * 1024
VMEM = pl.BlockSpec(memory_space=pltpu.VMEM)
SMEM = pl.BlockSpec(memory_space=pltpu.SMEM)
ANY = pl.BlockSpec(memory_space=pl.ANY)


def swap(array, axis, bits):
    return lax.ppermute(array, axis, [(i, i ^ bits) for i in range(lax.axis_size(axis))])


def swap_pairs(array, axis, odd, unit=1):
    count = lax.axis_size(axis) // unit
    pairs = []
    for i in range(odd, count - 1, 2):
        for low in range(unit):
            here, there = i * unit + low, (i + 1) * unit + low
            pairs += [(here, there), (there, here)]
    return lax.ppermute(array, axis, pairs)


def rim(facing, away, ends, row_even, col_even):
    even = swap_pairs(facing, "row", 0)
    odd = swap_pairs(away, "row", 1)
    north, south = jnp.where(row_even, odd, even), jnp.where(row_even, even, odd)
    left = jnp.concatenate([north[:1], ends[0], south[:1]])
    right = jnp.concatenate([north[-1:], ends[1], south[-1:]])
    even = swap_pairs(jnp.where(col_even, right, left), "col", 0)
    odd = swap_pairs(jnp.where(col_even, left, right), "col", 1)
    west, east = jnp.where(col_even, odd, even), jnp.where(col_even, even, odd)
    return north, south, west, east


def outer_columns(cells):
    count = cells.shape[0]
    line = lax.broadcasted_iota(jnp.int32, (32, count), 0)
    cell = lax.broadcasted_iota(jnp.int32, (32, count), 1)
    wanted = (line & 15) * 32 + (line >> 4) * 31
    pick = (cell == wanted).astype(F32).astype(BF16)
    return jnp.dot(pick, cells[...], preferred_element_type=F32).astype(BF16)


def write_taps(taps, own, north, south, west, east, backwards):
    width = own.shape[1]
    line = north.shape[0]
    taps[:line, width : 2 * width] = north
    taps[line:-line, width : 2 * width] = own[...]
    taps[-line:, width : 2 * width] = south
    middle = taps[:, width : 2 * width].astype(F32)
    place = lax.broadcasted_iota(jnp.int32, middle.shape, 0) % line

    def stretched(ends):
        shape = (ends.shape[0], line, width)
        return jnp.broadcast_to(ends.astype(F32)[:, None], shape).reshape(middle.shape)

    left = jnp.where(place == 0, stretched(west), pltpu.roll(middle, 1, 0)).astype(BF16)
    right = jnp.where(
        place == line - 1, stretched(east), pltpu.roll(middle, middle.shape[0] - 1, 0)
    ).astype(BF16)
    taps[:, :width] = right if backwards else left
    taps[:, 2 * width :] = left if backwards else right


def tap_mask(radius, lead, backwards):
    cell = lax.broadcasted_iota(jnp.int32, (GROUP, WINDOW), 0)
    cell = GROUP - 1 - cell if backwards else cell
    tap = lax.broadcasted_iota(jnp.int32, (GROUP, WINDOW), 1)
    down = (tap >> 5) - REACH
    across = (tap & 31) - lead - REACH
    column = (cell & 31) + across
    return (
        (jnp.abs(down) <= radius)
        & (jnp.abs(across) <= radius)
        & (column >= 0)
        & (column < 32)
    )


def flip_matrix():
    return (
        (
            lax.broadcasted_iota(jnp.int32, (GROUP, GROUP), 0)
            + lax.broadcasted_iota(jnp.int32, (GROUP, GROUP), 1)
            == GROUP - 1
        )
        .astype(F32)
        .astype(BF16)
    )


def pack_kernel(tile, cotangent, out):
    cells = tile.shape[0]
    out[:cells] = tile[...]
    out[cells : cells + 32, :128] = cotangent[:32]
    out[cells : cells + 32, 128:] = cotangent[cells - 32 :]
    ends = outer_columns(cotangent)
    out[cells + 32 :, :128] = ends[:16]
    out[cells + 32 :, 128:] = ends[16:]


def role(step, even):
    step = jnp.asarray(step)
    return jnp.where(step == 0, 0, jnp.where((step > 0) == even, 1, 2))


def position():
    col = lax.axis_index("col")
    return lax.axis_index("row"), col >> 1, col & 1


def tile_of(offset):
    row, chip, core = position()
    down, across = offset // 5 - 1, offset % 5 - 2
    return (
        role(down, row % 2 == 0) * 6 + role((core + across) >> 1, chip % 2 == 0) * 2 + (across & 1)
    )


def tiles_beside():
    row, chip, core = position()
    row_even, chip_even = row % 2 == 0, chip % 2 == 0
    north, south = role(-1, row_even) * 6, role(1, row_even) * 6
    west = jnp.where(core == 0, role(-1, chip_even), 0) * 2 + 1
    east = jnp.where(core == 0, 0, role(1, chip_even)) * 2 + 1
    return [north, south, west, east, north + west, north + east, south + west, south + east]


def spread_kernel(weight, out, out_back, narrow, wide):
    narrow[...] = weight[...].astype(F32)
    for lead, ref in ((LEAD, out), (LEAD_BACK, out_back)):
        wide[...] = jnp.zeros_like(wide)
        for k in range(4):
            for u in range(SPAN):
                row = k * 128 + (u % 4) * 32 + (u // 4) * SPAN + lead
                at = (k * SPAN + u) * SPAN
                wide[row : row + SPAN] = narrow[at : at + SPAN]
        ref[...] = wide[...].astype(BF16)


def forward_kernel(partners, counts, radius, first, context, cotangent, conv_weight, corr_weight, *refs):
    tiles, refs = refs[:18], refs[18:]
    parts, motion, context_grad, facing, away, ends, weights_sent, weights_kept = refs[:8]
    edges, cot_taps, taps_back, taps, flipped, weight_grads, sems, edge_sems = refs[8:]
    cells = first.shape[0]
    slots = parts.shape[0]
    row_sides, chip_sides = (6, 12), (1, 3, 5)
    options = [row_sides] * 2 + [chip_sides] * 2 + [[r + x for r in row_sides for x in chip_sides]] * 4
    for n, tile in enumerate(tiles_beside()):
        for t in options[n]:
            @pl.when(tile == t)
            def _():
                pltpu.make_async_copy(
                    tiles[t].at[pl.ds(cells, 48)], edges.at[n], edge_sems.at[n]
                ).start()
    for k in range(slots):
        tile = tile_of(partners[0, 0, k])
        for t in range(18):
            @pl.when(tile == t)
            def _():
                pltpu.make_async_copy(
                    tiles[t].at[pl.ds(0, cells)], parts.at[k, pl.ds(GROUP, cells)], sems.at[k]
                ).start()
        parts[k, :GROUP] = jnp.zeros((GROUP, parts.shape[2]), BF16)
        parts[k, GROUP + cells :] = jnp.zeros((GROUP, parts.shape[2]), BF16)
    inside = tap_mask(radius[0, 0], LEAD, True)
    flip = flip_matrix()
    gains = []
    for k in range(slots):
        live = jnp.where(k < counts[0, 0], 1.0 / math.sqrt(first.shape[1]), 0.0).astype(F32)
        gains.append(jnp.where(inside, live, 0.0))
    for q in range(cells // GROUP):
        at = slice(q * GROUP, (q + 1) * GROUP)
        flipped[at] = jnp.dot(flip, first[at], preferred_element_type=F32).astype(BF16)
    for n in range(8):
        pltpu.make_async_copy(tiles[0].at[pl.ds(cells, 48)], edges.at[n], edge_sems.at[n]).wait()
    north, south = edges[0, :32, 128:], edges[1, :32, :128]
    west = jnp.concatenate(
        [
            edges[4, :32, 128:].astype(F32)[31:],
            edges[2, 32:, 128:].astype(F32),
            edges[6, :32, :128].astype(F32)[31:],
        ]
    )
    east = jnp.concatenate(
        [
            edges[5, :32, 128:].astype(F32)[:1],
            edges[3, 32:, :128].astype(F32),
            edges[7, :32, :128].astype(F32)[:1],
        ]
    )
    write_taps(cot_taps, cotangent, north, south, west, east, True)
    grad_motion = jnp.zeros(context_grad.shape, F32)
    for a in range(3):
        start = (2 - a) * 32
        for b in range(3):
            grad_motion += lax.dot_general(
                cot_taps[start : start + cells, b * 128 : (b + 1) * 128],
                conv_weight[a, b],
                (((1,), (1,)), ((), ())),
                preferred_element_type=F32,
            )
    for k in range(slots):
        pltpu.make_async_copy(
            tiles[0].at[pl.ds(0, cells)], parts.at[k, pl.ds(GROUP, cells)], sems.at[k]
        ).wait()
    for q in range(cells // GROUP):
        at = slice(q * GROUP, (q + 1) * GROUP)
        features = flipped[at]
        for k in range(slots):
            scores = lax.dot_general(
                features,
                parts[k, q * GROUP : q * GROUP + WINDOW],
                (((1,), (1,)), ((), ())),
                preferred_element_type=F32,
            )
            turn = WINDOW + REACH + LEAD - (GROUP - 1)
            band = pltpu.roll(scores, turn, 1, stride=1, stride_axis=0) * gains[k]
            packed = (
                band[:, :128]
                + pltpu.roll(band[:, 128:256], SPAN, 1)
                + pltpu.roll(band[:, 256:], 2 * SPAN, 1)
            )
            taps_back[at, k * 128 : (k + 1) * 128] = packed.astype(BF16)
    for q in range(cells // GROUP):
        at = slice(q * GROUP, (q + 1) * GROUP)
        taps[at] = jnp.dot(flip, taps_back[at], preferred_element_type=F32).astype(BF16)
    pre = jnp.dot(taps[...], corr_weight[...], preferred_element_type=F32) + context[...].astype(
        F32
    )
    sigma = jax.nn.sigmoid(pre)
    motion[...] = (pre * sigma).astype(BF16)
    context_grad[...] = (grad_motion * sigma * (1.0 + pre * (1.0 - sigma))).astype(BF16)
    row, _, core = position()
    row_odd = row % 2
    facing[...] = motion[pl.ds(pl.multiple_of((1 - row_odd) * (cells - 32), 32), 32)]
    away[...] = motion[pl.ds(pl.multiple_of(row_odd * (cells - 32), 32), 32)]
    ends[...] = outer_columns(motion).reshape(ends.shape)
    over_cells = (((0,), (0,)), ((), ()))
    for a in range(3):
        start = (2 - a) * 32
        term = lax.dot_general(
            motion[...], cot_taps[start : start + cells], over_cells, preferred_element_type=F32
        )
        for b in range(3):
            weight_grads[(3 * a + b) * 256 : (3 * a + b + 1) * 256] = term[
                :, b * 128 : (b + 1) * 128
            ]
    term = lax.dot_general(taps[...], context_grad[...], over_cells, preferred_element_type=F32)
    base = 9 * 256
    for h in range(2):
        weight_grads[base + h * 384 + 320 : base + (h + 1) * 384] = jnp.zeros((64, 128), F32)
        for k in range(slots):
            for u in range(SPAN):
                row = k * 128 + (u % 4) * 32 + (u // 4) * SPAN + LEAD
                to = base + h * 384 + (k * SPAN + u) * SPAN
                weight_grads[to : to + SPAN] = term[row : row + SPAN, h * 128 : (h + 1) * 128]
    half = weight_grads.shape[0] // 2
    weights_kept[...] = weight_grads[pl.ds(pl.multiple_of(core * half, half), half)]
    weights_sent[...] = weight_grads[pl.ds(pl.multiple_of((1 - core) * half, half), half)].astype(
        BF16
    )


def backward_kernel(
    partners, counts, radius, first, context_grad, corr_weight, parts, first_grad, *refs
):
    cells = first.shape[0]
    slots = parts.shape[0]
    scale = 1.0 / math.sqrt(first.shape[1])
    inside = tap_mask(radius[0, 0], LEAD_BACK, False)
    *kept, lent, totals = refs
    for ref in refs:
        ref[...] = jnp.zeros_like(ref)
    across = first[...].T
    for q in range(cells // GROUP):
        at = slice(q * GROUP, (q + 1) * GROUP)
        packed = (
            lax.dot_general(
                context_grad[at],
                corr_weight[...],
                (((1,), (1,)), ((), ())),
                preferred_element_type=F32,
            )
            .astype(BF16)
            .astype(F32)
        )
        first_here = jnp.zeros((GROUP, first.shape[1]), F32)
        for k in range(slots):
            mine = packed[:, k * 128 : (k + 1) * 128]
            band = jnp.concatenate(
                [mine, pltpu.roll(mine, 128 - SPAN, 1), pltpu.roll(mine, 128 - 2 * SPAN, 1)],
                axis=1,
            )
            band = jnp.where(inside & (k < counts[0, 0]), band, 0.0)
            scores = pltpu.roll(band, WINDOW - REACH - LEAD_BACK, 1, stride=1, stride_axis=0).astype(BF16)
            window = slice(q * GROUP, q * GROUP + WINDOW)
            first_here += jnp.dot(scores, parts[k, window], preferred_element_type=F32)
            totals[k, :, window] += jnp.dot(
                across[:, at], scores, preferred_element_type=F32
            )
        first_grad[at] = first_here * scale
    for k in range(slots):
        value = (totals[k, :, GROUP : GROUP + cells] * scale).astype(BF16).T
        place = tile_of(partners[0, 0, k])
        for x in range(3):
            @pl.when(place % 6 == 2 * x)
            def _():
                kept[x][place // 6] = value

        @pl.when(place % 2 == 1)
        def _():
            lent[(place % 6 > 1).astype(jnp.int32) * 3 + place // 6] = value


def features_kernel(motion, north, south, west, east, weight, out, taps):
    cells = out.shape[0]
    write_taps(taps, motion, north[...], south[...], west[...], east[...], False)
    total = jnp.zeros(out.shape, F32)
    for a in range(3):
        total += jnp.dot(taps[a * 32 : a * 32 + cells], weight[a], preferred_element_type=F32)
    out[...] = total.astype(BF16)


def finish_kernel(*refs):
    shards, (conv, corr, whole) = refs[:8], refs[8:]
    size = shards[0].shape[0]
    _, chip, core = position()
    half = whole.shape[0] // 2
    for n, ref in enumerate(shards):
        owner = core if n < 4 else 1 - core
        to = owner * half + (chip ^ (n % 4)) * size
        whole[pl.ds(pl.multiple_of(to, size), size)] = ref[...].astype(F32)
    conv[...] = whole[: conv.shape[0]]
    base = conv.shape[0]
    for h in range(2):
        corr[:, h * 128 : (h + 1) * 128] = whole[base + h * 384 : base + h * 384 + corr.shape[0]]


def call(kernel, out_shape, in_specs, scratch=(), flops=0):
    return pl.pallas_call(
        kernel,
        out_shape=out_shape,
        in_specs=in_specs,
        out_specs=jax.tree.map(lambda _: VMEM, out_shape),
        scratch_shapes=list(scratch),
        compiler_params=pltpu.CompilerParams(vmem_limit_bytes=VMEM_LIMIT),
        cost_estimate=pl.CostEstimate(flops=flops, bytes_accessed=flops // 300, transcendentals=0),
    )


def sum_everywhere(cur, axis, unit):
    mine = cur.astype(BF16)
    got = [swap(mine, axis, unit * s).astype(F32) for s in (1, 2, 3)]
    return (mine.astype(F32) + got[0]) + (got[1] + got[2])


def body(
    frame_one, frame_two, context, cotangent, corr_weight, conv_weight, partners, counts, radius
):
    rows_tile, cols_tile, channels = frame_one.shape
    slots = partners.shape[-1]
    cells = rows_tile * cols_tile
    hidden = context.shape[-1]
    out_width = conv_weight.shape[-1]
    row, col = lax.axis_index("row"), lax.axis_index("col")
    core, chip = col % 2, col // 2
    row_even, chip_even, col_even = row % 2 == 0, chip % 2 == 0, core == 0
    tables = (partners, counts, radius)
    first = frame_one.reshape(cells, channels)
    shape = jax.ShapeDtypeStruct
    cot = cotangent.reshape(cells, out_width)
    own = call(pack_kernel, shape((cells + 48, channels), BF16), [VMEM] * 2)(
        frame_two.reshape(cells, channels), cot
    )
    tiles = {(0, 0): own}
    for r in (1, 2):
        tiles[r, 0] = swap_pairs(own, "row", r - 1)
        tiles[0, r] = swap_pairs(own, "col", r - 1, 2)
    for r in (1, 2):
        tiles[r, r] = swap_pairs(tiles[r, 0], "col", r - 1, 2)
        tiles[r, 3 - r] = swap_pairs(tiles[0, 3 - r], "row", r - 1)
    around = []
    for r in range(3):
        for x in range(3):
            around += [tiles[r, x], swap(tiles[r, x], "col", 1)]
    spread, spread_back = call(
        spread_kernel,
        (shape((slots * 128, hidden), BF16), shape((slots * 128, hidden), BF16)),
        [VMEM],
        [pltpu.VMEM(corr_weight.shape, F32), pltpu.VMEM((slots * 128, hidden), F32)],
    )(corr_weight)
    total_rows = 9 * hidden + 2 * 384
    parts, motion, context_grad, facing, away, ends, weights_sent, weights_kept = call(
        forward_kernel,
        (
            shape((slots, cells + 2 * GROUP, channels), BF16),
            shape((cells, hidden), BF16),
            shape((cells, hidden), BF16),
            shape((cols_tile, hidden), BF16),
            shape((cols_tile, hidden), BF16),
            shape((2, rows_tile, hidden), BF16),
            shape((total_rows // 2, 128), BF16),
            shape((total_rows // 2, 128), F32),
        ),
        [SMEM] * 3 + [VMEM] * 5 + [ANY] * 18,
        [
            pltpu.VMEM((8, 48, channels), BF16),
            pltpu.VMEM(((rows_tile + 2) * cols_tile, 3 * out_width), BF16),
            pltpu.VMEM((cells, slots * 128), BF16),
            pltpu.VMEM((cells, slots * 128), BF16),
            pltpu.VMEM((cells, channels), BF16),
            pltpu.VMEM((total_rows, 128), F32),
            pltpu.SemaphoreType.DMA((slots,)),
            pltpu.SemaphoreType.DMA((8,)),
        ],
        flops=3 * 10**9,
    )(
        *tables,
        first,
        context.reshape(cells, hidden),
        cot,
        conv_weight,
        spread,
        *around,
    )
    total = weights_kept + swap(weights_sent, "col", 1).astype(F32)
    size = total.shape[0] // 4
    pieces = [lax.dynamic_slice_in_dim(total, (chip ^ s) * size, size) for s in range(4)]
    got = [swap(pieces[s].astype(BF16), "col", 2 * s) for s in (1, 2, 3)]
    first_grad, *kept, lent = call(
        backward_kernel,
        (
            shape((cells, channels), F32),
            *[shape((3, cells, channels), BF16)] * 3,
            shape((6, cells, channels), BF16),
        ),
        [SMEM] * 3 + [VMEM] * 4,
        [pltpu.VMEM((slots, channels, cells + 2 * GROUP), F32)],
        flops=3 * 10**9,
    )(*tables, first, context_grad, spread_back, parts)
    lent = swap(lent, "col", 1)
    side = jnp.where((core == 0) == chip_even, 1, 2)
    sent = [
        (kept[x].astype(F32) + jnp.where(side == x, lent[3:].astype(F32), 0.0)).astype(BF16)
        for x in (1, 2)
    ]
    total = (pieces[0] + got[0].astype(F32)) + (got[1].astype(F32) + got[2].astype(F32))
    around_motion = rim(facing, away, ends, row_even, col_even)
    total, *ready = lax.optimization_barrier((total, *sent, *around_motion))
    sent, around_motion = ready[:2], ready[2:]
    middle = kept[0].astype(F32) + lent[:3].astype(F32)
    for x in (1, 2):
        middle += swap_pairs(sent[x - 1], "col", x - 1, 2).astype(F32)
    total = sum_everywhere(sum_everywhere(total, "row", 1), "row", 4).astype(BF16)
    shards = [total] + [swap(total, "col", 2 * s) for s in (1, 2, 3)]
    shards += [swap(shard, "col", 1) for shard in shards]
    second_grad = middle[0]
    for r in (1, 2):
        second_grad += swap_pairs(middle[r].astype(BF16), "row", r - 1).astype(F32)
    features = call(
        features_kernel,
        shape((cells, out_width), BF16),
        [VMEM] * 6,
        [pltpu.VMEM(((rows_tile + 2) * cols_tile, 3 * hidden), BF16)],
        flops=10**9,
    )(
        motion,
        *around_motion,
        conv_weight.reshape(3, 3 * hidden, out_width),
    )
    conv_total, corr_total = call(
        finish_kernel,
        (shape((9 * hidden, out_width), F32), shape(corr_weight.shape, F32)),
        [VMEM] * 8,
        [pltpu.VMEM((total_rows, 128), F32)],
    )(*shards)
    return (
        features.reshape(rows_tile, cols_tile, out_width),
        context_grad.reshape(rows_tile, cols_tile, hidden),
        first_grad.reshape(frame_one.shape),
        second_grad.reshape(frame_two.shape),
        corr_total,
        conv_total.reshape(conv_weight.shape),
    )


def solution(mesh):
    return jax.shard_map(
        body,
        mesh=mesh,
        in_specs=(
            P("row", "col", None),
            P("row", "col", None),
            P("row", "col", None),
            P("row", "col", None),
            P(),
            P(),
            P("row", "col", None),
            P("row", "col"),
            P("row", "col"),
        ),
        out_specs=(
            P("row", "col", None),
            P("row", "col", None),
            P("row", "col", None),
            P("row", "col", None),
            P(),
            P(),
        ),
        check_vma=False,
    )
```

```python
import functools
import math

import jax
import jax.numpy as jnp
from jax import lax
from jax.experimental import pallas as pl
from jax.experimental.pallas import tpu as pltpu
from jax.sharding import PartitionSpec as P

REACH = 4
SPAN = 2 * REACH + 1
GROUP = 128
WINDOW = 384
LEAD, LEAD_BACK = 3, 4
F32 = jnp.float32
BF16 = jnp.bfloat16
VMEM_LIMIT = 56 * 1024 * 1024
VMEM = pl.BlockSpec(memory_space=pltpu.VMEM)
SMEM = pl.BlockSpec(memory_space=pltpu.SMEM)
ANY = pl.BlockSpec(memory_space=pl.ANY)


def swap(array, axis, bits):
    return lax.ppermute(array, axis, [(i, i ^ bits) for i in range(lax.axis_size(axis))])


def swap_pairs(array, axis, odd, unit=1):
    count = lax.axis_size(axis) // unit
    pairs = []
    for i in range(odd, count - 1, 2):
        for low in range(unit):
            here, there = i * unit + low, (i + 1) * unit + low
            pairs += [(here, there), (there, here)]
    return lax.ppermute(array, axis, pairs)


def rim(facing, away, ends, row_even, col_even):
    even = swap_pairs(facing, "row", 0)
    odd = swap_pairs(away, "row", 1)
    north, south = jnp.where(row_even, odd, even), jnp.where(row_even, even, odd)
    left = jnp.concatenate([north[:1], ends[0], south[:1]])
    right = jnp.concatenate([north[-1:], ends[1], south[-1:]])
    even = swap_pairs(jnp.where(col_even, right, left), "col", 0)
    odd = swap_pairs(jnp.where(col_even, left, right), "col", 1)
    west, east = jnp.where(col_even, odd, even), jnp.where(col_even, even, odd)
    return north, south, west, east


def outer_columns(cells):
    count = cells.shape[0]
    line = lax.broadcasted_iota(jnp.int32, (32, count), 0)
    cell = lax.broadcasted_iota(jnp.int32, (32, count), 1)
    wanted = (line & 15) * 32 + (line >> 4) * 31
    pick = (cell == wanted).astype(F32).astype(BF16)
    return jnp.dot(pick, cells[...], preferred_element_type=F32).astype(BF16)


def write_taps(taps, own, north, south, west, east, backwards):
    width = own.shape[1]
    line = north.shape[0]
    taps[:line, width : 2 * width] = north
    taps[line:-line, width : 2 * width] = own[...]
    taps[-line:, width : 2 * width] = south
    middle = taps[:, width : 2 * width].astype(F32)
    place = lax.broadcasted_iota(jnp.int32, middle.shape, 0) % line

    def stretched(ends):
        shape = (ends.shape[0], line, width)
        return jnp.broadcast_to(ends.astype(F32)[:, None], shape).reshape(middle.shape)

    left = jnp.where(place == 0, stretched(west), pltpu.roll(middle, 1, 0)).astype(BF16)
    right = jnp.where(
        place == line - 1, stretched(east), pltpu.roll(middle, middle.shape[0] - 1, 0)
    ).astype(BF16)
    taps[:, :width] = right if backwards else left
    taps[:, 2 * width :] = left if backwards else right


def tap_mask(radius, lead, backwards):
    cell = lax.broadcasted_iota(jnp.int32, (GROUP, WINDOW), 0)
    cell = GROUP - 1 - cell if backwards else cell
    tap = lax.broadcasted_iota(jnp.int32, (GROUP, WINDOW), 1)
    down = (tap >> 5) - REACH
    across = (tap & 31) - lead - REACH
    column = (cell & 31) + across
    return (
        (jnp.abs(down) <= radius)
        & (jnp.abs(across) <= radius)
        & (column >= 0)
        & (column < 32)
    )


def flip_matrix():
    return (
        (
            lax.broadcasted_iota(jnp.int32, (GROUP, GROUP), 0)
            + lax.broadcasted_iota(jnp.int32, (GROUP, GROUP), 1)
            == GROUP - 1
        )
        .astype(F32)
        .astype(BF16)
    )


def pack_kernel(tile, cotangent, out):
    cells = tile.shape[0]
    out[:cells] = tile[...]
    out[cells : cells + 32, :128] = cotangent[:32]
    out[cells : cells + 32, 128:] = cotangent[cells - 32 :]
    ends = outer_columns(cotangent)
    out[cells + 32 :, :128] = ends[:16]
    out[cells + 32 :, 128:] = ends[16:]


def role(step, even):
    step = jnp.asarray(step)
    return jnp.where(step == 0, 0, jnp.where((step > 0) == even, 1, 2))


def position():
    col = lax.axis_index("col")
    return lax.axis_index("row"), col >> 1, col & 1


def tile_of(offset):
    row, chip, core = position()
    down, across = offset // 5 - 1, offset % 5 - 2
    return (
        role(down, row % 2 == 0) * 6 + role((core + across) >> 1, chip % 2 == 0) * 2 + (across & 1)
    )


def tiles_beside():
    row, chip, core = position()
    row_even, chip_even = row % 2 == 0, chip % 2 == 0
    north, south = role(-1, row_even) * 6, role(1, row_even) * 6
    west = jnp.where(core == 0, role(-1, chip_even), 0) * 2 + 1
    east = jnp.where(core == 0, 0, role(1, chip_even)) * 2 + 1
    return [north, south, west, east, north + west, north + east, south + west, south + east]


def spread_kernel(weight, out, out_back, narrow, wide):
    narrow[...] = weight[...].astype(F32)
    for lead, ref in ((LEAD, out), (LEAD_BACK, out_back)):
        wide[...] = jnp.zeros_like(wide)
        for k in range(4):
            for u in range(SPAN):
                row = k * 128 + (u % 4) * 32 + (u // 4) * SPAN + lead
                at = (k * SPAN + u) * SPAN
                wide[row : row + SPAN] = narrow[at : at + SPAN]
        ref[...] = wide[...].astype(BF16)


def forward_kernel(partners, counts, radius, first, context, cotangent, conv_weight, corr_weight, *refs):
    tiles, refs = refs[:18], refs[18:]
    parts, motion, context_grad, facing, away, ends, weights_sent, weights_kept = refs[:8]
    edges, cot_taps, taps_back, taps, flipped, weight_grads, sems, edge_sems = refs[8:]
    cells = first.shape[0]
    slots = parts.shape[0]
    row_sides, chip_sides = (6, 12), (1, 3, 5)
    options = [row_sides] * 2 + [chip_sides] * 2 + [[r + x for r in row_sides for x in chip_sides]] * 4
    for n, tile in enumerate(tiles_beside()):
        for t in options[n]:
            @pl.when(tile == t)
            def _():
                pltpu.make_async_copy(
                    tiles[t].at[pl.ds(cells, 48)], edges.at[n], edge_sems.at[n]
                ).start()
    for k in range(slots):
        tile = tile_of(partners[0, 0, k])
        for t in range(18):
            @pl.when(tile == t)
            def _():
                pltpu.make_async_copy(
                    tiles[t].at[pl.ds(0, cells)], parts.at[k, pl.ds(GROUP, cells)], sems.at[k]
                ).start()
        parts[k, :GROUP] = jnp.zeros((GROUP, parts.shape[2]), BF16)
        parts[k, GROUP + cells :] = jnp.zeros((GROUP, parts.shape[2]), BF16)
    inside = tap_mask(radius[0, 0], LEAD, True)
    flip = flip_matrix()
    gains = []
    for k in range(slots):
        live = jnp.where(k < counts[0, 0], 1.0 / math.sqrt(first.shape[1]), 0.0).astype(F32)
        gains.append(jnp.where(inside, live, 0.0))
    for q in range(cells // GROUP):
        at = slice(q * GROUP, (q + 1) * GROUP)
        flipped[at] = jnp.dot(flip, first[at], preferred_element_type=F32).astype(BF16)
    for n in range(8):
        pltpu.make_async_copy(tiles[0].at[pl.ds(cells, 48)], edges.at[n], edge_sems.at[n]).wait()
    north, south = edges[0, :32, 128:], edges[1, :32, :128]
    west = jnp.concatenate(
        [
            edges[4, :32, 128:].astype(F32)[31:],
            edges[2, 32:, 128:].astype(F32),
            edges[6, :32, :128].astype(F32)[31:],
        ]
    )
    east = jnp.concatenate(
        [
            edges[5, :32, 128:].astype(F32)[:1],
            edges[3, 32:, :128].astype(F32),
            edges[7, :32, :128].astype(F32)[:1],
        ]
    )
    write_taps(cot_taps, cotangent, north, south, west, east, True)
    grad_motion = jnp.zeros(context_grad.shape, F32)
    for a in range(3):
        start = (2 - a) * 32
        for b in range(3):
            grad_motion += lax.dot_general(
                cot_taps[start : start + cells, b * 128 : (b + 1) * 128],
                conv_weight[a, b],
                (((1,), (1,)), ((), ())),
                preferred_element_type=F32,
            )
    for k in range(slots):
        pltpu.make_async_copy(
            tiles[0].at[pl.ds(0, cells)], parts.at[k, pl.ds(GROUP, cells)], sems.at[k]
        ).wait()
    for q in range(cells // GROUP):
        at = slice(q * GROUP, (q + 1) * GROUP)
        features = flipped[at]
        for k in range(slots):
            scores = lax.dot_general(
                features,
                parts[k, q * GROUP : q * GROUP + WINDOW],
                (((1,), (1,)), ((), ())),
                preferred_element_type=F32,
            )
            turn = WINDOW + REACH + LEAD - (GROUP - 1)
            band = pltpu.roll(scores, turn, 1, stride=1, stride_axis=0) * gains[k]
            packed = (
                band[:, :128]
                + pltpu.roll(band[:, 128:256], SPAN, 1)
                + pltpu.roll(band[:, 256:], 2 * SPAN, 1)
            )
            taps_back[at, k * 128 : (k + 1) * 128] = packed.astype(BF16)
    for q in range(cells // GROUP):
        at = slice(q * GROUP, (q + 1) * GROUP)
        taps[at] = jnp.dot(flip, taps_back[at], preferred_element_type=F32).astype(BF16)
    pre = jnp.dot(taps[...], corr_weight[...], preferred_element_type=F32) + context[...].astype(
        F32
    )
    sigma = jax.nn.sigmoid(pre)
    motion[...] = (pre * sigma).astype(BF16)
    context_grad[...] = (grad_motion * sigma * (1.0 + pre * (1.0 - sigma))).astype(BF16)
    row, _, core = position()
    row_odd = row % 2
    facing[...] = motion[pl.ds(pl.multiple_of((1 - row_odd) * (cells - 32), 32), 32)]
    away[...] = motion[pl.ds(pl.multiple_of(row_odd * (cells - 32), 32), 32)]
    ends[...] = outer_columns(motion).reshape(ends.shape)
    over_cells = (((0,), (0,)), ((), ()))
    for a in range(3):
        start = (2 - a) * 32
        term = lax.dot_general(
            motion[...], cot_taps[start : start + cells], over_cells, preferred_element_type=F32
        )
        for b in range(3):
            weight_grads[(3 * a + b) * 256 : (3 * a + b + 1) * 256] = term[
                :, b * 128 : (b + 1) * 128
            ]
    term = lax.dot_general(taps[...], context_grad[...], over_cells, preferred_element_type=F32)
    base = 9 * 256
    for h in range(2):
        weight_grads[base + h * 384 + 320 : base + (h + 1) * 384] = jnp.zeros((64, 128), F32)
        for k in range(slots):
            for u in range(SPAN):
                row = k * 128 + (u % 4) * 32 + (u // 4) * SPAN + LEAD
                to = base + h * 384 + (k * SPAN + u) * SPAN
                weight_grads[to : to + SPAN] = term[row : row + SPAN, h * 128 : (h + 1) * 128]
    half = weight_grads.shape[0] // 2
    weights_kept[...] = weight_grads[pl.ds(pl.multiple_of(core * half, half), half)]
    weights_sent[...] = weight_grads[pl.ds(pl.multiple_of((1 - core) * half, half), half)].astype(
        BF16
    )


def backward_kernel(
    partners, counts, radius, first, context_grad, corr_weight, parts, first_grad, *refs
):
    cells = first.shape[0]
    slots = parts.shape[0]
    scale = 1.0 / math.sqrt(first.shape[1])
    inside = tap_mask(radius[0, 0], LEAD_BACK, False)
    *kept, lent, totals = refs
    for ref in refs:
        ref[...] = jnp.zeros_like(ref)
    across = first[...].T
    for q in range(cells // GROUP):
        at = slice(q * GROUP, (q + 1) * GROUP)
        packed = (
            lax.dot_general(
                context_grad[at],
                corr_weight[...],
                (((1,), (1,)), ((), ())),
                preferred_element_type=F32,
            )
            .astype(BF16)
            .astype(F32)
        )
        first_here = jnp.zeros((GROUP, first.shape[1]), F32)
        for k in range(slots):
            mine = packed[:, k * 128 : (k + 1) * 128]
            band = jnp.concatenate(
                [mine, pltpu.roll(mine, 128 - SPAN, 1), pltpu.roll(mine, 128 - 2 * SPAN, 1)],
                axis=1,
            )
            band = jnp.where(inside & (k < counts[0, 0]), band, 0.0)
            scores = pltpu.roll(band, WINDOW - REACH - LEAD_BACK, 1, stride=1, stride_axis=0).astype(BF16)
            window = slice(q * GROUP, q * GROUP + WINDOW)
            first_here += jnp.dot(scores, parts[k, window], preferred_element_type=F32)
            totals[k, :, window] += jnp.dot(
                across[:, at], scores, preferred_element_type=F32
            )
        first_grad[at] = first_here * scale
    for k in range(slots):
        value = (totals[k, :, GROUP : GROUP + cells] * scale).astype(BF16).T
        place = tile_of(partners[0, 0, k])
        for x in range(3):
            @pl.when(place % 6 == 2 * x)
            def _():
                kept[x][place // 6] = value

        @pl.when(place % 2 == 1)
        def _():
            lent[(place % 6 > 1).astype(jnp.int32) * 3 + place // 6] = value


def features_kernel(motion, north, south, west, east, weight, out, taps):
    cells = out.shape[0]
    write_taps(taps, motion, north[...], south[...], west[...], east[...], False)
    total = jnp.zeros(out.shape, F32)
    for a in range(3):
        total += jnp.dot(taps[a * 32 : a * 32 + cells], weight[a], preferred_element_type=F32)
    out[...] = total.astype(BF16)


def finish_kernel(*refs):
    shards, (conv, corr) = refs[:8], refs[8:]
    size = shards[0].shape[0]
    blocks = conv.shape[0] // size
    _, chip, core = position()
    for n, ref in enumerate(shards):
        block = (core if n < 4 else 1 - core) * 4 + (chip ^ (n % 4))

        @pl.when(block < blocks)
        def _():
            conv[pl.ds(pl.multiple_of(block * size, size), size)] = ref[...].astype(F32)

        for h in range(2):
            @pl.when(block == blocks + h)
            def _():
                corr[:, h * 128 : (h + 1) * 128] = ref[...].astype(F32)[: corr.shape[0]]


def call(kernel, out_shape, in_specs, scratch=(), flops=0):
    return pl.pallas_call(
        kernel,
        out_shape=out_shape,
        in_specs=in_specs,
        out_specs=jax.tree.map(lambda _: VMEM, out_shape),
        scratch_shapes=list(scratch),
        compiler_params=pltpu.CompilerParams(vmem_limit_bytes=VMEM_LIMIT),
        cost_estimate=pl.CostEstimate(flops=flops, bytes_accessed=flops // 300, transcendentals=0),
    )


def sum_everywhere(cur, axis, unit):
    mine = cur.astype(BF16)
    got = [swap(mine, axis, unit * s).astype(F32) for s in (1, 2, 3)]
    return (mine.astype(F32) + got[0]) + (got[1] + got[2])


def body(
    frame_one, frame_two, context, cotangent, corr_weight, conv_weight, partners, counts, radius
):
    rows_tile, cols_tile, channels = frame_one.shape
    slots = partners.shape[-1]
    cells = rows_tile * cols_tile
    hidden = context.shape[-1]
    out_width = conv_weight.shape[-1]
    row, col = lax.axis_index("row"), lax.axis_index("col")
    core, chip = col % 2, col // 2
    row_even, chip_even, col_even = row % 2 == 0, chip % 2 == 0, core == 0
    tables = (partners, counts, radius)
    first = frame_one.reshape(cells, channels)
    shape = jax.ShapeDtypeStruct
    cot = cotangent.reshape(cells, out_width)
    own = call(pack_kernel, shape((cells + 48, channels), BF16), [VMEM] * 2)(
        frame_two.reshape(cells, channels), cot
    )
    tiles = {(0, 0): own}
    for r in (1, 2):
        tiles[r, 0] = swap_pairs(own, "row", r - 1)
        tiles[0, r] = swap_pairs(own, "col", r - 1, 2)
    for r in (1, 2):
        tiles[r, r] = swap_pairs(tiles[r, 0], "col", r - 1, 2)
        tiles[r, 3 - r] = swap_pairs(tiles[0, 3 - r], "row", r - 1)
    around = []
    for r in range(3):
        for x in range(3):
            around += [tiles[r, x], swap(tiles[r, x], "col", 1)]
    spread, spread_back = call(
        spread_kernel,
        (shape((slots * 128, hidden), BF16), shape((slots * 128, hidden), BF16)),
        [VMEM],
        [pltpu.VMEM(corr_weight.shape, F32), pltpu.VMEM((slots * 128, hidden), F32)],
    )(corr_weight)
    total_rows = 9 * hidden + 2 * 384
    parts, motion, context_grad, facing, away, ends, weights_sent, weights_kept = call(
        forward_kernel,
        (
            shape((slots, cells + 2 * GROUP, channels), BF16),
            shape((cells, hidden), BF16),
            shape((cells, hidden), BF16),
            shape((cols_tile, hidden), BF16),
            shape((cols_tile, hidden), BF16),
            shape((2, rows_tile, hidden), BF16),
            shape((total_rows // 2, 128), BF16),
            shape((total_rows // 2, 128), F32),
        ),
        [SMEM] * 3 + [VMEM] * 5 + [ANY] * 18,
        [
            pltpu.VMEM((8, 48, channels), BF16),
            pltpu.VMEM(((rows_tile + 2) * cols_tile, 3 * out_width), BF16),
            pltpu.VMEM((cells, slots * 128), BF16),
            pltpu.VMEM((cells, slots * 128), BF16),
            pltpu.VMEM((cells, channels), BF16),
            pltpu.VMEM((total_rows, 128), F32),
            pltpu.SemaphoreType.DMA((slots,)),
            pltpu.SemaphoreType.DMA((8,)),
        ],
        flops=3 * 10**9,
    )(
        *tables,
        first,
        context.reshape(cells, hidden),
        cot,
        conv_weight,
        spread,
        *around,
    )
    total = weights_kept + swap(weights_sent, "col", 1).astype(F32)
    size = total.shape[0] // 4
    pieces = [lax.dynamic_slice_in_dim(total, (chip ^ s) * size, size) for s in range(4)]
    got = [swap(pieces[s].astype(BF16), "col", 2 * s) for s in (1, 2, 3)]
    first_grad, *kept, lent = call(
        backward_kernel,
        (
            shape((cells, channels), F32),
            *[shape((3, cells, channels), BF16)] * 3,
            shape((6, cells, channels), BF16),
        ),
        [SMEM] * 3 + [VMEM] * 4,
        [pltpu.VMEM((slots, channels, cells + 2 * GROUP), F32)],
        flops=3 * 10**9,
    )(*tables, first, context_grad, spread_back, parts)
    lent = swap(lent, "col", 1)
    side = jnp.where((core == 0) == chip_even, 1, 2)
    sent = [
        (kept[x].astype(F32) + jnp.where(side == x, lent[3:].astype(F32), 0.0)).astype(BF16)
        for x in (1, 2)
    ]
    total = (pieces[0] + got[0].astype(F32)) + (got[1].astype(F32) + got[2].astype(F32))
    around_motion = rim(facing, away, ends, row_even, col_even)
    total, *ready = lax.optimization_barrier((total, *sent, *around_motion))
    sent, around_motion = ready[:2], ready[2:]
    middle = kept[0].astype(F32) + lent[:3].astype(F32)
    for x in (1, 2):
        middle += swap_pairs(sent[x - 1], "col", x - 1, 2).astype(F32)
    total = sum_everywhere(sum_everywhere(total, "row", 1), "row", 4).astype(BF16)
    shards = [total] + [swap(total, "col", 2 * s) for s in (1, 2, 3)]
    features = call(
        features_kernel,
        shape((cells, out_width), BF16),
        [VMEM] * 6,
        [pltpu.VMEM(((rows_tile + 2) * cols_tile, 3 * hidden), BF16)],
        flops=10**9,
    )(
        motion,
        *around_motion,
        conv_weight.reshape(3, 3 * hidden, out_width),
    )
    features, *shards = lax.optimization_barrier((features, *shards))
    shards += [swap(shard, "col", 1) for shard in shards]
    second_grad = middle[0]
    for r in (1, 2):
        second_grad += swap_pairs(middle[r].astype(BF16), "row", r - 1).astype(F32)
    conv_total, corr_total = call(
        finish_kernel,
        (shape((9 * hidden, out_width), F32), shape(corr_weight.shape, F32)),
        [VMEM] * 8,
    )(*shards)
    return (
        features.reshape(rows_tile, cols_tile, out_width),
        context_grad.reshape(rows_tile, cols_tile, hidden),
        first_grad.reshape(frame_one.shape),
        second_grad.reshape(frame_two.shape),
        corr_total,
        conv_total.reshape(conv_weight.shape),
    )


def solution(mesh):
    return jax.shard_map(
        body,
        mesh=mesh,
        in_specs=(
            P("row", "col", None),
            P("row", "col", None),
            P("row", "col", None),
            P("row", "col", None),
            P(),
            P(),
            P("row", "col", None),
            P("row", "col"),
            P("row", "col"),
        ),
        out_specs=(
            P("row", "col", None),
            P("row", "col", None),
            P("row", "col", None),
            P("row", "col", None),
            P(),
            P(),
        ),
        check_vma=False,
    )
```

```python
import functools
import math

import jax
import jax.numpy as jnp
from jax import lax
from jax.experimental import pallas as pl
from jax.experimental.pallas import tpu as pltpu
from jax.sharding import PartitionSpec as P

REACH = 4
SPAN = 2 * REACH + 1
GROUP = 128
WINDOW = 384
LEAD, LEAD_BACK = 3, 4
F32 = jnp.float32
BF16 = jnp.bfloat16
VMEM_LIMIT = 56 * 1024 * 1024
VMEM = pl.BlockSpec(memory_space=pltpu.VMEM)
SMEM = pl.BlockSpec(memory_space=pltpu.SMEM)
ANY = pl.BlockSpec(memory_space=pl.ANY)


def swap(array, axis, bits):
    return lax.ppermute(array, axis, [(i, i ^ bits) for i in range(lax.axis_size(axis))])


def swap_pairs(array, axis, odd, unit=1):
    count = lax.axis_size(axis) // unit
    pairs = []
    for i in range(odd, count - 1, 2):
        for low in range(unit):
            here, there = i * unit + low, (i + 1) * unit + low
            pairs += [(here, there), (there, here)]
    return lax.ppermute(array, axis, pairs)


def rim(facing, away, ends, row_even, col_even):
    even = swap_pairs(facing, "row", 0)
    odd = swap_pairs(away, "row", 1)
    north, south = jnp.where(row_even, odd, even), jnp.where(row_even, even, odd)
    left = jnp.concatenate([north[:1], ends[0], south[:1]])
    right = jnp.concatenate([north[-1:], ends[1], south[-1:]])
    even = swap_pairs(jnp.where(col_even, right, left), "col", 0)
    odd = swap_pairs(jnp.where(col_even, left, right), "col", 1)
    west, east = jnp.where(col_even, odd, even), jnp.where(col_even, even, odd)
    return north, south, west, east


def outer_columns(cells):
    count = cells.shape[0]
    line = lax.broadcasted_iota(jnp.int32, (32, count), 0)
    cell = lax.broadcasted_iota(jnp.int32, (32, count), 1)
    wanted = (line & 15) * 32 + (line >> 4) * 31
    pick = (cell == wanted).astype(F32).astype(BF16)
    return jnp.dot(pick, cells[...], preferred_element_type=F32).astype(BF16)


def write_taps(taps, own, north, south, west, east, backwards):
    width = own.shape[1]
    line = north.shape[0]
    taps[:line, width : 2 * width] = north
    taps[line:-line, width : 2 * width] = own[...]
    taps[-line:, width : 2 * width] = south
    middle = taps[:, width : 2 * width].astype(F32)
    place = lax.broadcasted_iota(jnp.int32, middle.shape, 0) % line

    def stretched(ends):
        shape = (ends.shape[0], line, width)
        return jnp.broadcast_to(ends.astype(F32)[:, None], shape).reshape(middle.shape)

    left = jnp.where(place == 0, stretched(west), pltpu.roll(middle, 1, 0)).astype(BF16)
    right = jnp.where(
        place == line - 1, stretched(east), pltpu.roll(middle, middle.shape[0] - 1, 0)
    ).astype(BF16)
    taps[:, :width] = right if backwards else left
    taps[:, 2 * width :] = left if backwards else right


def tap_mask(radius, lead, backwards):
    cell = lax.broadcasted_iota(jnp.int32, (GROUP, WINDOW), 0)
    cell = GROUP - 1 - cell if backwards else cell
    tap = lax.broadcasted_iota(jnp.int32, (GROUP, WINDOW), 1)
    down = (tap >> 5) - REACH
    across = (tap & 31) - lead - REACH
    column = (cell & 31) + across
    return (
        (jnp.abs(down) <= radius)
        & (jnp.abs(across) <= radius)
        & (column >= 0)
        & (column < 32)
    )


def flip_matrix():
    return (
        (
            lax.broadcasted_iota(jnp.int32, (GROUP, GROUP), 0)
            + lax.broadcasted_iota(jnp.int32, (GROUP, GROUP), 1)
            == GROUP - 1
        )
        .astype(F32)
        .astype(BF16)
    )


def pack_kernel(tile, cotangent, out):
    cells = tile.shape[0]
    out[:cells] = tile[...]
    out[cells : cells + 32, :128] = cotangent[:32]
    out[cells : cells + 32, 128:] = cotangent[cells - 32 :]
    ends = outer_columns(cotangent)
    out[cells + 32 :, :128] = ends[:16]
    out[cells + 32 :, 128:] = ends[16:]


def role(step, even):
    step = jnp.asarray(step)
    return jnp.where(step == 0, 0, jnp.where((step > 0) == even, 1, 2))


def position():
    col = lax.axis_index("col")
    return lax.axis_index("row"), col >> 1, col & 1


def tile_of(offset):
    row, chip, core = position()
    down, across = offset // 5 - 1, offset % 5 - 2
    return (
        role(down, row % 2 == 0) * 6 + role((core + across) >> 1, chip % 2 == 0) * 2 + (across & 1)
    )


def tiles_beside():
    row, chip, core = position()
    row_even, chip_even = row % 2 == 0, chip % 2 == 0
    north, south = role(-1, row_even) * 6, role(1, row_even) * 6
    west = jnp.where(core == 0, role(-1, chip_even), 0) * 2 + 1
    east = jnp.where(core == 0, 0, role(1, chip_even)) * 2 + 1
    return [north, south, west, east, north + west, north + east, south + west, south + east]


def spread_kernel(weight, out, out_back, narrow, wide):
    narrow[...] = weight[...].astype(F32)
    for lead, ref in ((LEAD, out), (LEAD_BACK, out_back)):
        wide[...] = jnp.zeros_like(wide)
        for k in range(4):
            for u in range(SPAN):
                row = k * 128 + (u % 4) * 32 + (u // 4) * SPAN + lead
                at = (k * SPAN + u) * SPAN
                wide[row : row + SPAN] = narrow[at : at + SPAN]
        ref[...] = wide[...].astype(BF16)


def forward_kernel(partners, counts, radius, first, context, cotangent, conv_weight, corr_weight, *refs):
    tiles, refs = refs[:18], refs[18:]
    parts, motion, context_grad, facing, away, ends, weights_sent, weights_kept = refs[:8]
    edges, cot_taps, taps_back, taps, flipped, weight_grads, sems, edge_sems = refs[8:]
    cells = first.shape[0]
    slots = parts.shape[0]
    row_sides, chip_sides = (6, 12), (1, 3, 5)
    options = [row_sides] * 2 + [chip_sides] * 2 + [[r + x for r in row_sides for x in chip_sides]] * 4
    for n, tile in enumerate(tiles_beside()):
        for t in options[n]:
            @pl.when(tile == t)
            def _():
                pltpu.make_async_copy(
                    tiles[t].at[pl.ds(cells, 48)], edges.at[n], edge_sems.at[n]
                ).start()
    for k in range(slots):
        tile = tile_of(partners[0, 0, k])
        for t in range(18):
            @pl.when(tile == t)
            def _():
                pltpu.make_async_copy(
                    tiles[t].at[pl.ds(0, cells)], parts.at[k, pl.ds(GROUP, cells)], sems.at[k]
                ).start()
        parts[k, :GROUP] = jnp.zeros((GROUP, parts.shape[2]), BF16)
        parts[k, GROUP + cells :] = jnp.zeros((GROUP, parts.shape[2]), BF16)
    inside = tap_mask(radius[0, 0], LEAD, True)
    flip = flip_matrix()
    gains = []
    for k in range(slots):
        live = jnp.where(k < counts[0, 0], 1.0 / math.sqrt(first.shape[1]), 0.0).astype(F32)
        gains.append(jnp.where(inside, live, 0.0))
    for q in range(cells // GROUP):
        at = slice(q * GROUP, (q + 1) * GROUP)
        flipped[at] = jnp.dot(flip, first[at], preferred_element_type=F32).astype(BF16)
    for n in range(8):
        pltpu.make_async_copy(tiles[0].at[pl.ds(cells, 48)], edges.at[n], edge_sems.at[n]).wait()
    north, south = edges[0, :32, 128:], edges[1, :32, :128]
    west = jnp.concatenate(
        [
            edges[4, :32, 128:].astype(F32)[31:],
            edges[2, 32:, 128:].astype(F32),
            edges[6, :32, :128].astype(F32)[31:],
        ]
    )
    east = jnp.concatenate(
        [
            edges[5, :32, 128:].astype(F32)[:1],
            edges[3, 32:, :128].astype(F32),
            edges[7, :32, :128].astype(F32)[:1],
        ]
    )
    write_taps(cot_taps, cotangent, north, south, west, east, True)
    grad_motion = jnp.zeros(context_grad.shape, F32)
    for a in range(3):
        start = (2 - a) * 32
        for b in range(3):
            grad_motion += lax.dot_general(
                cot_taps[start : start + cells, b * 128 : (b + 1) * 128],
                conv_weight[a, b],
                (((1,), (1,)), ((), ())),
                preferred_element_type=F32,
            )
    for k in range(slots):
        pltpu.make_async_copy(
            tiles[0].at[pl.ds(0, cells)], parts.at[k, pl.ds(GROUP, cells)], sems.at[k]
        ).wait()
    for q in range(cells // GROUP):
        at = slice(q * GROUP, (q + 1) * GROUP)
        features = flipped[at]
        for k in range(slots):
            scores = lax.dot_general(
                features,
                parts[k, q * GROUP : q * GROUP + WINDOW],
                (((1,), (1,)), ((), ())),
                preferred_element_type=F32,
            )
            turn = WINDOW + REACH + LEAD - (GROUP - 1)
            band = pltpu.roll(scores, turn, 1, stride=1, stride_axis=0) * gains[k]
            packed = (
                band[:, :128]
                + pltpu.roll(band[:, 128:256], SPAN, 1)
                + pltpu.roll(band[:, 256:], 2 * SPAN, 1)
            )
            taps_back[at, k * 128 : (k + 1) * 128] = packed.astype(BF16)
    for q in range(cells // GROUP):
        at = slice(q * GROUP, (q + 1) * GROUP)
        taps[at] = jnp.dot(flip, taps_back[at], preferred_element_type=F32).astype(BF16)
    pre = jnp.dot(taps[...], corr_weight[...], preferred_element_type=F32) + context[...].astype(
        F32
    )
    sigma = jax.nn.sigmoid(pre)
    motion[...] = (pre * sigma).astype(BF16)
    context_grad[...] = (grad_motion * sigma * (1.0 + pre * (1.0 - sigma))).astype(BF16)
    row, _, core = position()
    row_odd = row % 2
    facing[...] = motion[pl.ds(pl.multiple_of((1 - row_odd) * (cells - 32), 32), 32)]
    away[...] = motion[pl.ds(pl.multiple_of(row_odd * (cells - 32), 32), 32)]
    ends[...] = outer_columns(motion).reshape(ends.shape)
    over_cells = (((0,), (0,)), ((), ()))
    for a in range(3):
        start = (2 - a) * 32
        term = lax.dot_general(
            motion[...], cot_taps[start : start + cells], over_cells, preferred_element_type=F32
        )
        for b in range(3):
            weight_grads[(3 * a + b) * 256 : (3 * a + b + 1) * 256] = term[
                :, b * 128 : (b + 1) * 128
            ]
    term = lax.dot_general(taps[...], context_grad[...], over_cells, preferred_element_type=F32)
    base = 9 * 256
    for h in range(2):
        weight_grads[base + h * 384 + 320 : base + (h + 1) * 384] = jnp.zeros((64, 128), F32)
        for k in range(slots):
            for u in range(SPAN):
                row = k * 128 + (u % 4) * 32 + (u // 4) * SPAN + LEAD
                to = base + h * 384 + (k * SPAN + u) * SPAN
                weight_grads[to : to + SPAN] = term[row : row + SPAN, h * 128 : (h + 1) * 128]
    half = weight_grads.shape[0] // 2
    weights_kept[...] = weight_grads[pl.ds(pl.multiple_of(core * half, half), half)]
    weights_sent[...] = weight_grads[pl.ds(pl.multiple_of((1 - core) * half, half), half)].astype(
        BF16
    )


def backward_kernel(
    partners, counts, radius, first, context_grad, corr_weight, parts, first_grad, *refs
):
    cells = first.shape[0]
    slots = parts.shape[0]
    scale = 1.0 / math.sqrt(first.shape[1])
    inside = tap_mask(radius[0, 0], LEAD_BACK, False)
    *kept, lent, totals = refs
    for ref in refs:
        ref[...] = jnp.zeros_like(ref)
    across = first[...].T
    for q in range(cells // GROUP):
        at = slice(q * GROUP, (q + 1) * GROUP)
        packed = (
            lax.dot_general(
                context_grad[at],
                corr_weight[...],
                (((1,), (1,)), ((), ())),
                preferred_element_type=F32,
            )
            .astype(BF16)
            .astype(F32)
        )
        first_here = jnp.zeros((GROUP, first.shape[1]), F32)
        for k in range(slots):
            mine = packed[:, k * 128 : (k + 1) * 128]
            band = jnp.concatenate(
                [mine, pltpu.roll(mine, 128 - SPAN, 1), pltpu.roll(mine, 128 - 2 * SPAN, 1)],
                axis=1,
            )
            band = jnp.where(inside & (k < counts[0, 0]), band, 0.0)
            scores = pltpu.roll(band, WINDOW - REACH - LEAD_BACK, 1, stride=1, stride_axis=0).astype(BF16)
            window = slice(q * GROUP, q * GROUP + WINDOW)
            first_here += jnp.dot(scores, parts[k, window], preferred_element_type=F32)
            totals[k, :, window] += jnp.dot(
                across[:, at], scores, preferred_element_type=F32
            )
        first_grad[at] = first_here * scale
    for k in range(slots):
        value = (totals[k, :, GROUP : GROUP + cells] * scale).astype(BF16).T
        place = tile_of(partners[0, 0, k])
        for x in range(3):
            @pl.when(place % 6 == 2 * x)
            def _():
                kept[x][place // 6] = value

        @pl.when(place % 2 == 1)
        def _():
            lent[(place % 6 > 1).astype(jnp.int32) * 3 + place // 6] = value


def features_kernel(motion, north, south, west, east, weight, out, taps):
    cells = out.shape[0]
    write_taps(taps, motion, north[...], south[...], west[...], east[...], False)
    total = jnp.zeros(out.shape, F32)
    for a in range(3):
        total += jnp.dot(taps[a * 32 : a * 32 + cells], weight[a], preferred_element_type=F32)
    out[...] = total.astype(BF16)


def finish_kernel(*refs):
    shards, (conv, corr) = refs[:8], refs[8:]
    size = shards[0].shape[0]
    blocks = conv.shape[0] // size
    _, chip, core = position()
    for n, ref in enumerate(shards):
        block = (core if n < 4 else 1 - core) * 4 + (chip ^ (n % 4))

        @pl.when(block < blocks)
        def _():
            conv[pl.ds(pl.multiple_of(block * size, size), size)] = ref[...].astype(F32)

        for h in range(2):
            @pl.when(block == blocks + h)
            def _():
                corr[:, h * 128 : (h + 1) * 128] = ref[...].astype(F32)[: corr.shape[0]]


def call(kernel, out_shape, in_specs, scratch=(), flops=0):
    return pl.pallas_call(
        kernel,
        out_shape=out_shape,
        in_specs=in_specs,
        out_specs=jax.tree.map(lambda _: VMEM, out_shape),
        scratch_shapes=list(scratch),
        compiler_params=pltpu.CompilerParams(vmem_limit_bytes=VMEM_LIMIT),
        cost_estimate=pl.CostEstimate(flops=flops, bytes_accessed=flops // 300, transcendentals=0),
    )


def sum_everywhere(cur, axis, unit):
    mine = cur.astype(BF16)
    got = [swap(mine, axis, unit * s).astype(F32) for s in (1, 2, 3)]
    return (mine.astype(F32) + got[0]) + (got[1] + got[2])


def body(
    frame_one, frame_two, context, cotangent, corr_weight, conv_weight, partners, counts, radius
):
    rows_tile, cols_tile, channels = frame_one.shape
    slots = partners.shape[-1]
    cells = rows_tile * cols_tile
    hidden = context.shape[-1]
    out_width = conv_weight.shape[-1]
    row, col = lax.axis_index("row"), lax.axis_index("col")
    core, chip = col % 2, col // 2
    row_even, chip_even, col_even = row % 2 == 0, chip % 2 == 0, core == 0
    tables = (partners, counts, radius)
    first = frame_one.reshape(cells, channels)
    shape = jax.ShapeDtypeStruct
    cot = cotangent.reshape(cells, out_width)
    own = call(pack_kernel, shape((cells + 48, channels), BF16), [VMEM] * 2)(
        frame_two.reshape(cells, channels), cot
    )
    tiles = {(0, 0): own}
    for r in (1, 2):
        tiles[r, 0] = swap_pairs(own, "row", r - 1)
        tiles[0, r] = swap_pairs(own, "col", r - 1, 2)
    for r in (1, 2):
        tiles[r, r] = swap_pairs(tiles[r, 0], "col", r - 1, 2)
        tiles[r, 3 - r] = swap_pairs(tiles[0, 3 - r], "row", r - 1)
    around = []
    for r in range(3):
        for x in range(3):
            around += [tiles[r, x], swap(tiles[r, x], "col", 1)]
    spread, spread_back = call(
        spread_kernel,
        (shape((slots * 128, hidden), BF16), shape((slots * 128, hidden), BF16)),
        [VMEM],
        [pltpu.VMEM(corr_weight.shape, F32), pltpu.VMEM((slots * 128, hidden), F32)],
    )(corr_weight)
    total_rows = 9 * hidden + 2 * 384
    parts, motion, context_grad, facing, away, ends, weights_sent, weights_kept = call(
        forward_kernel,
        (
            shape((slots, cells + 2 * GROUP, channels), BF16),
            shape((cells, hidden), BF16),
            shape((cells, hidden), BF16),
            shape((cols_tile, hidden), BF16),
            shape((cols_tile, hidden), BF16),
            shape((2, rows_tile, hidden), BF16),
            shape((total_rows // 2, 128), BF16),
            shape((total_rows // 2, 128), F32),
        ),
        [SMEM] * 3 + [VMEM] * 5 + [ANY] * 18,
        [
            pltpu.VMEM((8, 48, channels), BF16),
            pltpu.VMEM(((rows_tile + 2) * cols_tile, 3 * out_width), BF16),
            pltpu.VMEM((cells, slots * 128), BF16),
            pltpu.VMEM((cells, slots * 128), BF16),
            pltpu.VMEM((cells, channels), BF16),
            pltpu.VMEM((total_rows, 128), F32),
            pltpu.SemaphoreType.DMA((slots,)),
            pltpu.SemaphoreType.DMA((8,)),
        ],
        flops=3 * 10**9,
    )(
        *tables,
        first,
        context.reshape(cells, hidden),
        cot,
        conv_weight,
        spread,
        *around,
    )
    total = weights_kept + swap(weights_sent, "col", 1).astype(F32)
    size = total.shape[0] // 4
    pieces = [lax.dynamic_slice_in_dim(total, (chip ^ s) * size, size) for s in range(4)]
    got = [swap(pieces[s].astype(BF16), "col", 2 * s) for s in (1, 2, 3)]
    first_grad, *kept, lent = call(
        backward_kernel,
        (
            shape((cells, channels), F32),
            *[shape((3, cells, channels), BF16)] * 3,
            shape((6, cells, channels), BF16),
        ),
        [SMEM] * 3 + [VMEM] * 4,
        [pltpu.VMEM((slots, channels, cells + 2 * GROUP), F32)],
        flops=3 * 10**9,
    )(*tables, first, context_grad, spread_back, parts)
    lent = swap(lent, "col", 1)
    side = jnp.where((core == 0) == chip_even, 1, 2)
    sent = [
        (kept[x].astype(F32) + jnp.where(side == x, lent[3:].astype(F32), 0.0)).astype(BF16)
        for x in (1, 2)
    ]
    total = (pieces[0] + got[0].astype(F32)) + (got[1].astype(F32) + got[2].astype(F32))
    around_motion = rim(facing, away, ends, row_even, col_even)
    ready = lax.optimization_barrier((*sent, *around_motion))
    sent, around_motion = ready[:2], ready[2:]
    middle = kept[0].astype(F32) + lent[:3].astype(F32)
    for x in (1, 2):
        middle += swap_pairs(sent[x - 1], "col", x - 1, 2).astype(F32)
    total = sum_everywhere(sum_everywhere(total, "row", 1), "row", 4).astype(BF16)
    shards = [total] + [swap(total, "col", 2 * s) for s in (1, 2, 3)]
    features = call(
        features_kernel,
        shape((cells, out_width), BF16),
        [VMEM] * 6,
        [pltpu.VMEM(((rows_tile + 2) * cols_tile, 3 * hidden), BF16)],
        flops=10**9,
    )(
        motion,
        *around_motion,
        conv_weight.reshape(3, 3 * hidden, out_width),
    )
    features, *shards = lax.optimization_barrier((features, *shards))
    shards += [swap(shard, "col", 1) for shard in shards]
    second_grad = middle[0]
    for r in (1, 2):
        second_grad += swap_pairs(middle[r].astype(BF16), "row", r - 1).astype(F32)
    conv_total, corr_total = call(
        finish_kernel,
        (shape((9 * hidden, out_width), F32), shape(corr_weight.shape, F32)),
        [VMEM] * 8,
    )(*shards)
    return (
        features.reshape(rows_tile, cols_tile, out_width),
        context_grad.reshape(rows_tile, cols_tile, hidden),
        first_grad.reshape(frame_one.shape),
        second_grad.reshape(frame_two.shape),
        corr_total,
        conv_total.reshape(conv_weight.shape),
    )


def solution(mesh):
    return jax.shard_map(
        body,
        mesh=mesh,
        in_specs=(
            P("row", "col", None),
            P("row", "col", None),
            P("row", "col", None),
            P("row", "col", None),
            P(),
            P(),
            P("row", "col", None),
            P("row", "col"),
            P("row", "col"),
        ),
        out_specs=(
            P("row", "col", None),
            P("row", "col", None),
            P("row", "col", None),
            P("row", "col", None),
            P(),
            P(),
        ),
        check_vma=False,
    )
```
